32 devices in a mesh: dp: 8 (over y, x, core), expert: 4 (over z).
Axes of the slice: x: 2, y: 2, z: 4, core: 2. Of those that a mesh axis runs over, the one named last changes fastest.
Arguments:
- grad_out: bfloat16 [8192, 3072], P(('dp', 'expert')), may hold values from -1.5 to 1.5
- routes: int32 [8192, 2], P(('dp', 'expert')), may hold values from 0 to 63, as said below
- gate_levels: int32 [8192, 2], P(('dp', 'expert')), may hold values from 1 to 15
- saved_inputs: bfloat16 [1536, 3072], P(('dp', 'expert')), may hold values from -6 to 6
- w_gate: bfloat16 [3072, 2048], P(None, 'expert'), may hold values from -0.109375 to 0.109375
- w_up: bfloat16 [3072, 2048], P(None, 'expert'), may hold values from -0.109375 to 0.109375
- w_down: bfloat16 [2048, 3072], P('expert'), may hold values from -0.1875 to 0.1875
Outputs:
- input_grad: bfloat16 [8192, 3072], P(('dp', 'expert'))
- gate_grad: float32 [8192, 2], P(('dp', 'expert'))
- weight_grad: float32 [3072, 3, 2048], P('dp', None, 'expert')
The draws below stay inside these ranges and needn't reach their ends.
Inputs may be any that keep to these rules, and one draw needn't show every extreme that they name: `routes`: the ids of one token differ. A device's tokens name each expert below 2 at most 12 times; in every block one of them is named exactly 12 times, and the same one for all 4 blocks of one replica.
All inputs are finite; a program needn't handle non-finite values.
Results may differ from the reference program's by a relative error of at most 0.012.
Values may be sent and summed in bfloat16 or wider, within the bound.
No kernel may reach another device: no remote copies, remote signals or barrier semaphores. Data moves between devices by JAX's collectives and lax.ppermute only.
A program may use at most 128 MiB of HBM per device.

```python
import jax
import jax.numpy as jnp
from jax import lax

D = 3072
FF = 1024
EXPERTS_ALL = 64
EXPERTS_W = 2
CAP = 12
TOK_DEV = 256
GROUP = 4
F_DEV = 512
TOKENS = 8192
SLOTS = 1536
N_DP = 8
N_EXPERT = 4


def draw_routes(key, part):
    blocks = TOKENS // TOK_DEV
    keys = jax.random.split(key, 6)
    shift = jax.random.randint(keys[0], (), 0, 2)
    block_ids = jnp.arange(blocks, dtype=jnp.int32)
    full_one = (block_ids // GROUP + shift) % 2
    other_count = jax.random.randint(keys[1], (blocks,), 1, CAP + 1)
    count_zero = jnp.where(full_one == 0, CAP, other_count)
    count_one = jnp.where(full_one == 1, CAP, other_count)
    scores = jax.random.randint(keys[2], (blocks, TOK_DEV), 0, 1 << 20) * TOK_DEV + jnp.arange(TOK_DEV, dtype=jnp.int32)
    position = jnp.argsort(jnp.argsort(scores, axis=1), axis=1)
    outside = 2 + jax.random.randint(keys[3], (blocks, TOK_DEV), 0, EXPERTS_ALL - 2)
    first = jnp.where(position < count_zero[:, None], 0, jnp.where(position < (count_zero + count_one)[:, None], 1, outside))
    offset = jax.random.randint(keys[4], (blocks, TOK_DEV), 0, EXPERTS_ALL - 3)
    second = jnp.where(first >= 2, 2 + (first - 2 + 1 + offset) % (EXPERTS_ALL - 2), 2 + offset)
    swapped = jax.random.randint(keys[5], (blocks, TOK_DEV), 0, 2)
    left = jnp.where(swapped == 1, second, first)
    right = jnp.where(swapped == 1, first, second)
    return jnp.stack([left, right], axis=2).reshape(TOKENS, 2).astype(jnp.int32)


def set_ends(result, own_key, least, top_value):
    index_at = [jax.random.randint(jax.random.fold_in(own_key, axis), (), 0, length) for axis, length in enumerate(result.shape)]
    longest = result.shape.index(max(result.shape))
    neighbour = index_at[:longest] + [(index_at[longest] + 1) % result.shape[longest]] + index_at[longest + 1:]
    return result.at[tuple(index_at)].set(least).at[tuple(neighbour)].set(top_value)


def block_scale(rng, shape, cuts, low, top_value):
    loudness, own = 1.0, jax.random.fold_in(rng, 6)
    for dim, shards_of in cuts:
        steps = jnp.exp(jax.random.uniform(jax.random.fold_in(own, dim), (shards_of,), jnp.float32, low / len(cuts), top_value / len(cuts)))
        loudness = loudness * jnp.repeat(steps, shape[dim] // shards_of).reshape([-1 if axis == dim else 1 for axis in range(len(shape))])
    return loudness


def bell_draw(own_key, shape, deviation, reach, cuts=(), held_as=jnp.bfloat16):
    drawn = jax.random.normal(own_key, shape, jnp.float32) * deviation
    if len(cuts) > 0:
        drawn = block_scale(own_key, shape, cuts, -0.22, 0.18) * drawn
    return jnp.clip(drawn, min=-reach, max=reach).astype(held_as)


def setup_inputs(seed: int = 0) -> dict:
    streams_of = jax.random.split(jax.random.key(seed), 8)
    return {
        "grad_out": bell_draw(streams_of[0], (TOKENS, D), 0.25, 1.5, ((0, 32),)),
        "routes": draw_routes(jax.random.fold_in(streams_of[7], 71), 0),
        "gate_levels": set_ends(jax.random.randint(streams_of[2], (TOKENS, 2), 1, 16), jax.random.fold_in(streams_of[2], 1), 1, 15).astype(jnp.int32),
        "saved_inputs": bell_draw(streams_of[3], (SLOTS, D), 1.0, 6.0, ((0, 32),)),
        "w_gate": bell_draw(streams_of[4], (D, N_EXPERT * F_DEV), D ** -0.5, 0.109375, ((1, 4),)),
        "w_up": bell_draw(streams_of[5], (D, N_EXPERT * F_DEV), D ** -0.5, 0.109375, ((1, 4),)),
        "w_down": bell_draw(streams_of[6], (N_EXPERT * F_DEV, D), FF ** -0.5, 0.1875, ((0, 4),)),
    }


def reference(grad_out, routes, gate_levels, saved_inputs, w_gate, w_up, w_down):
    group = N_EXPERT
    shards = group // EXPERTS_W
    f_dev = FF // shards
    blocks_out = grad_out.reshape(N_DP, group, TOK_DEV, D)
    route_blocks = routes.reshape(N_DP, group, TOK_DEV, 2)
    level_blocks = gate_levels.reshape(N_DP, group, TOK_DEV, 2)
    saved_blocks = saved_inputs.reshape(N_DP, group, group * CAP, D)
    gate_mats = w_gate.reshape(D, group, f_dev).transpose(1, 0, 2).astype(jnp.float32)
    up_mats = w_up.reshape(D, group, f_dev).transpose(1, 0, 2).astype(jnp.float32)
    down_mats = w_down.reshape(group, f_dev, D).astype(jnp.float32)
    owner = jnp.arange(group) // shards

    def one_row(carry, inputs):
        grads_row, routes_row, levels_row, saved_row = inputs
        hits = (routes_row[..., None] == jnp.arange(EXPERTS_W, dtype=jnp.int32)).astype(jnp.int32)
        member = jnp.sum(hits, axis=2)
        levels = jnp.sum(hits * levels_row[..., None], axis=2)
        slots = jnp.cumsum(member, axis=1) - 1
        placed = (member[..., None] == 1) & (slots[..., None] == jnp.arange(CAP, dtype=jnp.int32))
        token_index = jnp.sum(placed.astype(jnp.int32) * jnp.arange(TOK_DEV, dtype=jnp.int32)[None, :, None, None], axis=1)
        filled = jnp.any(placed, axis=1)
        flat_index = token_index.reshape(group, EXPERTS_W * CAP)
        picked = jnp.take_along_axis(grads_row, flat_index[:, :, None], axis=1).reshape(group, EXPERTS_W, CAP, D)
        picked = jnp.where(filled[..., None], picked, jnp.zeros_like(picked)).astype(jnp.bfloat16)
        level_slots = jnp.take_along_axis(jnp.transpose(levels, (0, 2, 1)), token_index, axis=2)
        slot_gate = jnp.where(filled, level_slots.astype(jnp.float32) / 16.0, jnp.float32(0.0))
        grad_rows = picked[:, owner].transpose(1, 0, 2, 3).reshape(group, group * CAP, D).astype(jnp.float32)
        gates = slot_gate[:, owner].transpose(1, 0, 2).reshape(group, group * CAP, 1)
        input_rows = saved_row.astype(jnp.float32)
        pre_gate = jnp.einsum("jrd,jdf->jrf", input_rows, gate_mats)
        pre_up = jnp.einsum("jrd,jdf->jrf", input_rows, up_mats)
        projected = jnp.einsum("jrd,jfd->jrf", grad_rows, down_mats)
        sigma = jax.nn.sigmoid(pre_gate)
        activ = pre_gate * sigma
        hidden = activ * pre_up
        gate_part = jnp.sum(hidden * projected, axis=2).astype(jnp.bfloat16)
        d_hidden = gates * projected
        d_up = (d_hidden * activ).astype(jnp.bfloat16)
        d_pre = (d_hidden * pre_up * sigma * (1.0 + pre_gate * (1.0 - sigma))).astype(jnp.bfloat16)
        scaled_hidden = (gates * hidden).astype(jnp.bfloat16)
        input_part = (jnp.einsum("jrf,jdf->jrd", d_pre.astype(jnp.float32), gate_mats)
                      + jnp.einsum("jrf,jdf->jrd", d_up.astype(jnp.float32), up_mats)).astype(jnp.bfloat16)
        term = jnp.stack([
            jnp.einsum("jrd,jrf->jdf", input_rows, d_pre.astype(jnp.float32)),
            jnp.einsum("jrd,jrf->jdf", input_rows, d_up.astype(jnp.float32)),
            jnp.einsum("jrd,jrf->jdf", grad_rows, scaled_hidden.astype(jnp.float32))], axis=2)
        carry = carry + term
        back = input_part.astype(jnp.float32).reshape(EXPERTS_W, shards, group, CAP, D).sum(axis=1).transpose(1, 0, 2, 3)
        gate_back = gate_part.astype(jnp.float32).reshape(EXPERTS_W, shards, group, CAP).sum(axis=1).transpose(1, 0, 2)
        clipped = jnp.transpose(jnp.clip(slots, 0, CAP - 1), (0, 2, 1))
        member_t = jnp.transpose(member, (0, 2, 1)).astype(jnp.float32)
        taken = jnp.take_along_axis(back, clipped[..., None], axis=2) * member_t[..., None]
        input_tok = jnp.sum(taken, axis=1).astype(jnp.bfloat16)
        per_expert = jnp.take_along_axis(gate_back, clipped, axis=2) * member_t
        gate_tok = jnp.sum(hits.astype(jnp.float32) * jnp.transpose(per_expert, (0, 2, 1))[:, :, None, :], axis=3)
        return carry, (input_tok, gate_tok)

    start = jnp.zeros((group, D, 3, f_dev), jnp.float32)
    total, (input_all, gate_all) = lax.scan(one_row, start, (blocks_out, route_blocks, level_blocks, saved_blocks))
    weight_grad = total.transpose(1, 2, 0, 3).reshape(D, 3, group * f_dev)
    return input_all.reshape(TOKENS, D), gate_all.reshape(TOKENS, 2), weight_grad
```

```python
import functools

import jax
import jax.numpy as jnp
from jax import lax
from jax.experimental import pallas as pl
from jax.experimental.pallas import tpu as pltpu
from jax.sharding import PartitionSpec as P

EXPERTS_W = 2
SEND_CUTS = 4
BACK_CUTS = 2
GATE_LANES = 128
W_CHUNKS = 4
PAIRED = 8
F32 = jnp.float32
BF16 = jnp.bfloat16
VMEM = pl.BlockSpec(memory_space=pltpu.VMEM)
HBM = pl.BlockSpec(memory_space=pl.ANY)


def nn(left, right):
    return lax.dot_general(left, right, (((1,), (0,)), ((), ())), preferred_element_type=F32)


def nt(left, right):
    return lax.dot_general(left, right, (((1,), (1,)), ((), ())), preferred_element_type=F32)


def tn(left, right):
    return lax.dot_general(left, right, (((0,), (0,)), ((), ())), preferred_element_type=F32)


def iota(shape, dim):
    return lax.broadcasted_iota(jnp.int32, shape, dim)


def call(kernel, outs, args, specs, scratch=(), flops=0, moved=0, name=None):
    return pl.pallas_call(
        kernel,
        out_shape=outs,
        in_specs=specs,
        out_specs=jax.tree.map(lambda _: VMEM, outs),
        scratch_shapes=scratch,
        compiler_params=pltpu.CompilerParams(vmem_limit_bytes=40 * 1024 * 1024),
        cost_estimate=pl.CostEstimate(flops=flops, bytes_accessed=moved, transcendentals=0),
        name=name,
    )(*args)


def pick_kernel(shards, capacity, routes, levels, grad, own_out, other_out, slots_out):
    tokens, width = grad.shape
    span = width // SEND_CUTS
    rows = SEND_CUTS * capacity
    mine = lax.axis_index("expert") // shards
    upto = (iota((tokens, tokens), 0) <= iota((tokens, tokens), 1)).astype(BF16)
    first, second = routes[0:1, :], routes[1:2, :]
    found = jnp.zeros((8, tokens), F32)
    for expert in range(EXPERTS_W):
        hit = ((first == expert) | (second == expert)).astype(F32)
        found = jnp.where(iota((8, tokens), 0) == expert, hit, found)
    counted = nn(found.astype(BF16), upto)
    slots = jnp.where(found > 0, counted - 1.0, -4096.0).astype(jnp.int32)
    slots_out[...] = slots
    for which, out in ((0, own_out), (1, other_out)):
        expert = mine if which == 0 else 1 - mine
        slot = jnp.where(expert == 0, slots[0:1, :], slots[1:2, :])
        level = jnp.where(first == expert, levels[0:1, :], levels[1:2, :])
        gate = level.astype(F32) * (1.0 / 16.0)
        total = jnp.zeros((rows, span), F32)
        for cut in range(SEND_CUTS):
            lead = jnp.where(slot == iota((rows, tokens), 0) - cut * capacity, gate, 0.0)
            total += nn(lead.astype(BF16), grad[:, cut * span : (cut + 1) * span])
        out[...] = total.astype(BF16)


def hidden_kernel(inputs, w_gate, w_up, u_out, v_out, h_out, gate_buf, up_buf, sems):
    width = inputs.shape[1]
    step = width // W_CHUNKS
    copies = []
    for k in range(W_CHUNKS):
        part = pl.ds(k * step, step)
        for n, (src, dst) in enumerate(((w_gate, gate_buf), (w_up, up_buf))):
            copy = pltpu.make_async_copy(src.at[part], dst.at[part], sems.at[n, k])
            copy.start()
            copies.append(copy)
    a = jnp.zeros(u_out.shape, F32)
    b = jnp.zeros(u_out.shape, F32)
    for k in range(W_CHUNKS):
        left = inputs[:, k * step : (k + 1) * step]
        copies[2 * k].wait()
        a += nn(left, gate_buf[k * step : (k + 1) * step, :])
        copies[2 * k + 1].wait()
        b += nn(left, up_buf[k * step : (k + 1) * step, :])
    s = jax.nn.sigmoid(a)
    u = a * s
    u_out[...] = u
    v_out[...] = b * s * (1.0 + a * (1.0 - s))
    h_out[...] = u * b


def project_kernel(group, capacity, n_dp, *refs):
    received = refs[:group]
    w_down, u_in, v_in, h_in, inputs = refs[group : group + 5]
    sends = refs[group + 5 : -6]
    da_out, db_out, gate_out, down_buf, rows_buf, sems = refs[-6:]
    rows, width = inputs.shape
    hidden = u_in.shape[1]
    span = width // SEND_CUTS
    me = lax.axis_index("expert")
    copies = []
    for cut in range(SEND_CUTS):
        part = pl.ds(cut * span, span)
        copy = pltpu.make_async_copy(w_down.at[:, part], down_buf.at[:, part], sems.at[cut])
        copy.start()
        copies.append(copy)
    packed = SEND_CUTS * capacity
    every = jnp.concatenate([ref[...] for ref in received], axis=0)
    to = iota((rows, group * packed), 0)
    at = iota((rows, group * packed), 1)
    source = (at // packed) ^ me
    within = at % packed
    match = (to // capacity == source) & (to % capacity == within % capacity)
    projected = jnp.zeros((rows, hidden), F32)
    for cut in range(SEND_CUTS):
        select = (match & (within // capacity == cut)).astype(F32).astype(BF16)
        piece = nn(select, every).astype(BF16)
        rows_buf[:, cut * span : (cut + 1) * span] = piece
        copies[cut].wait()
        projected += nt(piece, down_buf[:, cut * span : (cut + 1) * span])
    da = (projected * v_in[...]).astype(BF16)
    db = (projected * u_in[...]).astype(BF16)
    hid = h_in[...]
    da_out[...] = da
    db_out[...] = db
    gate = jnp.sum(hid * projected, axis=1, keepdims=True)
    lane = iota((rows, GATE_LANES), 1)
    gate_out[...] = jnp.where(lane == me // (group // EXPERTS_W), gate, 0.0).astype(BF16)
    hid = hid.astype(BF16)
    if n_dp != PAIRED:
        sends[0][...] = rows_buf[...]
        sends[1][...] = hid
        return
    pair = 2 * (width // n_dp)
    chip = lax.axis_index("dp") // 2
    for m, send in enumerate(sends):
        start = pl.multiple_of((chip ^ m) * pair, 128)
        send[:, 0:pair] = inputs[:, pl.ds(start, pair)]
        send[:, pair : 2 * pair] = rows_buf[:, pl.ds(start, pair)]
        send[:, 2 * pair : 2 * pair + hidden] = da
        send[:, 2 * pair + hidden : 2 * pair + 2 * hidden] = db
        send[:, 2 * pair + 2 * hidden :] = hid


def input_kernel(group, capacity, da, db, gate, w_gate, w_up, *refs):
    outs = refs[:group]
    gate_buf, up_buf, sems = refs[group:]
    rows = da.shape[0]
    width = w_gate.shape[0]
    span = width // BACK_CUTS
    step = width // W_CHUNKS
    per = W_CHUNKS // BACK_CUTS
    me = lax.axis_index("expert")
    copies = []
    for k in range(W_CHUNKS):
        part = pl.ds(k * step, step)
        for n, (src, dst) in enumerate(((w_gate, gate_buf), (w_up, up_buf))):
            copy = pltpu.make_async_copy(src.at[part], dst.at[part], sems.at[n, k])
            copy.start()
            copies.append(copy)
    packed = BACK_CUTS * capacity
    to = iota((group * packed, rows), 0)
    at = iota((group * packed, rows), 1)
    target = (to // packed) ^ me
    within = to % packed
    match = (at // capacity == target) & (at % capacity == within % capacity)
    selects = [
        (match & (within // capacity == cut)).astype(F32).astype(BF16) for cut in range(BACK_CUTS)
    ]
    total = [jnp.zeros((group * packed, step), F32) for _ in range(per)]
    for k in range(W_CHUNKS):
        copies[2 * k].wait()
        part = nt(da[...], gate_buf[k * step : (k + 1) * step, :])
        copies[2 * k + 1].wait()
        part += nt(db[...], up_buf[k * step : (k + 1) * step, :])
        total[k % per] += nn(selects[k // per], part.astype(BF16))
    gates = nn(selects[0], gate[...])
    for n, out in enumerate(outs):
        for q in range(per):
            out[:, q * step : (q + 1) * step] = total[q][n * packed : (n + 1) * packed].astype(BF16)
        out[:, span:] = gates[n * packed : (n + 1) * packed].astype(BF16)


def weight_kernel(block, hidden, *refs):
    buffers, out = refs[:-1], refs[-1]
    start = pl.multiple_of((lax.axis_index("dp") % 2) * block, 128)
    inputs = jnp.concatenate([ref[:, pl.ds(start, block)] for ref in buffers], axis=0)
    rows = jnp.concatenate([ref[:, pl.ds(start + 2 * block, block)] for ref in buffers], axis=0)
    base = 4 * block
    for n, left in ((0, inputs), (1, inputs), (2, rows)):
        right = jnp.concatenate(
            [ref[:, base + n * hidden : base + (n + 1) * hidden] for ref in buffers], axis=0
        )
        out[n] = tn(left, right)


def combine_kernel(group, capacity, *refs):
    backs = refs[:group]
    routes, levels, slots, input_out, gate_out = refs[group:]
    tokens, width = input_out.shape
    span = width // BACK_CUTS
    packed = BACK_CUTS * capacity
    shards = group // EXPERTS_W
    me = lax.axis_index("expert")
    every = jnp.concatenate([ref[...] for ref in backs], axis=0)
    row = iota((group * packed, tokens), 0)
    expert = ((row // packed) ^ me) // shards
    within = row % packed
    slot = jnp.where(expert == 0, slots[0:1, :], slots[1:2, :])
    match = within % capacity == slot
    for cut in range(BACK_CUTS):
        pick = (match & (within // capacity == cut)).astype(F32).astype(BF16)
        total = tn(pick, every[:, 0:span])
        input_out[:, cut * span : (cut + 1) * span] = total.astype(BF16)
        if cut == 0:
            gates = tn(every[:, span:], pick)
    for k in range(2):
        route = routes[k : k + 1, :]
        value = jnp.where(route == 0, gates[0:1, :], jnp.where(route == 1, gates[1:2, :], 0.0))
        gate_out[k : k + 1, :] = value * (16.0 / levels[k : k + 1, :].astype(F32))


def swap(array, axis, size, mask):
    return lax.ppermute(array, axis, [(n, n ^ mask) for n in range(size)])


def plain_weights(inputs, grads, rights):
    inputs = lax.all_to_all(inputs, "dp", split_axis=1, concat_axis=0, tiled=True)
    grads = lax.all_to_all(grads, "dp", split_axis=1, concat_axis=0, tiled=True)
    rights = [lax.all_gather(right, "dp", axis=0, tiled=True) for right in rights]
    return jnp.stack([tn(inputs, rights[0]), tn(inputs, rights[1]), tn(grads, rights[2])])


def per_device(grad_out, routes, gate_levels, saved_inputs, w_gate, w_up, w_down):
    group = lax.axis_size("expert")
    n_dp = lax.axis_size("dp")
    shards = group // EXPERTS_W
    rows, width = saved_inputs.shape
    capacity = rows // group
    hidden = w_gate.shape[1]
    tokens = grad_out.shape[0]
    block = width // n_dp
    paired = n_dp == PAIRED
    routes = routes.T
    gate_levels = gate_levels.T
    shape = jax.ShapeDtypeStruct
    weight_bytes = w_gate.size * 2
    product = 2 * rows * width * hidden

    packed = shape((SEND_CUTS * capacity, width // SEND_CUTS), BF16)
    own, other, slots = call(
        functools.partial(pick_kernel, shards, capacity),
        (packed, packed, shape((8, tokens), jnp.int32)),
        (routes, gate_levels, grad_out),
        [VMEM] * 3,
        flops=4 * packed.size * tokens,
        moved=grad_out.size * 2,
        name="pick",
    )
    received = [own] + [
        swap(own if mask < shards else other, "expert", group, mask) for mask in range(1, group)
    ]
    part = shape((rows, hidden), F32)
    weights_scratch = [
        pltpu.VMEM((width, hidden), BF16),
        pltpu.VMEM((width, hidden), BF16),
        pltpu.SemaphoreType.DMA((2, W_CHUNKS)),
    ]
    u, v, h = call(
        hidden_kernel,
        (part,) * 3,
        (saved_inputs, w_gate, w_up),
        [VMEM, HBM, HBM],
        weights_scratch,
        flops=2 * product,
        moved=2 * weight_bytes,
        name="hidden",
    )
    half = shape((rows, hidden), BF16)
    chips = n_dp // 2 if paired else 0
    late = shape((rows, 4 * block + 3 * hidden), BF16)
    outward = (late,) * chips if paired else (shape((rows, width), BF16), half)
    *sends, da, db, gate = call(
        functools.partial(project_kernel, group, capacity, n_dp),
        outward + (half, half, shape((rows, GATE_LANES), BF16)),
        (*received, w_down, u, v, h, saved_inputs),
        [VMEM] * group + [HBM] + [VMEM] * 4,
        [
            pltpu.VMEM((hidden, width), BF16),
            pltpu.VMEM((rows, width), BF16),
            pltpu.SemaphoreType.DMA((SEND_CUTS,)),
        ],
        flops=product,
        moved=weight_bytes,
        name="project",
    )
    back = shape((BACK_CUTS * capacity, width // BACK_CUTS + GATE_LANES), BF16)
    returns = call(
        functools.partial(input_kernel, group, capacity),
        (back,) * group,
        (da, db, gate, w_gate, w_up),
        [VMEM] * 3 + [HBM] * 2,
        weights_scratch,
        flops=2 * product,
        moved=2 * weight_bytes,
        name="input",
    )
    backs = [returns[0]] + [swap(returns[n], "expert", group, n) for n in range(1, group)]
    if paired:
        buffers = [sends[0]] + [swap(sends[m], "dp", n_dp, 2 * m) for m in range(1, chips)]
        buffers += [swap(buffer, "dp", n_dp, 1) for buffer in buffers]
        weight_grad = call(
            functools.partial(weight_kernel, block, hidden),
            shape((3, block, hidden), F32),
            buffers,
            [VMEM] * (2 * chips),
            flops=6 * n_dp * rows * block * hidden,
            moved=2 * chips * late.size * 2,
            name="weight",
        )
    else:
        weight_grad = plain_weights(saved_inputs, sends[0], (da, db, sends[1]))
    input_grad, gate_grad = call(
        functools.partial(combine_kernel, group, capacity),
        (shape((tokens, width), BF16), shape((2, tokens), F32)),
        (*backs, routes, gate_levels, slots),
        [VMEM] * (group + 3),
        flops=2 * group * back.size * tokens,
        moved=2 * tokens * width,
        name="combine",
    )
    return input_grad, gate_grad.T, weight_grad.transpose(1, 0, 2)


def solution(mesh):
    in_specs = (
        P(("dp", "expert"), None),
        P(("dp", "expert"), None),
        P(("dp", "expert"), None),
        P(("dp", "expert"), None),
        P(None, "expert"),
        P(None, "expert"),
        P("expert", None),
    )
    out_specs = (P(("dp", "expert"), None), P(("dp", "expert"), None), P("dp", None, "expert"))
    return jax.shard_map(
        per_device, mesh=mesh, in_specs=in_specs, out_specs=out_specs, check_vma=False
    )
```

```python
import functools

import jax
import jax.numpy as jnp
from jax import lax
from jax.experimental import pallas as pl
from jax.experimental.pallas import tpu as pltpu
from jax.sharding import PartitionSpec as P

EXPERTS_W = 2
SEND_CUTS = 4
BACK_CUTS = 2
GATE_LANES = 128
W_CHUNKS = 4
PAIRED = 8
F32 = jnp.float32
BF16 = jnp.bfloat16
VMEM = pl.BlockSpec(memory_space=pltpu.VMEM)
HBM = pl.BlockSpec(memory_space=pltpu.HBM)


def nn(left, right):
    return lax.dot_general(left, right, (((1,), (0,)), ((), ())), preferred_element_type=F32)


def nt(left, right):
    return lax.dot_general(left, right, (((1,), (1,)), ((), ())), preferred_element_type=F32)


def tn(left, right):
    return lax.dot_general(left, right, (((0,), (0,)), ((), ())), preferred_element_type=F32)


def iota(shape, dim):
    return lax.broadcasted_iota(jnp.int32, shape, dim)


def call(kernel, outs, args, specs, scratch=(), vmem=24, name=None):
    return pl.pallas_call(
        kernel,
        out_shape=outs,
        in_specs=specs,
        out_specs=jax.tree.map(lambda _: VMEM, outs),
        scratch_shapes=scratch,
        compiler_params=pltpu.CompilerParams(vmem_limit_bytes=vmem * 1024 * 1024),
        cost_estimate=pl.CostEstimate(flops=0, bytes_accessed=0, transcendentals=0),
        name=name,
    )(*args)


def pick_kernel(
    shards, capacity, routes_hbm, levels_hbm, grad_hbm, own_out, other_out, slots_out,
    routes, levels, grad, sems,
):
    tokens, width = grad.shape
    span = width // SEND_CUTS
    rows = SEND_CUTS * capacity
    small = [
        pltpu.make_async_copy(routes_hbm, routes, sems.at[0]),
        pltpu.make_async_copy(levels_hbm, levels, sems.at[1]),
    ]
    large = [
        pltpu.make_async_copy(
            grad_hbm.at[:, pl.ds(cut * span, span)],
            grad.at[:, pl.ds(cut * span, span)],
            sems.at[2 + cut],
        )
        for cut in range(SEND_CUTS)
    ]
    for copy in small + large:
        copy.start()
    mine = lax.axis_index("expert") // shards
    upto = (iota((tokens, tokens), 0) <= iota((tokens, tokens), 1)).astype(BF16)
    for copy in small:
        copy.wait()
    first, second = routes[0:1, :], routes[1:2, :]
    found = jnp.zeros((8, tokens), F32)
    for expert in range(EXPERTS_W):
        hit = ((first == expert) | (second == expert)).astype(F32)
        found = jnp.where(iota((8, tokens), 0) == expert, hit, found)
    counted = nn(found.astype(BF16), upto)
    slots = jnp.where(found > 0, counted - 1.0, -4096.0).astype(jnp.int32)
    slots_out[...] = slots
    slot_of, gate_of = [], []
    for expert in (mine, 1 - mine):
        level = jnp.where(first == expert, levels[0:1, :], levels[1:2, :])
        slot_of.append(jnp.where(expert == 0, slots[0:1, :], slots[1:2, :]))
        gate_of.append(level.astype(F32) * (1.0 / 16.0))
    row = iota((2 * rows, tokens), 0)
    slot = jnp.where(row < rows, slot_of[0], slot_of[1])
    gate = jnp.where(row < rows, gate_of[0], gate_of[1])
    place = row % rows
    total = jnp.zeros((2 * rows, span), F32)
    for cut in range(SEND_CUTS):
        lead = jnp.where(slot == place - cut * capacity, gate, 0.0).astype(BF16)
        large[cut].wait()
        total += nn(lead, grad[:, cut * span : (cut + 1) * span])
    own_out[...] = total[:rows].astype(BF16)
    other_out[...] = total[rows:].astype(BF16)


def hidden_kernel(inputs, w_gate, w_up, u_out, v_out, h_out, gate_buf, up_buf, sems):
    width = inputs.shape[1]
    step = width // W_CHUNKS
    copies = []
    for k in range(W_CHUNKS):
        part = pl.ds(k * step, step)
        for n, (src, dst) in enumerate(((w_gate, gate_buf), (w_up, up_buf))):
            copy = pltpu.make_async_copy(src.at[part], dst.at[part], sems.at[n, k])
            copy.start()
            copies.append(copy)
    a = jnp.zeros(u_out.shape, F32)
    b = jnp.zeros(u_out.shape, F32)
    for k in range(W_CHUNKS):
        left = inputs[:, k * step : (k + 1) * step]
        copies[2 * k].wait()
        a += nn(left, gate_buf[k * step : (k + 1) * step, :])
        copies[2 * k + 1].wait()
        b += nn(left, up_buf[k * step : (k + 1) * step, :])
    s = jax.nn.sigmoid(a)
    u = a * s
    u_out[...] = u
    v_out[...] = b * s * (1.0 + a * (1.0 - s))
    h_out[...] = u * b


def project_kernel(group, capacity, n_dp, *refs):
    received = refs[:group]
    w_down, u_in, v_in, h_in, inputs = refs[group : group + 5]
    sends = refs[group + 5 : -4]
    da_out, db_out, gate_out, rows_buf = refs[-4:]
    rows, hidden = u_in.shape
    width = w_down.shape[1]
    span = width // SEND_CUTS
    me = lax.axis_index("expert")
    packed = SEND_CUTS * capacity
    every = jnp.concatenate([ref[...] for ref in received], axis=0)
    to = iota((rows, group * packed), 0)
    at = iota((rows, group * packed), 1)
    source = (at // packed) ^ me
    within = at % packed
    match = (to // capacity == source) & (to % capacity == within % capacity)
    projected = jnp.zeros((rows, hidden), F32)
    for cut in range(SEND_CUTS):
        select = (match & (within // capacity == cut)).astype(F32).astype(BF16)
        piece = nn(select, every).astype(BF16)
        rows_buf[:, cut * span : (cut + 1) * span] = piece
        projected += nt(piece, w_down[:, cut * span : (cut + 1) * span])
    da = (projected * v_in[...]).astype(BF16)
    db = (projected * u_in[...]).astype(BF16)
    h = h_in[...]
    da_out[...] = da
    db_out[...] = db
    gate = jnp.sum(h * projected, axis=1, keepdims=True)
    lane = iota((rows, GATE_LANES), 1)
    gate_out[...] = jnp.where(lane == me // (group // EXPERTS_W), gate, 0.0).astype(BF16)
    h = h.astype(BF16)
    if n_dp != PAIRED:
        sends[0][...] = rows_buf[...]
        sends[1][...] = h
        return
    pair = 2 * (width // n_dp)
    chip = lax.axis_index("dp") // 2
    for m, send in enumerate(sends):
        start = pl.multiple_of((chip ^ m) * pair, 128)
        send[:, 0:pair] = inputs[:, pl.ds(start, pair)]
        send[:, pair : 2 * pair] = rows_buf[:, pl.ds(start, pair)]
        for n, value in enumerate((da, db, h)):
            send[:, 2 * pair + n * hidden : 2 * pair + (n + 1) * hidden] = value


def input_kernel(group, capacity, da, db, gate, w_gate, w_up, *refs):
    outs = refs
    rows = da.shape[0]
    width = w_gate.shape[0]
    span = width // BACK_CUTS
    step = width // W_CHUNKS
    per = W_CHUNKS // BACK_CUTS
    me = lax.axis_index("expert")
    packed = BACK_CUTS * capacity
    to = iota((group * packed, rows), 0)
    at = iota((group * packed, rows), 1)
    target = (to // packed) ^ me
    within = to % packed
    match = (at // capacity == target) & (at % capacity == within % capacity)
    selects = [
        (match & (within // capacity == cut)).astype(F32).astype(BF16) for cut in range(BACK_CUTS)
    ]
    total = [jnp.zeros((group * packed, step), F32) for _ in range(per)]
    for k in range(W_CHUNKS):
        part = nt(da[...], w_gate[k * step : (k + 1) * step, :])
        part += nt(db[...], w_up[k * step : (k + 1) * step, :])
        total[k % per] += nn(selects[k // per], part.astype(BF16))
    gates = nn(selects[0], gate[...])
    for n, out in enumerate(outs):
        for q in range(per):
            out[:, q * step : (q + 1) * step] = total[q][n * packed : (n + 1) * packed].astype(BF16)
        out[:, span:] = gates[n * packed : (n + 1) * packed].astype(BF16)


def share_kernel(block, chips, *refs):
    buffers, out = refs[:chips], refs[-1]
    rows = buffers[0].shape[0]
    start = pl.multiple_of((1 - lax.axis_index("dp") % 2) * block, 128)
    for m, ref in enumerate(buffers):
        part = slice(m * rows, (m + 1) * rows)
        out[part, 0:block] = ref[:, pl.ds(start, block)]
        out[part, block : 2 * block] = ref[:, pl.ds(start + 2 * block, block)]
        out[part, 2 * block :] = ref[:, 4 * block :]


def weight_kernel(block, hidden, chips, *refs):
    buffers, shared, out = refs[:chips], refs[chips], refs[-1]
    start = pl.multiple_of((lax.axis_index("dp") % 2) * block, 128)
    lefts = [
        jnp.concatenate([ref[:, pl.ds(start + at, block)] for ref in buffers], axis=0)
        for at in (0, 2 * block)
    ]
    for n in range(3):
        at = 4 * block + n * hidden
        right = jnp.concatenate([ref[:, at : at + hidden] for ref in buffers], axis=0)
        total = tn(lefts[n // 2], right)
        left = shared[:, (n // 2) * block : (n // 2 + 1) * block]
        at -= 2 * block
        out[n] = total + tn(left, shared[:, at : at + hidden])


def combine_kernel(group, capacity, *refs):
    backs = refs[:group]
    routes, levels, slots, _, input_out, gate_out = refs[group:]
    tokens, width = input_out.shape
    span = width // BACK_CUTS
    packed = BACK_CUTS * capacity
    shards = group // EXPERTS_W
    me = lax.axis_index("expert")
    every = jnp.concatenate([ref[...] for ref in backs], axis=0)
    row = iota((group * packed, tokens), 0)
    expert = ((row // packed) ^ me) // shards
    within = row % packed
    slot = jnp.where(expert == 0, slots[0:1, :], slots[1:2, :])
    match = within % capacity == slot
    for cut in range(BACK_CUTS):
        pick = (match & (within // capacity == cut)).astype(F32).astype(BF16)
        total = tn(pick, every[:, 0:span])
        input_out[:, cut * span : (cut + 1) * span] = total.astype(BF16)
        if cut == 0:
            gates = tn(every[:, span:], pick)
    for k in range(2):
        route = routes[k : k + 1, :]
        value = jnp.where(route == 0, gates[0:1, :], jnp.where(route == 1, gates[1:2, :], 0.0))
        gate_out[k : k + 1, :] = value * (16.0 / levels[k : k + 1, :].astype(F32))


def swap(array, axis, size, mask):
    return lax.ppermute(array, axis, [(n, n ^ mask) for n in range(size)])


def plain_weights(inputs, grads, rights):
    inputs = lax.all_to_all(inputs, "dp", split_axis=1, concat_axis=0, tiled=True)
    grads = lax.all_to_all(grads, "dp", split_axis=1, concat_axis=0, tiled=True)
    rights = [lax.all_gather(right, "dp", axis=0, tiled=True) for right in rights]
    return jnp.stack([tn(inputs, rights[0]), tn(inputs, rights[1]), tn(grads, rights[2])])


def per_device(grad_out, routes, gate_levels, saved_inputs, w_gate, w_up, w_down):
    group = lax.axis_size("expert")
    n_dp = lax.axis_size("dp")
    shards = group // EXPERTS_W
    rows, width = saved_inputs.shape
    capacity = rows // group
    hidden = w_gate.shape[1]
    tokens = grad_out.shape[0]
    block = width // n_dp
    paired = n_dp == PAIRED
    routes = routes.T
    gate_levels = gate_levels.T
    shape = jax.ShapeDtypeStruct

    packed = shape((SEND_CUTS * capacity, width // SEND_CUTS), BF16)
    own, other, slots = call(
        functools.partial(pick_kernel, shards, capacity),
        (packed, packed, shape((8, tokens), jnp.int32)),
        (routes, gate_levels, grad_out),
        [HBM] * 3,
        [
            pltpu.VMEM(routes.shape, jnp.int32),
            pltpu.VMEM(routes.shape, jnp.int32),
            pltpu.VMEM(grad_out.shape, BF16),
            pltpu.SemaphoreType.DMA((2 + SEND_CUTS,)),
        ],
        vmem=60,
        name="pick",
    )
    received = [own] + [
        swap(own if mask < shards else other, "expert", group, mask) for mask in range(1, group)
    ]
    part = shape((rows, hidden), F32)
    chips = n_dp // 2 if paired else 1
    weight = shape((width, hidden), BF16)
    u, v, h, near_gate, near_up = call(
        hidden_kernel,
        (part,) * 3 + (weight,) * 2,
        (saved_inputs, w_gate, w_up),
        [VMEM, HBM, HBM],
        [pltpu.SemaphoreType.DMA((2, W_CHUNKS))],
        vmem=47,
        name="hidden",
    )
    half = shape((rows, hidden), BF16)
    late = shape((rows, 4 * block + 3 * hidden), BF16)
    outward = (late,) * chips if paired else (shape((rows, width), BF16), half)
    *sends, da, db, gate = call(
        functools.partial(project_kernel, group, capacity, n_dp),
        outward + (half, half, shape((rows, GATE_LANES), BF16)),
        (*received, w_down, u, v, h, saved_inputs),
        [VMEM] * (group + 5),
        [pltpu.VMEM((rows, width), BF16)],
        name="project",
    )
    back = shape((BACK_CUTS * capacity, width // BACK_CUTS + GATE_LANES), BF16)
    returns = call(
        functools.partial(input_kernel, group, capacity),
        (back,) * group,
        (da, db, gate, near_gate, near_up),
        [VMEM] * 5,
        name="input",
    )
    backs = [returns[0]] + [swap(returns[n], "expert", group, n) for n in range(1, group)]
    if paired:
        buffers = [sends[0]] + [swap(sends[m], "dp", n_dp, 2 * m) for m in range(1, chips)]
        sharing = call(
            functools.partial(share_kernel, block, chips),
            shape((chips * rows, 2 * block + 3 * hidden), BF16),
            (*buffers, *backs[1:]),
            [VMEM] * chips + [HBM] * (group - 1),
            name="share",
        )
        shared = swap(sharing, "dp", n_dp, 1)
        weight_grad = call(
            functools.partial(weight_kernel, block, hidden, chips),
            shape((3, block, hidden), F32),
            (*buffers, shared),
            [VMEM] * (chips + 1),
            name="weight",
        )
    else:
        sharing = returns[group - 1]
        weight_grad = plain_weights(saved_inputs, sends[0], (da, db, sends[1]))
    input_grad, gate_grad = call(
        functools.partial(combine_kernel, group, capacity),
        (shape((tokens, width), BF16), shape((2, tokens), F32)),
        (*backs, routes, gate_levels, slots, sharing),
        [VMEM] * (group + 3) + [HBM],
        name="combine",
    )
    return input_grad, gate_grad.T, weight_grad.transpose(1, 0, 2)


def solution(mesh):
    in_specs = (
        P(("dp", "expert"), None),
        P(("dp", "expert"), None),
        P(("dp", "expert"), None),
        P(("dp", "expert"), None),
        P(None, "expert"),
        P(None, "expert"),
        P("expert", None),
    )
    out_specs = (P(("dp", "expert"), None), P(("dp", "expert"), None), P("dp", None, "expert"))
    return jax.shard_map(
        per_device, mesh=mesh, in_specs=in_specs, out_specs=out_specs, check_vma=False
    )
```

```python
import functools

import jax
import jax.numpy as jnp
from jax import lax
from jax.experimental import pallas as pl
from jax.experimental.pallas import tpu as pltpu
from jax.sharding import PartitionSpec as P

EXPERTS_W = 2
SEND_CUTS = 4
BACK_CUTS = 2
GATE_LANES = 128
W_CHUNKS = 4
EARLY = (1, 2, 3)
DISPATCH_ORDER = (0, 3, 2, 1)
PAIRED = 8
F32 = jnp.float32
BF16 = jnp.bfloat16
VMEM = pl.BlockSpec(memory_space=pltpu.VMEM)
HBM = pl.BlockSpec(memory_space=pltpu.HBM)
UNUSED = pl.BlockSpec(memory_space=pl.ANY)


def nn(left, right):
    return lax.dot_general(left, right, (((1,), (0,)), ((), ())), preferred_element_type=F32)


def nt(left, right):
    return lax.dot_general(left, right, (((1,), (1,)), ((), ())), preferred_element_type=F32)


def tn(left, right):
    return lax.dot_general(left, right, (((0,), (0,)), ((), ())), preferred_element_type=F32)


def iota(shape, dim):
    return lax.broadcasted_iota(jnp.int32, shape, dim)


def call(kernel, outs, args, specs, scratch=(), near=True, out_specs=None, name=None):
    args = [
        pltpu.with_memory_space_constraint(arg, pltpu.HBM) if spec is HBM else arg
        for arg, spec in zip(args, specs)
    ]
    if near:
        outs = jax.tree.map(lambda out: pltpu.VMEM(out.shape, out.dtype), outs)
    return pl.pallas_call(
        kernel,
        out_shape=outs,
        in_specs=specs,
        out_specs=out_specs or jax.tree.map(lambda _: VMEM, outs),
        scratch_shapes=scratch,
        compiler_params=pltpu.CompilerParams(vmem_limit_bytes=24 * 1024 * 1024),
        cost_estimate=pl.CostEstimate(flops=0, bytes_accessed=0, transcendentals=0),
        name=name,
    )(*args)


def order(count):
    return DISPATCH_ORDER if count == 4 else range(count)


def arrange(arrays):
    return [arrays[mask] for mask in order(len(arrays))]


def restore(refs):
    places = list(order(len(refs)))
    return [refs[places.index(mask)] for mask in range(len(refs))]


def pick_kernel(
    shards, capacity, routes_hbm, levels_hbm, grad_hbm, own_out, other_out, slots_out,
    routes, levels, grad, sems,
):
    tokens, width = grad.shape
    span = width // SEND_CUTS
    rows = SEND_CUTS * capacity
    small = [
        pltpu.make_async_copy(routes_hbm, routes, sems.at[0]),
        pltpu.make_async_copy(levels_hbm, levels, sems.at[1]),
    ]
    large = [
        pltpu.make_async_copy(
            grad_hbm.at[:, pl.ds(cut * span, span)],
            grad.at[:, pl.ds(cut * span, span)],
            sems.at[2 + cut],
        )
        for cut in range(SEND_CUTS)
    ]
    for copy in small + large:
        copy.start()
    mine = lax.axis_index("expert") // shards
    upto = (iota((tokens, tokens), 0) <= iota((tokens, tokens), 1)).astype(BF16)
    for copy in small:
        copy.wait()
    first, second = routes[0:1, :], routes[1:2, :]
    found = jnp.zeros((8, tokens), F32)
    for expert in range(EXPERTS_W):
        hit = ((first == expert) | (second == expert)).astype(F32)
        found = jnp.where(iota((8, tokens), 0) == expert, hit, found)
    counted = nn(found.astype(BF16), upto)
    slots = jnp.where(found > 0, counted - 1.0, -4096.0).astype(jnp.int32)
    slots_out[...] = slots
    slot_of, gate_of = [], []
    for expert in (mine, 1 - mine):
        level = jnp.where(first == expert, levels[0:1, :], levels[1:2, :])
        slot_of.append(jnp.where(expert == 0, slots[0:1, :], slots[1:2, :]))
        gate_of.append(level.astype(F32) * (1.0 / 16.0))
    row = iota((2 * rows, tokens), 0)
    slot = jnp.where(row < rows, slot_of[0], slot_of[1])
    gate = jnp.where(row < rows, gate_of[0], gate_of[1])
    place = row % rows
    total = jnp.zeros((2 * rows, span), F32)
    for cut in range(SEND_CUTS):
        lead = jnp.where(slot == place - cut * capacity, gate, 0.0).astype(BF16)
        large[cut].wait()
        total += nn(lead, grad[:, cut * span : (cut + 1) * span])
    own_out[...] = total[:rows].astype(BF16)
    other_out[...] = total[rows:].astype(BF16)


def hidden_kernel(
    inputs_hbm, w_gate, w_up, u_out, v_out, h_out, inputs, gate_buf, up_buf, sems
):
    first = pltpu.make_async_copy(inputs_hbm, inputs, sems.at[2, 0])
    first.start()
    width = inputs.shape[1]
    step = width // W_CHUNKS
    copies = []
    for k in range(W_CHUNKS):
        part = pl.ds(k * step, step)
        for n, (src, dst) in enumerate(((w_gate, gate_buf), (w_up, up_buf))):
            copy = pltpu.make_async_copy(src.at[part], dst.at[part], sems.at[n, k])
            copy.start()
            copies.append(copy)
    first.wait()
    a = jnp.zeros(u_out.shape, F32)
    b = jnp.zeros(u_out.shape, F32)
    for k in range(W_CHUNKS):
        left = inputs[:, k * step : (k + 1) * step]
        copies[2 * k].wait()
        a += nn(left, gate_buf[k * step : (k + 1) * step, :])
        copies[2 * k + 1].wait()
        b += nn(left, up_buf[k * step : (k + 1) * step, :])
    s = jax.nn.sigmoid(a)
    u = a * s
    u_out[...] = u
    v_out[...] = b * s * (1.0 + a * (1.0 - s))
    h_out[...] = u * b


def project_kernel(group, capacity, n_dp, *refs):
    received = restore(refs[:group])
    w_down, u_in, v_in, h_in, inputs = refs[group : group + 5]
    sends = refs[group + 5 : -4]
    da_out, db_out, gate_out, rows_buf = refs[-4:]
    rows, hidden = u_in.shape
    width = w_down.shape[1]
    span = width // SEND_CUTS
    me = lax.axis_index("expert")
    packed = SEND_CUTS * capacity
    every = jnp.concatenate([ref[...] for ref in received], axis=0)
    to = iota((rows, group * packed), 0)
    at = iota((rows, group * packed), 1)
    source = (at // packed) ^ me
    within = at % packed
    match = (to // capacity == source) & (to % capacity == within % capacity)
    projected = jnp.zeros((rows, hidden), F32)
    for cut in range(SEND_CUTS):
        select = (match & (within // capacity == cut)).astype(F32).astype(BF16)
        piece = nn(select, every).astype(BF16)
        rows_buf[:, cut * span : (cut + 1) * span] = piece
        projected += nt(piece, w_down[:, cut * span : (cut + 1) * span])
    da = (projected * v_in[...]).astype(BF16)
    db = (projected * u_in[...]).astype(BF16)
    h = h_in[...]
    da_out[...] = da
    db_out[...] = db
    gate = jnp.sum(h * projected, axis=1, keepdims=True)
    lane = iota((rows, GATE_LANES), 1)
    gate_out[...] = jnp.where(lane == me // (group // EXPERTS_W), gate, 0.0).astype(BF16)
    h = h.astype(BF16)
    if n_dp != PAIRED:
        sends[0][...] = rows_buf[...]
        sends[1][...] = h
        return
    pair = 2 * (width // n_dp)
    chip = lax.axis_index("dp") // 2
    for m, send in enumerate(sends):
        start = pl.multiple_of((chip ^ m) * pair, 128)
        send[:, 0:pair] = inputs[:, pl.ds(start, pair)]
        send[:, pair : 2 * pair] = rows_buf[:, pl.ds(start, pair)]
        for n, value in enumerate((da, db, h)):
            send[:, 2 * pair + n * hidden : 2 * pair + (n + 1) * hidden] = value


def input_kernel(group, capacity, da, db, gate, w_gate, w_up, *refs):
    outs = refs[-group:]
    rows = da.shape[0]
    width = w_gate.shape[0]
    span = width // BACK_CUTS
    step = width // W_CHUNKS
    per = W_CHUNKS // BACK_CUTS
    me = lax.axis_index("expert")
    packed = BACK_CUTS * capacity
    to = iota((group * packed, rows), 0)
    at = iota((group * packed, rows), 1)
    target = (to // packed) ^ me
    within = to % packed
    match = (at // capacity == target) & (at % capacity == within % capacity)
    selects = [
        (match & (within // capacity == cut)).astype(F32).astype(BF16) for cut in range(BACK_CUTS)
    ]
    total = [jnp.zeros((group * packed, step), F32) for _ in range(per)]
    for k in range(W_CHUNKS):
        part = nt(da[...], w_gate[k * step : (k + 1) * step, :])
        part += nt(db[...], w_up[k * step : (k + 1) * step, :])
        total[k % per] += nn(selects[k // per], part.astype(BF16))
    gates = nn(selects[0], gate[...])
    for n, out in enumerate(outs):
        for q in range(per):
            out[:, q * step : (q + 1) * step] = total[q][n * packed : (n + 1) * packed].astype(BF16)
        out[:, span:] = gates[n * packed : (n + 1) * packed].astype(BF16)


def share_kernel(block, chips, *refs):
    buffers, out = refs[:chips], refs[-1]
    rows = buffers[0].shape[0]
    start = pl.multiple_of((1 - lax.axis_index("dp") % 2) * block, 128)
    for m, ref in enumerate(buffers):
        part = slice(m * rows, (m + 1) * rows)
        out[part, 0:block] = ref[:, pl.ds(start, block)]
        out[part, block : 2 * block] = ref[:, pl.ds(start + 2 * block, block)]
        out[part, 2 * block :] = ref[:, 4 * block :]


def weight_kernel(block, hidden, chips, *refs):
    buffers, out = refs[:chips], refs[-1]
    start = pl.multiple_of((lax.axis_index("dp") % 2) * block, 128)
    lefts = [
        jnp.concatenate([ref[:, pl.ds(start + at, block)] for ref in buffers], axis=0)
        for at in (0, 2 * block)
    ]
    for n in range(3):
        at = 4 * block + n * hidden
        right = jnp.concatenate([ref[:, at : at + hidden] for ref in buffers], axis=0)
        out[n] = tn(lefts[n // 2], right)


def finish_kernel(block, hidden, partial, shared, out_hbm, buf, sems):
    copies = []
    for n in range(3):
        left = shared[:, (n // 2) * block : (n // 2 + 1) * block]
        at = 2 * block + n * hidden
        buf[n] = partial[n] + tn(left, shared[:, at : at + hidden])
        copies.append(pltpu.make_async_copy(buf.at[n], out_hbm.at[n], sems.at[n]))
        copies[-1].start()
    for copy in copies:
        copy.wait()


def combine_kernel(group, capacity, *refs):
    backs = refs[:group]
    routes, levels, slots, _, input_hbm, gate_out, input_buf, sems = refs[group:]
    tokens, width = input_buf.shape
    span = width // BACK_CUTS
    packed = BACK_CUTS * capacity
    shards = group // EXPERTS_W
    me = lax.axis_index("expert")
    every = jnp.concatenate([ref[...] for ref in backs], axis=0)
    row = iota((group * packed, tokens), 0)
    expert = ((row // packed) ^ me) // shards
    within = row % packed
    slot = jnp.where(expert == 0, slots[0:1, :], slots[1:2, :])
    match = within % capacity == slot
    copies = []
    for cut in range(BACK_CUTS):
        pick = (match & (within // capacity == cut)).astype(F32).astype(BF16)
        half = span // 2
        for at in (0, half):
            part = pl.ds(cut * span + at, half)
            input_buf[:, part] = tn(pick, every[:, at : at + half]).astype(BF16)
            copies.append(
                pltpu.make_async_copy(
                    input_buf.at[:, part], input_hbm.at[:, part], sems.at[len(copies)]
                )
            )
            copies[-1].start()
        if cut == 0:
            gates = tn(every[:, span:], pick)
    for k in range(2):
        route = routes[k : k + 1, :]
        value = jnp.where(route == 0, gates[0:1, :], jnp.where(route == 1, gates[1:2, :], 0.0))
        gate_out[k : k + 1, :] = value * (16.0 / levels[k : k + 1, :].astype(F32))
    for copy in copies:
        copy.wait()


def swap(array, axis, size, mask):
    return lax.ppermute(array, axis, [(n, n ^ mask) for n in range(size)])


def far_first(group):
    return [*range(group // 2, group), *range(1, group // 2)]


def plain_weights(inputs, grads, rights):
    inputs = lax.all_to_all(inputs, "dp", split_axis=1, concat_axis=0, tiled=True)
    grads = lax.all_to_all(grads, "dp", split_axis=1, concat_axis=0, tiled=True)
    rights = [lax.all_gather(right, "dp", axis=0, tiled=True) for right in rights]
    return jnp.stack([tn(inputs, rights[0]), tn(inputs, rights[1]), tn(grads, rights[2])])


def per_device(grad_out, routes, gate_levels, saved_inputs, w_gate, w_up, w_down):
    group = lax.axis_size("expert")
    n_dp = lax.axis_size("dp")
    shards = group // EXPERTS_W
    rows, width = saved_inputs.shape
    capacity = rows // group
    hidden = w_gate.shape[1]
    tokens = grad_out.shape[0]
    block = width // n_dp
    paired = n_dp == PAIRED
    routes = routes.T
    gate_levels = gate_levels.T
    shape = jax.ShapeDtypeStruct

    packed = shape((SEND_CUTS * capacity, width // SEND_CUTS), BF16)
    own, other, slots = call(
        functools.partial(pick_kernel, shards, capacity),
        (packed, packed, shape((8, tokens), jnp.int32)),
        (routes, gate_levels, grad_out),
        [HBM] * 3,
        [
            pltpu.VMEM(routes.shape, jnp.int32),
            pltpu.VMEM(routes.shape, jnp.int32),
            pltpu.VMEM(grad_out.shape, BF16),
            pltpu.SemaphoreType.DMA((2 + SEND_CUTS,)),
        ],
        name="pick",
    )
    received = [own] + [None] * (group - 1)
    for mask in far_first(group):
        received[mask] = swap(own if mask < shards else other, "expert", group, mask)
    part = shape((rows, hidden), F32)
    weight = shape((width, hidden), BF16)
    u, v, h, near_inputs, near_gate, near_up = call(
        hidden_kernel,
        (part,) * 3 + (shape((rows, width), BF16),) + (weight,) * 2,
        (saved_inputs, w_gate, w_up),
        [HBM] * 3,
        [pltpu.SemaphoreType.DMA((3, W_CHUNKS))],
        name="hidden",
    )
    half = shape((rows, hidden), BF16)
    chips = n_dp // 2 if paired else 0
    late = shape((rows, 4 * block + 3 * hidden), BF16)
    outward = (late,) * chips if paired else (shape((rows, width), BF16), half)
    *sends, da, db, gate = call(
        functools.partial(project_kernel, group, capacity, n_dp),
        outward + (half, half, shape((rows, GATE_LANES), BF16)),
        (*arrange(received), w_down, u, v, h, near_inputs),
        [VMEM] * (group + 5),
        [pltpu.VMEM((rows, width), BF16)],
        name="project",
    )
    back = shape((BACK_CUTS * capacity, width // BACK_CUTS + GATE_LANES), BF16)
    returns = call(
        functools.partial(input_kernel, group, capacity),
        (back,) * group,
        (da, db, gate, near_gate, near_up),
        [VMEM] * 5,
        name="input",
    )
    backs = [returns[0]] + [None] * (group - 1)
    for mask in far_first(group):
        backs[mask] = swap(returns[mask], "expert", group, mask)
    if paired:
        buffers = [sends[0]] + [swap(sends[m], "dp", n_dp, 2 * m) for m in range(1, chips)]
        sharing = call(
            functools.partial(share_kernel, block, chips),
            shape((chips * rows, 2 * block + 3 * hidden), BF16),
            (*buffers, *[backs[mask] for mask in EARLY]),
            [VMEM] * chips + [UNUSED] * len(EARLY),
            name="share",
        )
        shared = swap(sharing, "dp", n_dp, 1)
        block_shape = shape((3, block, hidden), F32)
        partial = call(
            functools.partial(weight_kernel, block, hidden, chips),
            block_shape,
            buffers,
            [VMEM] * chips,
            name="weight",
        )
        weight_grad = call(
            functools.partial(finish_kernel, block, hidden),
            block_shape,
            (partial, shared),
            [VMEM] * 2,
            [pltpu.VMEM(block_shape.shape, F32), pltpu.SemaphoreType.DMA((3,))],
            near=False,
            out_specs=HBM,
            name="finish",
        )
    else:
        sharing = returns[0]
        weight_grad = plain_weights(saved_inputs, sends[0], (da, db, sends[1]))
    input_grad, gate_grad = call(
        functools.partial(combine_kernel, group, capacity),
        (shape((tokens, width), BF16), shape((2, tokens), F32)),
        (*backs, routes, gate_levels, slots, sharing),
        [VMEM] * (group + 3) + [UNUSED],
        [pltpu.VMEM((tokens, width), BF16), pltpu.SemaphoreType.DMA((2 * BACK_CUTS,))],
        near=False,
        out_specs=(HBM, VMEM),
        name="combine",
    )
    return input_grad, gate_grad.T, weight_grad.transpose(1, 0, 2)


def solution(mesh):
    in_specs = (
        P(("dp", "expert"), None),
        P(("dp", "expert"), None),
        P(("dp", "expert"), None),
        P(("dp", "expert"), None),
        P(None, "expert"),
        P(None, "expert"),
        P("expert", None),
    )
    out_specs = (P(("dp", "expert"), None), P(("dp", "expert"), None), P("dp", None, "expert"))
    return jax.shard_map(
        per_device, mesh=mesh, in_specs=in_specs, out_specs=out_specs, check_vma=False
    )
```

```python
import functools

import jax
import jax.numpy as jnp
from jax import lax
from jax.experimental import pallas as pl
from jax.experimental.pallas import tpu as pltpu
from jax.sharding import PartitionSpec as P

EXPERTS_W = 2
SEND_CUTS = 4
BACK_CUTS = 2
GATE_LANES = 128
W_CHUNKS = 4
LAST = 3
HEAVY = 10**11
DISPATCH_ORDER = (0, 3, 2, 1)
PAIRED = 8
F32 = jnp.float32
BF16 = jnp.bfloat16
VMEM = pl.BlockSpec(memory_space=pltpu.VMEM)
HBM = pl.BlockSpec(memory_space=pltpu.HBM)
UNUSED = pl.BlockSpec(memory_space=pl.ANY)


def nn(left, right):
    return lax.dot_general(left, right, (((1,), (0,)), ((), ())), preferred_element_type=F32)


def nt(left, right):
    return lax.dot_general(left, right, (((1,), (1,)), ((), ())), preferred_element_type=F32)


def tn(left, right):
    return lax.dot_general(left, right, (((0,), (0,)), ((), ())), preferred_element_type=F32)


def iota(shape, dim):
    return lax.broadcasted_iota(jnp.int32, shape, dim)


def call(kernel, outs, args, specs, scratch=(), near=True, out_specs=None, flops=0, name=None):
    args = [
        pltpu.with_memory_space_constraint(arg, pltpu.HBM) if spec is HBM else arg
        for arg, spec in zip(args, specs)
    ]
    if near:
        outs = jax.tree.map(lambda out: pltpu.VMEM(out.shape, out.dtype), outs)
    return pl.pallas_call(
        kernel,
        out_shape=outs,
        in_specs=specs,
        out_specs=out_specs or jax.tree.map(lambda _: VMEM, outs),
        scratch_shapes=scratch,
        compiler_params=pltpu.CompilerParams(vmem_limit_bytes=24 * 1024 * 1024),
        cost_estimate=pl.CostEstimate(flops=flops, bytes_accessed=0, transcendentals=0),
        name=name,
    )(*args)


def order(count):
    return DISPATCH_ORDER if count == 4 else range(count)


def arrange(arrays):
    return [arrays[mask] for mask in order(len(arrays))]


def restore(refs):
    places = list(order(len(refs)))
    return [refs[places.index(mask)] for mask in range(len(refs))]


def pick_kernel(
    shards, capacity, routes_hbm, levels_hbm, grad_hbm, own_out, other_out, slots_out,
    routes, levels, grad, sems,
):
    tokens, width = grad.shape
    span = width // SEND_CUTS
    rows = SEND_CUTS * capacity
    small = [
        pltpu.make_async_copy(routes_hbm, routes, sems.at[0]),
        pltpu.make_async_copy(levels_hbm, levels, sems.at[1]),
    ]
    large = [
        pltpu.make_async_copy(
            grad_hbm.at[:, pl.ds(cut * span, span)],
            grad.at[:, pl.ds(cut * span, span)],
            sems.at[2 + cut],
        )
        for cut in range(SEND_CUTS)
    ]
    for copy in small + large:
        copy.start()
    mine = lax.axis_index("expert") // shards
    upto = (iota((tokens, tokens), 0) <= iota((tokens, tokens), 1)).astype(BF16)
    for copy in small:
        copy.wait()
    first, second = routes[0:1, :], routes[1:2, :]
    found = jnp.zeros((8, tokens), F32)
    for expert in range(EXPERTS_W):
        hit = ((first == expert) | (second == expert)).astype(F32)
        found = jnp.where(iota((8, tokens), 0) == expert, hit, found)
    counted = nn(found.astype(BF16), upto)
    slots = jnp.where(found > 0, counted - 1.0, -4096.0).astype(jnp.int32)
    slots_out[...] = slots
    slot_of, gate_of = [], []
    for expert in (mine, 1 - mine):
        level = jnp.where(first == expert, levels[0:1, :], levels[1:2, :])
        slot_of.append(jnp.where(expert == 0, slots[0:1, :], slots[1:2, :]))
        gate_of.append(level.astype(F32) * (1.0 / 16.0))
    row = iota((2 * rows, tokens), 0)
    slot = jnp.where(row < rows, slot_of[0], slot_of[1])
    gate = jnp.where(row < rows, gate_of[0], gate_of[1])
    place = row % rows
    total = jnp.zeros((2 * rows, span), F32)
    for cut in range(SEND_CUTS):
        lead = jnp.where(slot == place - cut * capacity, gate, 0.0).astype(BF16)
        large[cut].wait()
        total += nn(lead, grad[:, cut * span : (cut + 1) * span])
    own_out[...] = total[:rows].astype(BF16)
    other_out[...] = total[rows:].astype(BF16)


def hidden_kernel(n_dp, inputs_hbm, w_gate, w_up, *refs):
    ahead, (u_out, v_out, h_out, inputs, gate_buf, up_buf, sems) = refs[:-7], refs[-7:]
    first = pltpu.make_async_copy(inputs_hbm, inputs, sems.at[2, 0])
    first.start()
    width = inputs.shape[1]
    step = width // W_CHUNKS
    copies = []
    for k in range(W_CHUNKS):
        part = pl.ds(k * step, step)
        for n, (src, dst) in enumerate(((w_gate, gate_buf), (w_up, up_buf))):
            copy = pltpu.make_async_copy(src.at[part], dst.at[part], sems.at[n, k])
            copy.start()
            copies.append(copy)
    first.wait()
    a = jnp.zeros(u_out.shape, F32)
    b = jnp.zeros(u_out.shape, F32)
    for k in range(W_CHUNKS):
        left = inputs[:, k * step : (k + 1) * step]
        copies[2 * k].wait()
        a += nn(left, gate_buf[k * step : (k + 1) * step, :])
        copies[2 * k + 1].wait()
        b += nn(left, up_buf[k * step : (k + 1) * step, :])
    s = jax.nn.sigmoid(a)
    u = a * s
    u_out[...] = u
    v_out[...] = b * s * (1.0 + a * (1.0 - s))
    h = u * b
    h_out[...] = h
    pair = 2 * (width // n_dp)
    for m, out in enumerate(ahead):
        start = pl.multiple_of(((lax.axis_index("dp") // 2) ^ m) * pair, 128)
        out[:, 0:pair] = inputs[:, pl.ds(start, pair)]
        out[:, pair:] = h.astype(BF16)


def project_kernel(group, capacity, n_dp, *refs):
    received = restore(refs[:group])
    w_down, u_in, v_in, h_in, inputs = refs[group : group + 5]
    sends = refs[group + 5 : -4]
    da_out, db_out, gate_out, rows_buf = refs[-4:]
    rows, hidden = u_in.shape
    width = w_down.shape[1]
    span = width // SEND_CUTS
    me = lax.axis_index("expert")
    packed = SEND_CUTS * capacity
    every = jnp.concatenate([ref[...] for ref in received], axis=0)
    to = iota((rows, group * packed), 0)
    at = iota((rows, group * packed), 1)
    source = (at // packed) ^ me
    within = at % packed
    match = (to // capacity == source) & (to % capacity == within % capacity)
    projected = jnp.zeros((rows, hidden), F32)
    for cut in range(SEND_CUTS):
        select = (match & (within // capacity == cut)).astype(F32).astype(BF16)
        piece = nn(select, every).astype(BF16)
        rows_buf[:, cut * span : (cut + 1) * span] = piece
        projected += nt(piece, w_down[:, cut * span : (cut + 1) * span])
    da = (projected * v_in[...]).astype(BF16)
    db = (projected * u_in[...]).astype(BF16)
    h = h_in[...]
    da_out[...] = da
    db_out[...] = db
    gate = jnp.sum(h * projected, axis=1, keepdims=True)
    lane = iota((rows, GATE_LANES), 1)
    gate_out[...] = jnp.where(lane == me // (group // EXPERTS_W), gate, 0.0).astype(BF16)
    h = h.astype(BF16)
    if n_dp != PAIRED:
        sends[0][...] = rows_buf[...]
        sends[1][...] = h
        return
    pair = 2 * (width // n_dp)
    chip = lax.axis_index("dp") // 2
    for m, send in enumerate(sends):
        start = pl.multiple_of((chip ^ m) * pair, 128)
        base = 0
        if m == LAST:
            send[:, 0:pair] = inputs[:, pl.ds(start, pair)]
            send[:, pair : pair + hidden] = h
            base = pair + hidden
        send[:, base : base + pair] = rows_buf[:, pl.ds(start, pair)]
        send[:, base + pair : base + pair + hidden] = da
        send[:, base + pair + hidden :] = db


def input_kernel(group, capacity, da, db, gate, w_gate, w_up, *refs):
    outs = refs[-group:]
    rows = da.shape[0]
    width = w_gate.shape[0]
    span = width // BACK_CUTS
    step = width // W_CHUNKS
    per = W_CHUNKS // BACK_CUTS
    me = lax.axis_index("expert")
    packed = BACK_CUTS * capacity
    to = iota((group * packed, rows), 0)
    at = iota((group * packed, rows), 1)
    target = (to // packed) ^ me
    within = to % packed
    match = (at // capacity == target) & (at % capacity == within % capacity)
    selects = [
        (match & (within // capacity == cut)).astype(F32).astype(BF16) for cut in range(BACK_CUTS)
    ]
    total = [jnp.zeros((group * packed, step), F32) for _ in range(per)]
    for k in range(W_CHUNKS):
        part = nt(da[...], w_gate[k * step : (k + 1) * step, :])
        part += nt(db[...], w_up[k * step : (k + 1) * step, :])
        total[k % per] += nn(selects[k // per], part.astype(BF16))
    gates = nn(selects[0], gate[...])
    for n, out in enumerate(outs):
        for q in range(per):
            out[:, q * step : (q + 1) * step] = total[q][n * packed : (n + 1) * packed].astype(BF16)
        out[:, span:] = gates[n * packed : (n + 1) * packed].astype(BF16)


def halves(columns, refs):
    first = [(ref, 0) for ref in (*refs[:LAST], refs[-1])]
    second = [(ref, 0) for ref in refs[LAST:-1]] + [(refs[-1], columns)]
    return first, second


def share_kernel(block, hidden, *refs):
    buffers, out = refs[:-1], refs[-1]
    rows = buffers[0].shape[0]
    start = (1 - lax.axis_index("dp") % 2) * block
    first, second = halves(2 * block + hidden, buffers)
    middle = block + hidden
    for m in range(LAST + 1):
        part = slice(m * rows, (m + 1) * rows)
        for (ref, at), to, wide in ((first[m], 0, middle), (second[m], middle, middle + hidden)):
            out[part, to : to + block] = ref[:, pl.ds(pl.multiple_of(at + start, 128), block)]
            at += 2 * block
            out[part, to + block : to + wide] = ref[:, at : at + wide - block]


def weight_kernel(block, hidden, *refs):
    buffers, out = refs[:-1], refs[-1]
    start = (lax.axis_index("dp") % 2) * block
    first, second = halves(2 * block + hidden, buffers)

    def gather(side, skip, wide):
        parts = [ref[:, pl.ds(pl.multiple_of(at + skip, 128), wide)] for ref, at in side]
        return jnp.concatenate(parts, axis=0)

    inputs, grads = gather(first, start, block), gather(second, start, block)
    out[0] = tn(inputs, gather(second, 2 * block, hidden))
    out[1] = tn(inputs, gather(second, 2 * block + hidden, hidden))
    out[2] = tn(grads, gather(first, 2 * block, hidden))


def finish_kernel(block, hidden, partial, shared, out_hbm, buf, sems):
    middle = block + hidden
    inputs, h = shared[:, 0:block], shared[:, block:middle]
    grads, da = shared[:, middle : middle + block], shared[:, middle + block : 2 * middle]
    copies = []
    for n, (left, right) in enumerate(((inputs, da), (inputs, shared[:, 2 * middle :]), (grads, h))):
        buf[n] = partial[n] + tn(left, right)
        copies.append(pltpu.make_async_copy(buf.at[n], out_hbm.at[n], sems.at[n]))
        copies[-1].start()
    for copy in copies:
        copy.wait()


def combine_kernel(group, capacity, *refs):
    backs = refs[:group]
    routes, levels, slots = refs[group : group + 3]
    input_hbm, gate_out, input_buf, sems = refs[-4:]
    tokens, width = input_buf.shape
    span = width // BACK_CUTS
    packed = BACK_CUTS * capacity
    shards = group // EXPERTS_W
    me = lax.axis_index("expert")
    every = jnp.concatenate([ref[...] for ref in backs], axis=0)
    row = iota((group * packed, tokens), 0)
    expert = ((row // packed) ^ me) // shards
    within = row % packed
    slot = jnp.where(expert == 0, slots[0:1, :], slots[1:2, :])
    match = within % capacity == slot
    copies = []
    for cut in range(BACK_CUTS):
        pick = (match & (within // capacity == cut)).astype(F32).astype(BF16)
        half = span // 2
        for at in (0, half):
            part = pl.ds(cut * span + at, half)
            input_buf[:, part] = tn(pick, every[:, at : at + half]).astype(BF16)
            copies.append(
                pltpu.make_async_copy(
                    input_buf.at[:, part], input_hbm.at[:, part], sems.at[len(copies)]
                )
            )
            copies[-1].start()
        if cut == 0:
            gates = tn(every[:, span:], pick)
    for k in range(2):
        route = routes[k : k + 1, :]
        value = jnp.where(route == 0, gates[0:1, :], jnp.where(route == 1, gates[1:2, :], 0.0))
        gate_out[k : k + 1, :] = value * (16.0 / levels[k : k + 1, :].astype(F32))
    for copy in copies:
        copy.wait()


def swap(array, axis, size, mask):
    return lax.ppermute(array, axis, [(n, n ^ mask) for n in range(size)])


def far_first(group):
    return [*range(group // 2, group), *range(1, group // 2)]


def plain_weights(inputs, grads, rights):
    inputs = lax.all_to_all(inputs, "dp", split_axis=1, concat_axis=0, tiled=True)
    grads = lax.all_to_all(grads, "dp", split_axis=1, concat_axis=0, tiled=True)
    rights = [lax.all_gather(right, "dp", axis=0, tiled=True) for right in rights]
    return jnp.stack([tn(inputs, rights[0]), tn(inputs, rights[1]), tn(grads, rights[2])])


def per_device(grad_out, routes, gate_levels, saved_inputs, w_gate, w_up, w_down):
    group = lax.axis_size("expert")
    n_dp = lax.axis_size("dp")
    shards = group // EXPERTS_W
    rows, width = saved_inputs.shape
    capacity = rows // group
    hidden = w_gate.shape[1]
    tokens = grad_out.shape[0]
    block = width // n_dp
    paired = n_dp == PAIRED
    routes = routes.T
    gate_levels = gate_levels.T
    shape = jax.ShapeDtypeStruct

    packed = shape((SEND_CUTS * capacity, width // SEND_CUTS), BF16)
    own, other, slots = call(
        functools.partial(pick_kernel, shards, capacity),
        (packed, packed, shape((8, tokens), jnp.int32)),
        (routes, gate_levels, grad_out),
        [HBM] * 3,
        [
            pltpu.VMEM(routes.shape, jnp.int32),
            pltpu.VMEM(routes.shape, jnp.int32),
            pltpu.VMEM(grad_out.shape, BF16),
            pltpu.SemaphoreType.DMA((2 + SEND_CUTS,)),
        ],
        name="pick",
    )
    received = [own] + [None] * (group - 1)
    for mask in far_first(group):
        received[mask] = swap(own if mask < shards else other, "expert", group, mask)
    part = shape((rows, hidden), F32)
    weight = shape((width, hidden), BF16)
    ahead = shape((rows, 2 * block + hidden), BF16)
    *ahead, u, v, h, near_inputs, near_gate, near_up = call(
        functools.partial(hidden_kernel, n_dp),
        (ahead,) * (LAST * paired) + (part,) * 3 + (shape((rows, width), BF16),) + (weight,) * 2,
        (saved_inputs, w_gate, w_up),
        [HBM] * 3,
        [pltpu.SemaphoreType.DMA((3, W_CHUNKS))],
        flops=HEAVY,
        name="hidden",
    )
    half = shape((rows, hidden), BF16)
    late = shape((rows, 2 * block + 2 * hidden), BF16)
    full = shape((rows, 4 * block + 3 * hidden), BF16)
    outward = (late,) * LAST + (full,) if paired else (shape((rows, width), BF16), half)
    *sends, da, db, gate = call(
        functools.partial(project_kernel, group, capacity, n_dp),
        outward + (half, half, shape((rows, GATE_LANES), BF16)),
        (*arrange(received), w_down, u, v, h, near_inputs),
        [VMEM] * (group + 5),
        [pltpu.VMEM((rows, width), BF16)],
        flops=HEAVY,
        name="project",
    )
    ahead = [swap(array, "dp", n_dp, 2 * m) if m > 0 else array for m, array in enumerate(ahead)]
    back = shape((BACK_CUTS * capacity, width // BACK_CUTS + GATE_LANES), BF16)
    returns = call(
        functools.partial(input_kernel, group, capacity),
        (back,) * group,
        (da, db, gate, near_gate, near_up, *ahead[1:]),
        [VMEM] * 5 + [UNUSED] * len(ahead[1:]),
        flops=HEAVY,
        name="input",
    )
    backs = [returns[0]] + [None] * (group - 1)
    for mask in far_first(group):
        backs[mask] = swap(returns[mask], "expert", group, mask)
    if paired:
        buffers = ahead + [sends[0]]
        buffers += [swap(sends[m], "dp", n_dp, 2 * m) for m in range(1, LAST + 1)]
        sharing = call(
            functools.partial(share_kernel, block, hidden),
            shape(((LAST + 1) * rows, 2 * block + 3 * hidden), BF16),
            buffers,
            [VMEM] * len(buffers),
            name="share",
        )
        shared = swap(sharing, "dp", n_dp, 1)
        block_shape = shape((3, block, hidden), F32)
        partial = call(
            functools.partial(weight_kernel, block, hidden),
            block_shape,
            buffers,
            [VMEM] * len(buffers),
            flops=HEAVY,
            name="weight",
        )
        weight_grad = call(
            functools.partial(finish_kernel, block, hidden),
            block_shape,
            (partial, shared),
            [VMEM] * 2,
            [pltpu.VMEM(block_shape.shape, F32), pltpu.SemaphoreType.DMA((3,))],
            near=False,
            out_specs=HBM,
            name="finish",
        )
    else:
        weight_grad = plain_weights(saved_inputs, sends[0], (da, db, sends[1]))
    after = [weight_grad] if paired else []
    input_grad, gate_grad = call(
        functools.partial(combine_kernel, group, capacity),
        (shape((tokens, width), BF16), shape((2, tokens), F32)),
        (*backs, routes, gate_levels, slots, *after),
        [VMEM] * (group + 3) + [HBM] * len(after),
        [pltpu.VMEM((tokens, width), BF16), pltpu.SemaphoreType.DMA((2 * BACK_CUTS,))],
        near=False,
        out_specs=(HBM, VMEM),
        flops=HEAVY,
        name="combine",
    )
    return input_grad, gate_grad.T, weight_grad.transpose(1, 0, 2)


def solution(mesh):
    in_specs = (
        P(("dp", "expert"), None),
        P(("dp", "expert"), None),
        P(("dp", "expert"), None),
        P(("dp", "expert"), None),
        P(None, "expert"),
        P(None, "expert"),
        P("expert", None),
    )
    out_specs = (P(("dp", "expert"), None), P(("dp", "expert"), None), P("dp", None, "expert"))
    return jax.shard_map(
        per_device, mesh=mesh, in_specs=in_specs, out_specs=out_specs, check_vma=False
    )
```

```python
import functools

import jax
import jax.numpy as jnp
from jax import lax
from jax.experimental import pallas as pl
from jax.experimental.pallas import tpu as pltpu
from jax.sharding import PartitionSpec as P

EXPERTS_W = 2
SEND_CUTS = 4
BACK_CUTS = 2
GATE_LANES = 128
W_CHUNKS = 4
LAST = 3
HEAVY = 10**11
DISPATCH_ORDER = (0, 3, 2, 1)
RETURN_ORDER = (0, 3, 1, 2)
PAIRED = 8
F32 = jnp.float32
BF16 = jnp.bfloat16
VMEM = pl.BlockSpec(memory_space=pltpu.VMEM)
HBM = pl.BlockSpec(memory_space=pltpu.HBM)
UNUSED = pl.BlockSpec(memory_space=pl.ANY)


def nn(left, right):
    return lax.dot_general(left, right, (((1,), (0,)), ((), ())), preferred_element_type=F32)


def nt(left, right):
    return lax.dot_general(left, right, (((1,), (1,)), ((), ())), preferred_element_type=F32)


def tn(left, right):
    return lax.dot_general(left, right, (((0,), (0,)), ((), ())), preferred_element_type=F32)


def iota(shape, dim):
    return lax.broadcasted_iota(jnp.int32, shape, dim)


def call(kernel, outs, args, specs, scratch=(), near=True, out_specs=None, flops=0, name=None):
    args = [
        pltpu.with_memory_space_constraint(arg, pltpu.HBM) if spec is HBM else arg
        for arg, spec in zip(args, specs)
    ]
    if near:
        outs = jax.tree.map(lambda out: pltpu.VMEM(out.shape, out.dtype), outs)
    return pl.pallas_call(
        kernel,
        out_shape=outs,
        in_specs=specs,
        out_specs=out_specs or jax.tree.map(lambda _: VMEM, outs),
        scratch_shapes=scratch,
        compiler_params=pltpu.CompilerParams(vmem_limit_bytes=24 * 1024 * 1024),
        cost_estimate=pl.CostEstimate(flops=flops, bytes_accessed=0, transcendentals=0),
        name=name,
    )(*args)


def arrange(arrays, order):
    return [arrays[mask] for mask in order] if len(arrays) == len(order) else arrays


def restore(refs, order):
    if len(refs) != len(order):
        return refs
    return [refs[order.index(mask)] for mask in range(len(refs))]


def pick_kernel(
    shards, capacity, routes_hbm, levels_hbm, grad_hbm, own_out, other_out, slots_out,
    routes, levels, grad, sems,
):
    tokens, width = grad.shape
    span = width // SEND_CUTS
    rows = SEND_CUTS * capacity
    small = [
        pltpu.make_async_copy(routes_hbm, routes, sems.at[0]),
        pltpu.make_async_copy(levels_hbm, levels, sems.at[1]),
    ]
    large = [
        pltpu.make_async_copy(
            grad_hbm.at[:, pl.ds(cut * span, span)],
            grad.at[:, pl.ds(cut * span, span)],
            sems.at[2 + cut],
        )
        for cut in range(SEND_CUTS)
    ]
    for copy in small + large:
        copy.start()
    mine = lax.axis_index("expert") // shards
    upto = (iota((tokens, tokens), 0) <= iota((tokens, tokens), 1)).astype(BF16)
    for copy in small:
        copy.wait()
    first, second = routes[0:1, :], routes[1:2, :]
    found = jnp.zeros((8, tokens), F32)
    for expert in range(EXPERTS_W):
        hit = ((first == expert) | (second == expert)).astype(F32)
        found = jnp.where(iota((8, tokens), 0) == expert, hit, found)
    counted = nn(found.astype(BF16), upto)
    slots = jnp.where(found > 0, counted - 1.0, -4096.0).astype(jnp.int32)
    slots_out[...] = slots
    slot_of, gate_of = [], []
    for expert in (mine, 1 - mine):
        level = jnp.where(first == expert, levels[0:1, :], levels[1:2, :])
        slot_of.append(jnp.where(expert == 0, slots[0:1, :], slots[1:2, :]))
        gate_of.append(level.astype(F32) * (1.0 / 16.0))
    row = iota((2 * rows, tokens), 0)
    slot = jnp.where(row < rows, slot_of[0], slot_of[1])
    gate = jnp.where(row < rows, gate_of[0], gate_of[1])
    place = row % rows
    total = jnp.zeros((2 * rows, span), F32)
    for cut in range(SEND_CUTS):
        lead = jnp.where(slot == place - cut * capacity, gate, 0.0).astype(BF16)
        large[cut].wait()
        total += nn(lead, grad[:, cut * span : (cut + 1) * span])
    own_out[...] = total[:rows].astype(BF16)
    other_out[...] = total[rows:].astype(BF16)


def hidden_kernel(n_dp, inputs_hbm, w_gate, w_up, *refs):
    ahead, (u_out, v_out, h_out, inputs, gate_buf, up_buf, sems) = refs[:-7], refs[-7:]
    first = pltpu.make_async_copy(inputs_hbm, inputs, sems.at[2, 0])
    first.start()
    width = inputs.shape[1]
    step = width // W_CHUNKS
    copies = []
    for k in range(W_CHUNKS):
        part = pl.ds(k * step, step)
        for n, (src, dst) in enumerate(((w_gate, gate_buf), (w_up, up_buf))):
            copy = pltpu.make_async_copy(src.at[part], dst.at[part], sems.at[n, k])
            copy.start()
            copies.append(copy)
    first.wait()
    a = jnp.zeros(u_out.shape, F32)
    b = jnp.zeros(u_out.shape, F32)
    for k in range(W_CHUNKS):
        left = inputs[:, k * step : (k + 1) * step]
        copies[2 * k].wait()
        a += nn(left, gate_buf[k * step : (k + 1) * step, :])
        copies[2 * k + 1].wait()
        b += nn(left, up_buf[k * step : (k + 1) * step, :])
    s = jax.nn.sigmoid(a)
    u = a * s
    u_out[...] = u
    v_out[...] = b * s * (1.0 + a * (1.0 - s))
    h = u * b
    h_out[...] = h
    pair = 2 * (width // n_dp)
    for out in ahead:
        start = pl.multiple_of(((lax.axis_index("dp") // 2) ^ LAST) * pair, 128)
        out[:, 0:pair] = inputs[:, pl.ds(start, pair)]
        out[:, pair:] = h.astype(BF16)


def project_kernel(group, capacity, n_dp, *refs):
    received = restore(refs[:group], DISPATCH_ORDER)
    w_down, u_in, v_in, h_in, inputs = refs[group : group + 5]
    sends = refs[group + 5 : -4]
    da_out, db_out, gate_out, rows_buf = refs[-4:]
    rows, hidden = u_in.shape
    width = w_down.shape[1]
    span = width // SEND_CUTS
    me = lax.axis_index("expert")
    packed = SEND_CUTS * capacity
    every = jnp.concatenate([ref[...] for ref in received], axis=0)
    to = iota((rows, group * packed), 0)
    at = iota((rows, group * packed), 1)
    source = (at // packed) ^ me
    within = at % packed
    match = (to // capacity == source) & (to % capacity == within % capacity)
    projected = jnp.zeros((rows, hidden), F32)
    for cut in range(SEND_CUTS):
        select = (match & (within // capacity == cut)).astype(F32).astype(BF16)
        piece = nn(select, every).astype(BF16)
        rows_buf[:, cut * span : (cut + 1) * span] = piece
        projected += nt(piece, w_down[:, cut * span : (cut + 1) * span])
    da = (projected * v_in[...]).astype(BF16)
    db = (projected * u_in[...]).astype(BF16)
    h = h_in[...]
    da_out[...] = da
    db_out[...] = db
    gate = jnp.sum(h * projected, axis=1, keepdims=True)
    lane = iota((rows, GATE_LANES), 1)
    gate_out[...] = jnp.where(lane == me // (group // EXPERTS_W), gate, 0.0).astype(BF16)
    h = h.astype(BF16)
    if n_dp != PAIRED:
        sends[0][...] = rows_buf[...]
        sends[1][...] = h
        return
    pair = 2 * (width // n_dp)
    chip = lax.axis_index("dp") // 2
    for m, send in enumerate(sends):
        start = pl.multiple_of((chip ^ m) * pair, 128)
        base = 0
        if m < LAST:
            send[:, 0:pair] = inputs[:, pl.ds(start, pair)]
            send[:, pair : pair + hidden] = h
            base = pair + hidden
        send[:, base : base + pair] = rows_buf[:, pl.ds(start, pair)]
        send[:, base + pair : base + pair + hidden] = da
        send[:, base + pair + hidden :] = db


def input_kernel(group, capacity, da, db, gate, w_gate, w_up, *refs):
    outs = refs[-group:]
    rows = da.shape[0]
    width = w_gate.shape[0]
    span = width // BACK_CUTS
    step = width // W_CHUNKS
    per = W_CHUNKS // BACK_CUTS
    me = lax.axis_index("expert")
    packed = BACK_CUTS * capacity
    to = iota((group * packed, rows), 0)
    at = iota((group * packed, rows), 1)
    target = (to // packed) ^ me
    within = to % packed
    match = (at // capacity == target) & (at % capacity == within % capacity)
    selects = [
        (match & (within // capacity == cut)).astype(F32).astype(BF16) for cut in range(BACK_CUTS)
    ]
    total = [jnp.zeros((group * packed, step), F32) for _ in range(per)]
    for k in range(W_CHUNKS):
        part = nt(da[...], w_gate[k * step : (k + 1) * step, :])
        part += nt(db[...], w_up[k * step : (k + 1) * step, :])
        total[k % per] += nn(selects[k // per], part.astype(BF16))
    gates = nn(selects[0], gate[...])
    for n, out in enumerate(outs):
        for q in range(per):
            out[:, q * step : (q + 1) * step] = total[q][n * packed : (n + 1) * packed].astype(BF16)
        out[:, span:] = gates[n * packed : (n + 1) * packed].astype(BF16)


def halves(columns, refs):
    first = [(ref, 0) for ref in refs[: LAST + 1]]
    second = [(ref, columns) for ref in refs[:LAST]] + [(refs[-1], 0)]
    return first, second


def share_kernel(block, hidden, *refs):
    buffers, out = refs[:-1], refs[-1]
    rows = buffers[0].shape[0]
    start = (1 - lax.axis_index("dp") % 2) * block
    first, second = halves(2 * block + hidden, buffers)
    middle = block + hidden
    for m in range(LAST + 1):
        part = slice(m * rows, (m + 1) * rows)
        for (ref, at), to, wide in ((first[m], 0, middle), (second[m], middle, middle + hidden)):
            out[part, to : to + block] = ref[:, pl.ds(pl.multiple_of(at + start, 128), block)]
            at += 2 * block
            out[part, to + block : to + wide] = ref[:, at : at + wide - block]


def weight_kernel(block, hidden, *refs):
    buffers, out = refs[:-1], refs[-1]
    start = (lax.axis_index("dp") % 2) * block
    first, second = halves(2 * block + hidden, buffers)

    def gather(side, skip, wide):
        parts = [ref[:, pl.ds(pl.multiple_of(at + skip, 128), wide)] for ref, at in side]
        return jnp.concatenate(parts, axis=0)

    inputs, grads = gather(first, start, block), gather(second, start, block)
    out[0] = tn(inputs, gather(second, 2 * block, hidden))
    out[1] = tn(inputs, gather(second, 2 * block + hidden, hidden))
    out[2] = tn(grads, gather(first, 2 * block, hidden))


def finish_weights(hidden, partial, shared, out_hbm, buf, sems):
    block = buf.shape[1]
    middle = block + hidden
    inputs, h = shared[:, 0:block], shared[:, block:middle]
    grads, da = shared[:, middle : middle + block], shared[:, middle + block : 2 * middle]
    copies = []
    for n, (left, right) in enumerate(((inputs, da), (inputs, shared[:, 2 * middle :]), (grads, h))):
        buf[n] = partial[n] + tn(left, right)
        copies.append(pltpu.make_async_copy(buf.at[n], out_hbm.at[n], sems.at[n]))
        copies[-1].start()
    return copies


def finish_kernel(group, capacity, hidden, *refs):
    backs = restore(refs[:group], RETURN_ORDER)
    routes, levels, slots = refs[group : group + 3]
    copies = []
    if hidden > 0:
        partial, shared = refs[group + 3 : group + 5]
        input_hbm, gate_out, weight_hbm, weight_buf, weight_sems, input_buf, sems = refs[-7:]
        copies += finish_weights(hidden, partial, shared, weight_hbm, weight_buf, weight_sems)
    else:
        input_hbm, gate_out, input_buf, sems = refs[-4:]
    tokens, width = input_buf.shape
    span = width // BACK_CUTS
    packed = BACK_CUTS * capacity
    shards = group // EXPERTS_W
    me = lax.axis_index("expert")
    every = jnp.concatenate([ref[...] for ref in backs], axis=0)
    row = iota((group * packed, tokens), 0)
    expert = ((row // packed) ^ me) // shards
    within = row % packed
    slot = jnp.where(expert == 0, slots[0:1, :], slots[1:2, :])
    match = within % capacity == slot
    for cut in range(BACK_CUTS):
        pick = (match & (within // capacity == cut)).astype(F32).astype(BF16)
        half = span // 2
        for n in range(2):
            part = pl.ds(cut * span + n * half, half)
            input_buf[:, part] = tn(pick, every[:, n * half : (n + 1) * half]).astype(BF16)
            copy = pltpu.make_async_copy(
                input_buf.at[:, part], input_hbm.at[:, part], sems.at[2 * cut + n]
            )
            copy.start()
            copies.append(copy)
        if cut == 0:
            gates = tn(every[:, span:], pick)
    for k in range(2):
        route = routes[k : k + 1, :]
        value = jnp.where(route == 0, gates[0:1, :], jnp.where(route == 1, gates[1:2, :], 0.0))
        gate_out[k : k + 1, :] = value * (16.0 / levels[k : k + 1, :].astype(F32))
    for copy in copies:
        copy.wait()


def swap(array, axis, size, mask):
    return lax.ppermute(array, axis, [(n, n ^ mask) for n in range(size)])


def far_first(group):
    return [*range(group // 2, group), *range(1, group // 2)]


def plain_weights(inputs, grads, rights):
    inputs = lax.all_to_all(inputs, "dp", split_axis=1, concat_axis=0, tiled=True)
    grads = lax.all_to_all(grads, "dp", split_axis=1, concat_axis=0, tiled=True)
    rights = [lax.all_gather(right, "dp", axis=0, tiled=True) for right in rights]
    return jnp.stack([tn(inputs, rights[0]), tn(inputs, rights[1]), tn(grads, rights[2])])


def per_device(grad_out, routes, gate_levels, saved_inputs, w_gate, w_up, w_down):
    group = lax.axis_size("expert")
    n_dp = lax.axis_size("dp")
    shards = group // EXPERTS_W
    rows, width = saved_inputs.shape
    capacity = rows // group
    hidden = w_gate.shape[1]
    tokens = grad_out.shape[0]
    block = width // n_dp
    paired = n_dp == PAIRED
    routes = routes.T
    gate_levels = gate_levels.T
    shape = jax.ShapeDtypeStruct

    packed = shape((SEND_CUTS * capacity, width // SEND_CUTS), BF16)
    own, other, slots = call(
        functools.partial(pick_kernel, shards, capacity),
        (packed, packed, shape((8, tokens), jnp.int32)),
        (routes, gate_levels, grad_out),
        [HBM] * 3,
        [
            pltpu.VMEM(routes.shape, jnp.int32),
            pltpu.VMEM(routes.shape, jnp.int32),
            pltpu.VMEM(grad_out.shape, BF16),
            pltpu.SemaphoreType.DMA((2 + SEND_CUTS,)),
        ],
        name="pick",
    )
    received = [own] + [None] * (group - 1)
    for mask in far_first(group):
        received[mask] = swap(own if mask < shards else other, "expert", group, mask)
    part = shape((rows, hidden), F32)
    weight = shape((width, hidden), BF16)
    ahead = shape((rows, 2 * block + hidden), BF16)
    *ahead, u, v, h, near_inputs, near_gate, near_up = call(
        functools.partial(hidden_kernel, n_dp),
        (ahead,) * paired + (part,) * 3 + (shape((rows, width), BF16),) + (weight,) * 2,
        (saved_inputs, w_gate, w_up),
        [HBM] * 3,
        [pltpu.SemaphoreType.DMA((3, W_CHUNKS))],
        flops=HEAVY,
        name="hidden",
    )
    half = shape((rows, hidden), BF16)
    late = shape((rows, 2 * block + 2 * hidden), BF16)
    full = shape((rows, 4 * block + 3 * hidden), BF16)
    outward = (full,) * LAST + (late,) if paired else (shape((rows, width), BF16), half)
    *sends, da, db, gate = call(
        functools.partial(project_kernel, group, capacity, n_dp),
        outward + (half, half, shape((rows, GATE_LANES), BF16)),
        (*arrange(received, DISPATCH_ORDER), w_down, u, v, h, near_inputs),
        [VMEM] * (group + 5),
        [pltpu.VMEM((rows, width), BF16)],
        flops=HEAVY,
        name="project",
    )
    ahead = [swap(array, "dp", n_dp, 2 * LAST) for array in ahead]
    back = shape((BACK_CUTS * capacity, width // BACK_CUTS + GATE_LANES), BF16)
    returns = call(
        functools.partial(input_kernel, group, capacity),
        (back,) * group,
        (da, db, gate, near_gate, near_up, *ahead),
        [VMEM] * 5 + [UNUSED] * len(ahead),
        flops=HEAVY,
        name="input",
    )
    backs = [returns[0]] + [None] * (group - 1)
    for mask in far_first(group):
        backs[mask] = swap(returns[mask], "expert", group, mask)
    if paired:
        got = [sends[0]] + [swap(sends[m], "dp", n_dp, 2 * m) for m in range(1, LAST + 1)]
        buffers = got[:LAST] + ahead + got[LAST:]
        sharing = call(
            functools.partial(share_kernel, block, hidden),
            shape(((LAST + 1) * rows, 2 * block + 3 * hidden), BF16),
            buffers,
            [VMEM] * len(buffers),
            name="share",
        )
        shared = swap(sharing, "dp", n_dp, 1)
        block_shape = shape((3, block, hidden), F32)
        partial = call(
            functools.partial(weight_kernel, block, hidden),
            block_shape,
            buffers,
            [VMEM] * len(buffers),
            flops=HEAVY,
            name="weight",
        )
        extra = (partial, shared)
    else:
        extra = ()
    finished = (shape((tokens, width), BF16), shape((2, tokens), F32))
    scratch = [pltpu.VMEM((tokens, width), BF16), pltpu.SemaphoreType.DMA((2 * BACK_CUTS,))]
    if paired:
        finished += (block_shape,)
        scratch = [pltpu.VMEM(block_shape.shape, F32), pltpu.SemaphoreType.DMA((3,))] + scratch
    input_grad, gate_grad, *weight_grad = call(
        functools.partial(finish_kernel, group, capacity, hidden if paired else 0),
        finished,
        (*arrange(backs, RETURN_ORDER), routes, gate_levels, slots, *extra),
        [VMEM] * (group + 3 + len(extra)),
        scratch,
        near=False,
        out_specs=(HBM, VMEM, HBM)[: len(finished)],
        flops=HEAVY,
        name="finish",
    )
    if paired:
        (weight_grad,) = weight_grad
    else:
        weight_grad = plain_weights(saved_inputs, sends[0], (da, db, sends[1]))
    return input_grad, gate_grad.T, weight_grad.transpose(1, 0, 2)


def solution(mesh):
    in_specs = (
        P(("dp", "expert"), None),
        P(("dp", "expert"), None),
        P(("dp", "expert"), None),
        P(("dp", "expert"), None),
        P(None, "expert"),
        P(None, "expert"),
        P("expert", None),
    )
    out_specs = (P(("dp", "expert"), None), P(("dp", "expert"), None), P("dp", None, "expert"))
    return jax.shard_map(
        per_device, mesh=mesh, in_specs=in_specs, out_specs=out_specs, check_vma=False
    )
```

```python
import functools

import jax
import jax.numpy as jnp
from jax import lax
from jax.experimental import pallas as pl
from jax.experimental.pallas import tpu as pltpu
from jax.sharding import PartitionSpec as P

EXPERTS_W = 2
SEND_CUTS = 4
BACK_CUTS = 2
GATE_LANES = 128
W_CHUNKS = 4
LAST = 3
HEAVY = 10**11
DISPATCH_ORDER = (0, 3, 2, 1)
RETURN_ORDER = (0, 3, 1, 2)
PAIRED = 8
F32 = jnp.float32
BF16 = jnp.bfloat16
VMEM = pl.BlockSpec(memory_space=pltpu.VMEM)
HBM = pl.BlockSpec(memory_space=pltpu.HBM)
UNUSED = pl.BlockSpec(memory_space=pl.ANY)


def nn(left, right):
    return lax.dot_general(left, right, (((1,), (0,)), ((), ())), preferred_element_type=F32)


def nt(left, right):
    return lax.dot_general(left, right, (((1,), (1,)), ((), ())), preferred_element_type=F32)


def tn(left, right):
    return lax.dot_general(left, right, (((0,), (0,)), ((), ())), preferred_element_type=F32)


def iota(shape, dim):
    return lax.broadcasted_iota(jnp.int32, shape, dim)


def call(kernel, outs, args, specs, scratch=(), near=True, out_specs=None, flops=0, name=None):
    args = [
        pltpu.with_memory_space_constraint(arg, pltpu.HBM) if spec is HBM else arg
        for arg, spec in zip(args, specs)
    ]
    if near:
        outs = jax.tree.map(lambda out: pltpu.VMEM(out.shape, out.dtype), outs)
    return pl.pallas_call(
        kernel,
        out_shape=outs,
        in_specs=specs,
        out_specs=out_specs or jax.tree.map(lambda _: VMEM, outs),
        scratch_shapes=scratch,
        compiler_params=pltpu.CompilerParams(vmem_limit_bytes=24 * 1024 * 1024),
        cost_estimate=pl.CostEstimate(flops=flops, bytes_accessed=0, transcendentals=0),
        name=name,
    )(*args)


def arrange(arrays, order):
    return [arrays[mask] for mask in order] if len(arrays) == len(order) else arrays


def restore(refs, order):
    if len(refs) != len(order):
        return refs
    return [refs[order.index(mask)] for mask in range(len(refs))]


def pick_kernel(
    shards, capacity, routes_hbm, levels_hbm, grad_hbm, own_out, other_out, slots_out,
    routes, levels, grad, sems,
):
    tokens, width = grad.shape
    span = width // SEND_CUTS
    rows = SEND_CUTS * capacity
    small = [
        pltpu.make_async_copy(routes_hbm, routes, sems.at[0]),
        pltpu.make_async_copy(levels_hbm, levels, sems.at[1]),
    ]
    large = [
        pltpu.make_async_copy(
            grad_hbm.at[:, pl.ds(cut * span, span)],
            grad.at[:, pl.ds(cut * span, span)],
            sems.at[2 + cut],
        )
        for cut in range(SEND_CUTS)
    ]
    for copy in small + large:
        copy.start()
    mine = lax.axis_index("expert") // shards
    upto = (iota((tokens, tokens), 0) <= iota((tokens, tokens), 1)).astype(BF16)
    for copy in small:
        copy.wait()
    first, second = routes[0:1, :], routes[1:2, :]
    found = jnp.zeros((8, tokens), F32)
    for expert in range(EXPERTS_W):
        hit = ((first == expert) | (second == expert)).astype(F32)
        found = jnp.where(iota((8, tokens), 0) == expert, hit, found)
    counted = nn(found.astype(BF16), upto)
    slots = jnp.where(found > 0, counted - 1.0, -4096.0).astype(jnp.int32)
    slots_out[...] = slots
    slot_of, gate_of = [], []
    for expert in (mine, 1 - mine):
        level = jnp.where(first == expert, levels[0:1, :], levels[1:2, :])
        slot_of.append(jnp.where(expert == 0, slots[0:1, :], slots[1:2, :]))
        gate_of.append(level.astype(F32) * (1.0 / 16.0))
    row = iota((2 * rows, tokens), 0)
    slot = jnp.where(row < rows, slot_of[0], slot_of[1])
    gate = jnp.where(row < rows, gate_of[0], gate_of[1])
    place = row % rows
    total = jnp.zeros((2 * rows, span), F32)
    for cut in range(SEND_CUTS):
        lead = jnp.where(slot == place - cut * capacity, gate, 0.0).astype(BF16)
        large[cut].wait()
        total += nn(lead, grad[:, cut * span : (cut + 1) * span])
    own_out[...] = total[:rows].astype(BF16)
    other_out[...] = total[rows:].astype(BF16)


def hidden_kernel(n_dp, inputs_hbm, w_gate, w_up, *refs):
    ahead, (u_out, v_out, h_out, inputs, gate_buf, up_buf, sems) = refs[:-7], refs[-7:]
    first = pltpu.make_async_copy(inputs_hbm, inputs, sems.at[2, 0])
    first.start()
    width = inputs.shape[1]
    step = width // W_CHUNKS
    copies = []
    for k in range(W_CHUNKS):
        part = pl.ds(k * step, step)
        for n, (src, dst) in enumerate(((w_gate, gate_buf), (w_up, up_buf))):
            copy = pltpu.make_async_copy(src.at[part], dst.at[part], sems.at[n, k])
            copy.start()
            copies.append(copy)
    first.wait()
    a = jnp.zeros(u_out.shape, F32)
    b = jnp.zeros(u_out.shape, F32)
    for k in range(W_CHUNKS):
        left = inputs[:, k * step : (k + 1) * step]
        copies[2 * k].wait()
        a += nn(left, gate_buf[k * step : (k + 1) * step, :])
        copies[2 * k + 1].wait()
        b += nn(left, up_buf[k * step : (k + 1) * step, :])
    s = jax.nn.sigmoid(a)
    u = a * s
    u_out[...] = u
    v_out[...] = b * s * (1.0 + a * (1.0 - s))
    h = u * b
    h_out[...] = h
    pair = 2 * (width // n_dp)
    for out in ahead:
        start = pl.multiple_of(((lax.axis_index("dp") // 2) ^ LAST) * pair, 128)
        out[:, 0:pair] = inputs[:, pl.ds(start, pair)]
        out[:, pair:] = h.astype(BF16)


def project_kernel(group, capacity, n_dp, *refs):
    received = restore(refs[:group], DISPATCH_ORDER)
    w_down, u_in, v_in, h_in, inputs = refs[group : group + 5]
    sends = refs[group + 5 : -4]
    da_out, db_out, gate_out, rows_buf = refs[-4:]
    rows, hidden = u_in.shape
    width = w_down.shape[1]
    span = width // SEND_CUTS
    me = lax.axis_index("expert")
    packed = SEND_CUTS * capacity
    every = jnp.concatenate([ref[...] for ref in received], axis=0)
    to = iota((rows, group * packed), 0)
    at = iota((rows, group * packed), 1)
    source = (at // packed) ^ me
    within = at % packed
    match = (to // capacity == source) & (to % capacity == within % capacity)
    projected = jnp.zeros((rows, hidden), F32)
    for cut in range(SEND_CUTS):
        select = (match & (within // capacity == cut)).astype(F32).astype(BF16)
        piece = nn(select, every).astype(BF16)
        rows_buf[:, cut * span : (cut + 1) * span] = piece
        projected += nt(piece, w_down[:, cut * span : (cut + 1) * span])
    da = (projected * v_in[...]).astype(BF16)
    db = (projected * u_in[...]).astype(BF16)
    h = h_in[...]
    da_out[...] = da
    db_out[...] = db
    gate = jnp.sum(h * projected, axis=1, keepdims=True)
    lane = iota((rows, GATE_LANES), 1)
    gate_out[...] = jnp.where(lane == me // (group // EXPERTS_W), gate, 0.0).astype(BF16)
    h = h.astype(BF16)
    if n_dp != PAIRED:
        sends[0][...] = rows_buf[...]
        sends[1][...] = h
        return
    pair = 2 * (width // n_dp)
    chip = lax.axis_index("dp") // 2
    for m, send in enumerate(sends):
        start = pl.multiple_of((chip ^ m) * pair, 128)
        base = 0
        if m < LAST:
            send[:, 0:pair] = inputs[:, pl.ds(start, pair)]
            send[:, pair : pair + hidden] = h
            base = pair + hidden
        send[:, base : base + pair] = rows_buf[:, pl.ds(start, pair)]
        send[:, base + pair : base + pair + hidden] = da
        send[:, base + pair + hidden :] = db


def input_kernel(group, capacity, da, db, gate, w_gate, w_up, *refs):
    outs = refs[-group:]
    rows = da.shape[0]
    width = w_gate.shape[0]
    span = width // BACK_CUTS
    step = width // W_CHUNKS
    per = W_CHUNKS // BACK_CUTS
    me = lax.axis_index("expert")
    packed = BACK_CUTS * capacity
    to = iota((group * packed, rows), 0)
    at = iota((group * packed, rows), 1)
    target = (to // packed) ^ me
    within = to % packed
    match = (at // capacity == target) & (at % capacity == within % capacity)
    selects = [
        (match & (within // capacity == cut)).astype(F32).astype(BF16) for cut in range(BACK_CUTS)
    ]
    total = [jnp.zeros((group * packed, step), F32) for _ in range(per)]
    for k in range(W_CHUNKS):
        part = nt(da[...], w_gate[k * step : (k + 1) * step, :])
        part += nt(db[...], w_up[k * step : (k + 1) * step, :])
        total[k % per] += nn(selects[k // per], part.astype(BF16))
    gates = nn(selects[0], gate[...])
    for n, out in enumerate(outs):
        for q in range(per):
            out[:, q * step : (q + 1) * step] = total[q][n * packed : (n + 1) * packed].astype(BF16)
        out[:, span:] = gates[n * packed : (n + 1) * packed].astype(BF16)


def halves(columns, refs):
    first = [(ref, 0) for ref in refs[: LAST + 1]]
    second = [(ref, columns) for ref in refs[:LAST]] + [(refs[-1], 0)]
    return first, second


def share_kernel(block, hidden, *refs):
    buffers, out = refs[:-1], refs[-1]
    rows = buffers[0].shape[0]
    start = (1 - lax.axis_index("dp") % 2) * block
    first, second = halves(2 * block + hidden, buffers)
    middle = block + hidden
    for m in range(LAST + 1):
        part = slice(m * rows, (m + 1) * rows)
        for (ref, at), to, wide in ((first[m], 0, middle), (second[m], middle, middle + hidden)):
            out[part, to : to + block] = ref[:, pl.ds(pl.multiple_of(at + start, 128), block)]
            at += 2 * block
            out[part, to + block : to + wide] = ref[:, at : at + wide - block]


def weight_kernel(block, hidden, *refs):
    buffers, out = refs[:-1], refs[-1]
    start = (lax.axis_index("dp") % 2) * block
    first, second = halves(2 * block + hidden, buffers)

    def gather(side, skip, wide):
        parts = [ref[:, pl.ds(pl.multiple_of(at + skip, 128), wide)] for ref, at in side]
        return jnp.concatenate(parts, axis=0)

    inputs, grads = gather(first, start, block), gather(second, start, block)
    out[0] = tn(inputs, gather(second, 2 * block, hidden))
    out[1] = tn(inputs, gather(second, 2 * block + hidden, hidden))
    out[2] = tn(grads, gather(first, 2 * block, hidden))


def finish_weights(hidden, partial, shared, out_hbm, buf, sems):
    block = buf.shape[1]
    middle = block + hidden
    inputs, h = shared[:, 0:block], shared[:, block:middle]
    grads, da = shared[:, middle : middle + block], shared[:, middle + block : 2 * middle]
    copies = []
    for n, (left, right) in enumerate(((inputs, da), (inputs, shared[:, 2 * middle :]), (grads, h))):
        buf[n] = partial[n] + tn(left, right)
        copies.append(pltpu.make_async_copy(buf.at[n], out_hbm.at[n], sems.at[n]))
        copies[-1].start()
    return copies


def finish_kernel(group, capacity, hidden, *refs):
    backs = restore(refs[:group], RETURN_ORDER)
    routes, levels, slots = refs[group : group + 3]
    copies = []
    if hidden > 0:
        partial, shared = refs[group + 3 : group + 5]
        input_hbm, gate_hbm, weight_hbm, weight_buf, weight_sems = refs[-8:-3]
        copies += finish_weights(hidden, partial, shared, weight_hbm, weight_buf, weight_sems)
    else:
        input_hbm, gate_hbm = refs[-5:-3]
    input_buf, gate_buf, sems = refs[-3:]
    tokens, width = input_buf.shape
    span = width // BACK_CUTS
    packed = BACK_CUTS * capacity
    shards = group // EXPERTS_W
    me = lax.axis_index("expert")
    every = jnp.concatenate([ref[...] for ref in backs], axis=0)
    row = iota((group * packed, tokens), 0)
    expert = ((row // packed) ^ me) // shards
    within = row % packed
    slot = jnp.where(expert == 0, slots[0:1, :], slots[1:2, :])
    match = within % capacity == slot
    picks = [
        (match & (within // capacity == cut)).astype(F32).astype(BF16) for cut in range(BACK_CUTS)
    ]
    gates = tn(every[:, span:], picks[0])
    for k in range(2):
        route = routes[k : k + 1, :]
        value = jnp.where(route == 0, gates[0:1, :], jnp.where(route == 1, gates[1:2, :], 0.0))
        gate_buf[k : k + 1, :] = value * (16.0 / levels[k : k + 1, :].astype(F32))
    copies.append(pltpu.make_async_copy(gate_buf, gate_hbm, sems.at[2 * BACK_CUTS]))
    copies[-1].start()
    for cut, pick in enumerate(picks):
        half = span // 2
        for n in range(2):
            part = pl.ds(cut * span + n * half, half)
            input_buf[:, part] = tn(pick, every[:, n * half : (n + 1) * half]).astype(BF16)
            copy = pltpu.make_async_copy(
                input_buf.at[:, part], input_hbm.at[:, part], sems.at[2 * cut + n]
            )
            copy.start()
            copies.append(copy)
    for copy in copies:
        copy.wait()


def swap(array, axis, size, mask):
    return lax.ppermute(array, axis, [(n, n ^ mask) for n in range(size)])


def far_first(group):
    return [*range(group // 2, group), *range(1, group // 2)]


def plain_weights(inputs, grads, rights):
    inputs = lax.all_to_all(inputs, "dp", split_axis=1, concat_axis=0, tiled=True)
    grads = lax.all_to_all(grads, "dp", split_axis=1, concat_axis=0, tiled=True)
    rights = [lax.all_gather(right, "dp", axis=0, tiled=True) for right in rights]
    return jnp.stack([tn(inputs, rights[0]), tn(inputs, rights[1]), tn(grads, rights[2])])


def per_device(grad_out, routes, gate_levels, saved_inputs, w_gate, w_up, w_down):
    group = lax.axis_size("expert")
    n_dp = lax.axis_size("dp")
    shards = group // EXPERTS_W
    rows, width = saved_inputs.shape
    capacity = rows // group
    hidden = w_gate.shape[1]
    tokens = grad_out.shape[0]
    block = width // n_dp
    paired = n_dp == PAIRED
    routes = routes.T
    gate_levels = gate_levels.T
    shape = jax.ShapeDtypeStruct

    packed = shape((SEND_CUTS * capacity, width // SEND_CUTS), BF16)
    own, other, slots = call(
        functools.partial(pick_kernel, shards, capacity),
        (packed, packed, shape((8, tokens), jnp.int32)),
        (routes, gate_levels, grad_out),
        [HBM] * 3,
        [
            pltpu.VMEM(routes.shape, jnp.int32),
            pltpu.VMEM(routes.shape, jnp.int32),
            pltpu.VMEM(grad_out.shape, BF16),
            pltpu.SemaphoreType.DMA((2 + SEND_CUTS,)),
        ],
        name="pick",
    )
    received = [own] + [None] * (group - 1)
    for mask in far_first(group):
        received[mask] = swap(own if mask < shards else other, "expert", group, mask)
    part = shape((rows, hidden), F32)
    weight = shape((width, hidden), BF16)
    ahead = shape((rows, 2 * block + hidden), BF16)
    *ahead, u, v, h, near_inputs, near_gate, near_up = call(
        functools.partial(hidden_kernel, n_dp),
        (ahead,) * paired + (part,) * 3 + (shape((rows, width), BF16),) + (weight,) * 2,
        (saved_inputs, w_gate, w_up),
        [HBM] * 3,
        [pltpu.SemaphoreType.DMA((3, W_CHUNKS))],
        flops=HEAVY,
        name="hidden",
    )
    half = shape((rows, hidden), BF16)
    late = shape((rows, 2 * block + 2 * hidden), BF16)
    full = shape((rows, 4 * block + 3 * hidden), BF16)
    outward = (full,) * LAST + (late,) if paired else (shape((rows, width), BF16), half)
    *sends, da, db, gate = call(
        functools.partial(project_kernel, group, capacity, n_dp),
        outward + (half, half, shape((rows, GATE_LANES), BF16)),
        (*arrange(received, DISPATCH_ORDER), w_down, u, v, h, near_inputs),
        [VMEM] * (group + 5),
        [pltpu.VMEM((rows, width), BF16)],
        flops=HEAVY,
        name="project",
    )
    ahead = [swap(array, "dp", n_dp, 2 * LAST) for array in ahead]
    back = shape((BACK_CUTS * capacity, width // BACK_CUTS + GATE_LANES), BF16)
    returns = call(
        functools.partial(input_kernel, group, capacity),
        (back,) * group,
        (da, db, gate, near_gate, near_up, *ahead),
        [VMEM] * 5 + [UNUSED] * len(ahead),
        flops=HEAVY,
        name="input",
    )
    backs = [returns[0]] + [None] * (group - 1)
    for mask in far_first(group):
        backs[mask] = swap(returns[mask], "expert", group, mask)
    if paired:
        got = [sends[0]] + [swap(sends[m], "dp", n_dp, 2 * m) for m in range(1, LAST + 1)]
        buffers = got[:LAST] + ahead + got[LAST:]
        sharing = call(
            functools.partial(share_kernel, block, hidden),
            shape(((LAST + 1) * rows, 2 * block + 3 * hidden), BF16),
            buffers,
            [VMEM] * len(buffers),
            name="share",
        )
        shared = swap(sharing, "dp", n_dp, 1)
        block_shape = shape((3, block, hidden), F32)
        partial = call(
            functools.partial(weight_kernel, block, hidden),
            block_shape,
            buffers,
            [VMEM] * len(buffers),
            flops=HEAVY,
            name="weight",
        )
        extra = (partial, shared)
    else:
        extra = ()
    finished = (shape((tokens, width), BF16), shape((2, tokens), F32))
    scratch = [
        pltpu.VMEM((tokens, width), BF16),
        pltpu.VMEM((2, tokens), F32),
        pltpu.SemaphoreType.DMA((2 * BACK_CUTS + 1,)),
    ]
    if paired:
        finished += (block_shape,)
        scratch = [pltpu.VMEM(block_shape.shape, F32), pltpu.SemaphoreType.DMA((3,))] + scratch
    input_grad, gate_grad, *weight_grad = call(
        functools.partial(finish_kernel, group, capacity, hidden if paired else 0),
        finished,
        (*arrange(backs, RETURN_ORDER), routes, gate_levels, slots, *extra),
        [VMEM] * (group + 3 + len(extra)),
        scratch,
        near=False,
        out_specs=(HBM,) * len(finished),
        flops=HEAVY,
        name="finish",
    )
    if paired:
        (weight_grad,) = weight_grad
    else:
        weight_grad = plain_weights(saved_inputs, sends[0], (da, db, sends[1]))
    return input_grad, gate_grad.T, weight_grad.transpose(1, 0, 2)


def solution(mesh):
    in_specs = (
        P(("dp", "expert"), None),
        P(("dp", "expert"), None),
        P(("dp", "expert"), None),
        P(("dp", "expert"), None),
        P(None, "expert"),
        P(None, "expert"),
        P("expert", None),
    )
    out_specs = (P(("dp", "expert"), None), P(("dp", "expert"), None), P("dp", None, "expert"))
    return jax.shard_map(
        per_device, mesh=mesh, in_specs=in_specs, out_specs=out_specs, check_vma=False
    )
```

```python
import functools

import jax
import jax.numpy as jnp
from jax import lax
from jax.experimental import pallas as pl
from jax.experimental.pallas import tpu as pltpu
from jax.sharding import PartitionSpec as P

EXPERTS_W = 2
SEND_CUTS = 4
BACK_CUTS = 2
GATE_LANES = 128
W_CHUNKS = 4
LAST = 3
HEAVY = 10**11
DISPATCH_ORDER = (0, 3, 2, 1)
RETURN_ORDER = (0, 3, 1, 2)
PAIRED = 8
F32 = jnp.float32
BF16 = jnp.bfloat16
VMEM = pl.BlockSpec(memory_space=pltpu.VMEM)
HBM = pl.BlockSpec(memory_space=pltpu.HBM)
UNUSED = pl.BlockSpec(memory_space=pl.ANY)


def nn(left, right):
    return lax.dot_general(left, right, (((1,), (0,)), ((), ())), preferred_element_type=F32)


def nt(left, right):
    return lax.dot_general(left, right, (((1,), (1,)), ((), ())), preferred_element_type=F32)


def tn(left, right):
    return lax.dot_general(left, right, (((0,), (0,)), ((), ())), preferred_element_type=F32)


def iota(shape, dim):
    return lax.broadcasted_iota(jnp.int32, shape, dim)


def call(kernel, outs, args, specs, scratch=(), near=True, out_specs=None, aliases=None, flops=0, name=None):
    args = [
        pltpu.with_memory_space_constraint(arg, pltpu.HBM) if spec is HBM else arg
        for arg, spec in zip(args, specs)
    ]
    if near:
        outs = jax.tree.map(lambda out: pltpu.VMEM(out.shape, out.dtype), outs)
    return pl.pallas_call(
        kernel,
        out_shape=outs,
        in_specs=specs,
        out_specs=out_specs or jax.tree.map(lambda _: VMEM, outs),
        scratch_shapes=scratch,
        input_output_aliases=aliases or {},
        compiler_params=pltpu.CompilerParams(vmem_limit_bytes=24 * 1024 * 1024),
        cost_estimate=pl.CostEstimate(flops=flops, bytes_accessed=0, transcendentals=0),
        name=name,
    )(*args)


def arrange(arrays, order):
    return [arrays[mask] for mask in order] if len(arrays) == len(order) else arrays


def restore(refs, order):
    if len(refs) != len(order):
        return refs
    return [refs[order.index(mask)] for mask in range(len(refs))]


def pick_kernel(
    shards, capacity, routes_hbm, levels_hbm, grad_hbm, own_out, other_out, slots_out,
    routes, levels, grad, sems,
):
    tokens, width = grad.shape
    span = width // SEND_CUTS
    rows = SEND_CUTS * capacity
    small = [
        pltpu.make_async_copy(routes_hbm, routes, sems.at[0]),
        pltpu.make_async_copy(levels_hbm, levels, sems.at[1]),
    ]
    large = [
        pltpu.make_async_copy(
            grad_hbm.at[:, pl.ds(cut * span, span)],
            grad.at[:, pl.ds(cut * span, span)],
            sems.at[2 + cut],
        )
        for cut in range(SEND_CUTS)
    ]
    for copy in small + large:
        copy.start()
    mine = lax.axis_index("expert") // shards
    upto = (iota((tokens, tokens), 0) <= iota((tokens, tokens), 1)).astype(BF16)
    for copy in small:
        copy.wait()
    first, second = routes[0:1, :], routes[1:2, :]
    found = jnp.zeros((8, tokens), F32)
    for expert in range(EXPERTS_W):
        hit = ((first == expert) | (second == expert)).astype(F32)
        found = jnp.where(iota((8, tokens), 0) == expert, hit, found)
    counted = nn(found.astype(BF16), upto)
    slots = jnp.where(found > 0, counted - 1.0, -4096.0).astype(jnp.int32)
    slots_out[...] = slots
    slot_of, gate_of = [], []
    for expert in (mine, 1 - mine):
        level = jnp.where(first == expert, levels[0:1, :], levels[1:2, :])
        slot_of.append(jnp.where(expert == 0, slots[0:1, :], slots[1:2, :]))
        gate_of.append(level.astype(F32) * (1.0 / 16.0))
    row = iota((2 * rows, tokens), 0)
    slot = jnp.where(row < rows, slot_of[0], slot_of[1])
    gate = jnp.where(row < rows, gate_of[0], gate_of[1])
    place = row % rows
    total = jnp.zeros((2 * rows, span), F32)
    for cut in range(SEND_CUTS):
        lead = jnp.where(slot == place - cut * capacity, gate, 0.0).astype(BF16)
        large[cut].wait()
        total += nn(lead, grad[:, cut * span : (cut + 1) * span])
    own_out[...] = total[:rows].astype(BF16)
    other_out[...] = total[rows:].astype(BF16)


def hidden_kernel(n_dp, inputs, w_gate, w_up, *refs):
    ahead, (u_out, v_out, h_out) = refs[:-3], refs[-3:]
    a = nn(inputs[...], w_gate[...])
    b = nn(inputs[...], w_up[...])
    s = jax.nn.sigmoid(a)
    u = a * s
    u_out[...] = u
    v_out[...] = b * s * (1.0 + a * (1.0 - s))
    h = u * b
    h_out[...] = h
    pair = 2 * (inputs.shape[1] // n_dp)
    for out in ahead:
        start = pl.multiple_of(((lax.axis_index("dp") // 2) ^ LAST) * pair, 128)
        out[:, 0:pair] = inputs[:, pl.ds(start, pair)]
        out[:, pair:] = h.astype(BF16)


def pass_kernel(*refs):
    pass


def project_kernel(group, capacity, n_dp, *refs):
    received = restore(refs[:group], DISPATCH_ORDER)
    w_down, u_in, v_in, h_in, inputs = refs[group : group + 5]
    sends = refs[group + 5 : -4]
    da_out, db_out, gate_out, rows_buf = refs[-4:]
    rows, hidden = u_in.shape
    width = w_down.shape[1]
    span = width // SEND_CUTS
    me = lax.axis_index("expert")
    packed = SEND_CUTS * capacity
    every = jnp.concatenate([ref[...] for ref in received], axis=0)
    to = iota((rows, group * packed), 0)
    at = iota((rows, group * packed), 1)
    source = (at // packed) ^ me
    within = at % packed
    match = (to // capacity == source) & (to % capacity == within % capacity)
    projected = jnp.zeros((rows, hidden), F32)
    for cut in range(SEND_CUTS):
        select = (match & (within // capacity == cut)).astype(F32).astype(BF16)
        piece = nn(select, every).astype(BF16)
        rows_buf[:, cut * span : (cut + 1) * span] = piece
        projected += nt(piece, w_down[:, cut * span : (cut + 1) * span])
    da = (projected * v_in[...]).astype(BF16)
    db = (projected * u_in[...]).astype(BF16)
    h = h_in[...]
    da_out[...] = da
    db_out[...] = db
    gate = jnp.sum(h * projected, axis=1, keepdims=True)
    lane = iota((rows, GATE_LANES), 1)
    gate_out[...] = jnp.where(lane == me // (group // EXPERTS_W), gate, 0.0).astype(BF16)
    h = h.astype(BF16)
    if n_dp != PAIRED:
        sends[0][...] = rows_buf[...]
        sends[1][...] = h
        return
    pair = 2 * (width // n_dp)
    chip = lax.axis_index("dp") // 2
    for m, send in enumerate(sends):
        start = pl.multiple_of((chip ^ m) * pair, 128)
        base = 0
        if m < LAST:
            send[:, 0:pair] = inputs[:, pl.ds(start, pair)]
            send[:, pair : pair + hidden] = h
            base = pair + hidden
        send[:, base : base + pair] = rows_buf[:, pl.ds(start, pair)]
        send[:, base + pair : base + pair + hidden] = da
        send[:, base + pair + hidden :] = db


def input_kernel(group, capacity, da, db, gate, w_gate, w_up, *refs):
    outs = refs[-group:]
    rows = da.shape[0]
    width = w_gate.shape[0]
    span = width // BACK_CUTS
    step = width // W_CHUNKS
    per = W_CHUNKS // BACK_CUTS
    me = lax.axis_index("expert")
    packed = BACK_CUTS * capacity
    to = iota((group * packed, rows), 0)
    at = iota((group * packed, rows), 1)
    target = (to // packed) ^ me
    within = to % packed
    match = (at // capacity == target) & (at % capacity == within % capacity)
    selects = [
        (match & (within // capacity == cut)).astype(F32).astype(BF16) for cut in range(BACK_CUTS)
    ]
    total = [jnp.zeros((group * packed, step), F32) for _ in range(per)]
    for k in range(W_CHUNKS):
        part = nt(da[...], w_gate[k * step : (k + 1) * step, :])
        part += nt(db[...], w_up[k * step : (k + 1) * step, :])
        total[k % per] += nn(selects[k // per], part.astype(BF16))
    gates = nn(selects[0], gate[...])
    for n, out in enumerate(outs):
        for q in range(per):
            out[:, q * step : (q + 1) * step] = total[q][n * packed : (n + 1) * packed].astype(BF16)
        out[:, span:] = gates[n * packed : (n + 1) * packed].astype(BF16)


def halves(columns, refs):
    first = [(ref, 0) for ref in refs[: LAST + 1]]
    second = [(ref, columns) for ref in refs[:LAST]] + [(refs[-1], 0)]
    return first, second


def share_kernel(block, hidden, *refs):
    buffers, out = refs[:-1], refs[-1]
    rows = buffers[0].shape[0]
    start = (1 - lax.axis_index("dp") % 2) * block
    first, second = halves(2 * block + hidden, buffers)
    middle = block + hidden
    for m in range(LAST + 1):
        part = slice(m * rows, (m + 1) * rows)
        for (ref, at), to, wide in ((first[m], 0, middle), (second[m], middle, middle + hidden)):
            out[part, to : to + block] = ref[:, pl.ds(pl.multiple_of(at + start, 128), block)]
            at += 2 * block
            out[part, to + block : to + wide] = ref[:, at : at + wide - block]


def weight_kernel(block, hidden, *refs):
    buffers, out = refs[:-1], refs[-1]
    start = (lax.axis_index("dp") % 2) * block
    first, second = halves(2 * block + hidden, buffers)

    def gather(side, skip, wide):
        parts = [ref[:, pl.ds(pl.multiple_of(at + skip, 128), wide)] for ref, at in side]
        return jnp.concatenate(parts, axis=0)

    inputs, grads = gather(first, start, block), gather(second, start, block)
    out[0] = tn(inputs, gather(second, 2 * block, hidden))
    out[1] = tn(inputs, gather(second, 2 * block + hidden, hidden))
    out[2] = tn(grads, gather(first, 2 * block, hidden))


def finish_weights(hidden, partial, shared, out_hbm, buf, sems):
    block = buf.shape[1]
    middle = block + hidden
    inputs, h = shared[:, 0:block], shared[:, block:middle]
    grads, da = shared[:, middle : middle + block], shared[:, middle + block : 2 * middle]
    copies = []
    for n, (left, right) in enumerate(((inputs, da), (inputs, shared[:, 2 * middle :]), (grads, h))):
        buf[n] = partial[n] + tn(left, right)
        copies.append(pltpu.make_async_copy(buf.at[n], out_hbm.at[n], sems.at[n]))
        copies[-1].start()
    return copies


def finish_kernel(group, capacity, hidden, *refs):
    backs = restore(refs[:group], RETURN_ORDER)
    routes, levels, slots = refs[group : group + 3]
    copies = []
    if hidden > 0:
        partial, shared = refs[group + 3 : group + 5]
        input_hbm, gate_hbm, weight_hbm, weight_buf, weight_sems = refs[-8:-3]
        copies += finish_weights(hidden, partial, shared, weight_hbm, weight_buf, weight_sems)
    else:
        input_hbm, gate_hbm = refs[-5:-3]
    input_buf, gate_buf, sems = refs[-3:]
    tokens, width = input_buf.shape
    span = width // BACK_CUTS
    packed = BACK_CUTS * capacity
    shards = group // EXPERTS_W
    me = lax.axis_index("expert")
    every = jnp.concatenate([ref[...] for ref in backs], axis=0)
    row = iota((group * packed, tokens), 0)
    expert = ((row // packed) ^ me) // shards
    within = row % packed
    slot = jnp.where(expert == 0, slots[0:1, :], slots[1:2, :])
    match = within % capacity == slot
    picks = [
        (match & (within // capacity == cut)).astype(F32).astype(BF16) for cut in range(BACK_CUTS)
    ]
    gates = tn(every[:, span:], picks[0])
    for k in range(2):
        route = routes[k : k + 1, :]
        value = jnp.where(route == 0, gates[0:1, :], jnp.where(route == 1, gates[1:2, :], 0.0))
        gate_buf[k : k + 1, :] = value * (16.0 / levels[k : k + 1, :].astype(F32))
    copies.append(pltpu.make_async_copy(gate_buf, gate_hbm, sems.at[2 * BACK_CUTS]))
    copies[-1].start()
    for cut, pick in enumerate(picks):
        half = span // 2
        for n in range(2):
            part = pl.ds(cut * span + n * half, half)
            input_buf[:, part] = tn(pick, every[:, n * half : (n + 1) * half]).astype(BF16)
            copy = pltpu.make_async_copy(
                input_buf.at[:, part], input_hbm.at[:, part], sems.at[2 * cut + n]
            )
            copy.start()
            copies.append(copy)
    for copy in copies:
        copy.wait()


def swap(array, axis, size, mask):
    return lax.ppermute(array, axis, [(n, n ^ mask) for n in range(size)])


def far_first(group):
    return [*range(group // 2, group), *range(1, group // 2)]


def plain_weights(inputs, grads, rights):
    inputs = lax.all_to_all(inputs, "dp", split_axis=1, concat_axis=0, tiled=True)
    grads = lax.all_to_all(grads, "dp", split_axis=1, concat_axis=0, tiled=True)
    rights = [lax.all_gather(right, "dp", axis=0, tiled=True) for right in rights]
    return jnp.stack([tn(inputs, rights[0]), tn(inputs, rights[1]), tn(grads, rights[2])])


def per_device(grad_out, routes, gate_levels, saved_inputs, w_gate, w_up, w_down):
    group = lax.axis_size("expert")
    n_dp = lax.axis_size("dp")
    shards = group // EXPERTS_W
    rows, width = saved_inputs.shape
    capacity = rows // group
    hidden = w_gate.shape[1]
    tokens = grad_out.shape[0]
    block = width // n_dp
    paired = n_dp == PAIRED
    routes = routes.T
    gate_levels = gate_levels.T
    shape = jax.ShapeDtypeStruct

    packed = shape((SEND_CUTS * capacity, width // SEND_CUTS), BF16)
    own, other, slots = call(
        functools.partial(pick_kernel, shards, capacity),
        (packed, packed, shape((8, tokens), jnp.int32)),
        (routes, gate_levels, grad_out),
        [HBM] * 3,
        [
            pltpu.VMEM(routes.shape, jnp.int32),
            pltpu.VMEM(routes.shape, jnp.int32),
            pltpu.VMEM(grad_out.shape, BF16),
            pltpu.SemaphoreType.DMA((2 + SEND_CUTS,)),
        ],
        name="pick",
    )
    own, other = call(
        pass_kernel,
        (packed,) * 2,
        (own, other),
        [VMEM] * 2,
        aliases={0: 0, 1: 1},
        flops=HEAVY,
        name="pass",
    )
    received = [own] + [None] * (group - 1)
    for mask in far_first(group):
        received[mask] = swap(own if mask < shards else other, "expert", group, mask)
    part = shape((rows, hidden), F32)
    ahead = shape((rows, 2 * block + hidden), BF16)
    *ahead, u, v, h = call(
        functools.partial(hidden_kernel, n_dp),
        (ahead,) * paired + (part,) * 3,
        (saved_inputs, w_gate, w_up),
        [VMEM] * 3,
        flops=HEAVY,
        name="hidden",
    )
    half = shape((rows, hidden), BF16)
    late = shape((rows, 2 * block + 2 * hidden), BF16)
    full = shape((rows, 4 * block + 3 * hidden), BF16)
    outward = (full,) * LAST + (late,) if paired else (shape((rows, width), BF16), half)
    *sends, da, db, gate = call(
        functools.partial(project_kernel, group, capacity, n_dp),
        outward + (half, half, shape((rows, GATE_LANES), BF16)),
        (*arrange(received, DISPATCH_ORDER), w_down, u, v, h, saved_inputs),
        [VMEM] * (group + 5),
        [pltpu.VMEM((rows, width), BF16)],
        flops=HEAVY,
        name="project",
    )
    ahead = [swap(array, "dp", n_dp, 2 * LAST) for array in ahead]
    back = shape((BACK_CUTS * capacity, width // BACK_CUTS + GATE_LANES), BF16)
    returns = call(
        functools.partial(input_kernel, group, capacity),
        (back,) * group,
        (da, db, gate, w_gate, w_up, *ahead),
        [VMEM] * 5 + [UNUSED] * len(ahead),
        flops=HEAVY,
        name="input",
    )
    backs = [returns[0]] + [None] * (group - 1)
    for mask in far_first(group):
        backs[mask] = swap(returns[mask], "expert", group, mask)
    if paired:
        got = [sends[0]] + [swap(sends[m], "dp", n_dp, 2 * m) for m in range(1, LAST + 1)]
        buffers = got[:LAST] + ahead + got[LAST:]
        sharing = call(
            functools.partial(share_kernel, block, hidden),
            shape(((LAST + 1) * rows, 2 * block + 3 * hidden), BF16),
            buffers,
            [VMEM] * len(buffers),
            name="share",
        )
        shared = swap(sharing, "dp", n_dp, 1)
        block_shape = shape((3, block, hidden), F32)
        partial = call(
            functools.partial(weight_kernel, block, hidden),
            block_shape,
            buffers,
            [VMEM] * len(buffers),
            flops=HEAVY,
            name="weight",
        )
        extra = (partial, shared)
    else:
        extra = ()
    finished = (shape((tokens, width), BF16), shape((2, tokens), F32))
    scratch = [
        pltpu.VMEM((tokens, width), BF16),
        pltpu.VMEM((2, tokens), F32),
        pltpu.SemaphoreType.DMA((2 * BACK_CUTS + 1,)),
    ]
    if paired:
        finished += (block_shape,)
        scratch = [pltpu.VMEM(block_shape.shape, F32), pltpu.SemaphoreType.DMA((3,))] + scratch
    input_grad, gate_grad, *weight_grad = call(
        functools.partial(finish_kernel, group, capacity, hidden if paired else 0),
        finished,
        (*arrange(backs, RETURN_ORDER), routes, gate_levels, slots, *extra),
        [VMEM] * (group + 3 + len(extra)),
        scratch,
        near=False,
        out_specs=(HBM,) * len(finished),
        flops=HEAVY,
        name="finish",
    )
    if paired:
        (weight_grad,) = weight_grad
    else:
        weight_grad = plain_weights(saved_inputs, sends[0], (da, db, sends[1]))
    return input_grad, gate_grad.T, weight_grad.transpose(1, 0, 2)


def solution(mesh):
    in_specs = (
        P(("dp", "expert"), None),
        P(("dp", "expert"), None),
        P(("dp", "expert"), None),
        P(("dp", "expert"), None),
        P(None, "expert"),
        P(None, "expert"),
        P("expert", None),
    )
    out_specs = (P(("dp", "expert"), None), P(("dp", "expert"), None), P("dp", None, "expert"))
    return jax.shard_map(
        per_device, mesh=mesh, in_specs=in_specs, out_specs=out_specs, check_vma=False
    )
```

```python
import functools

import jax
import jax.numpy as jnp
from jax import lax
from jax.experimental import pallas as pl
from jax.experimental.pallas import tpu as pltpu
from jax.sharding import PartitionSpec as P

EXPERTS_W = 2
SEND_CUTS = 4
BACK_CUTS = 2
GATE_LANES = 128
W_CHUNKS = 4
TURNED = 2
LAST = 3
HEAVY = 10**10
DISPATCH_ORDER = (0, 3, 2, 1)
RETURN_ORDER = (0, 3, 2, 1)
PAIRED = 8
F32 = jnp.float32
BF16 = jnp.bfloat16
VMEM = pl.BlockSpec(memory_space=pltpu.VMEM)
HBM = pl.BlockSpec(memory_space=pltpu.HBM)
UNUSED = pl.BlockSpec(memory_space=pl.ANY)


def nn(left, right):
    return lax.dot_general(left, right, (((1,), (0,)), ((), ())), preferred_element_type=F32)


def nt(left, right):
    return lax.dot_general(left, right, (((1,), (1,)), ((), ())), preferred_element_type=F32)


def tn(left, right):
    return lax.dot_general(left, right, (((0,), (0,)), ((), ())), preferred_element_type=F32)


def iota(shape, dim):
    return lax.broadcasted_iota(jnp.int32, shape, dim)


def call(kernel, outs, args, specs, scratch=(), near=True, out_specs=None, aliases=None, flops=0, name=None):
    args = [
        pltpu.with_memory_space_constraint(arg, pltpu.HBM) if spec is HBM else arg
        for arg, spec in zip(args, specs)
    ]
    if near:
        outs = jax.tree.map(lambda out: pltpu.VMEM(out.shape, out.dtype), outs)
    return pl.pallas_call(
        kernel,
        out_shape=outs,
        in_specs=specs,
        out_specs=out_specs or jax.tree.map(lambda _: VMEM, outs),
        scratch_shapes=scratch,
        input_output_aliases=aliases or {},
        compiler_params=pltpu.CompilerParams(vmem_limit_bytes=24 * 1024 * 1024),
        cost_estimate=pl.CostEstimate(flops=flops, bytes_accessed=0, transcendentals=0),
        name=name,
    )(*args)


def arrange(arrays, order):
    return [arrays[mask] for mask in order] if len(arrays) == len(order) else arrays


def restore(refs, order):
    if len(refs) != len(order):
        return refs
    return [refs[order.index(mask)] for mask in range(len(refs))]


def pick_kernel(
    shards, capacity, routes_hbm, levels_hbm, grad_hbm, own_out, other_out, slots_out,
    routes, levels, grad, sems,
):
    tokens, width = grad.shape
    span = width // SEND_CUTS
    rows = SEND_CUTS * capacity
    small = [
        pltpu.make_async_copy(routes_hbm, routes, sems.at[0]),
        pltpu.make_async_copy(levels_hbm, levels, sems.at[1]),
    ]
    large = [
        pltpu.make_async_copy(
            grad_hbm.at[:, pl.ds(cut * span, span)],
            grad.at[:, pl.ds(cut * span, span)],
            sems.at[2 + cut],
        )
        for cut in range(SEND_CUTS)
    ]
    for copy in small + large:
        copy.start()
    mine = lax.axis_index("expert") // shards
    upto = (iota((tokens, tokens), 0) <= iota((tokens, tokens), 1)).astype(BF16)
    for copy in small:
        copy.wait()
    first, second = routes[0:1, :], routes[1:2, :]
    found = jnp.zeros((8, tokens), F32)
    for expert in range(EXPERTS_W):
        hit = ((first == expert) | (second == expert)).astype(F32)
        found = jnp.where(iota((8, tokens), 0) == expert, hit, found)
    counted = nn(found.astype(BF16), upto)
    slots = jnp.where(found > 0, counted - 1.0, -4096.0).astype(jnp.int32)
    slots_out[...] = slots
    slot_of, gate_of = [], []
    for expert in (mine, 1 - mine):
        level = jnp.where(first == expert, levels[0:1, :], levels[1:2, :])
        slot_of.append(jnp.where(expert == 0, slots[0:1, :], slots[1:2, :]))
        gate_of.append(level.astype(F32) * (1.0 / 16.0))
    row = iota((2 * rows, tokens), 0)
    slot = jnp.where(row < rows, slot_of[0], slot_of[1])
    gate = jnp.where(row < rows, gate_of[0], gate_of[1])
    place = row % rows
    total = jnp.zeros((2 * rows, span), F32)
    for cut in range(SEND_CUTS):
        lead = jnp.where(slot == place - cut * capacity, gate, 0.0).astype(BF16)
        large[cut].wait()
        total += nn(lead, grad[:, cut * span : (cut + 1) * span])
    own_out[...] = total[:rows].astype(BF16)
    other_out[...] = total[rows:].astype(BF16)


def hidden_kernel(n_dp, inputs, w_gate, w_up, *refs):
    ahead, (u_out, v_out, h_out) = refs[:-3], refs[-3:]
    a = nn(inputs[...], w_gate[...])
    b = nn(inputs[...], w_up[...])
    s = jax.nn.sigmoid(a)
    u = a * s
    v = b * s * (1.0 + a * (1.0 - s))
    u_out[...] = u
    v_out[...] = v
    h = u * b
    h_out[...] = h
    pair = 2 * (inputs.shape[1] // n_dp)
    for out in ahead:
        start = pl.multiple_of(((lax.axis_index("dp") // 2) ^ LAST) * pair, 128)
        out[:, 0:pair] = inputs[:, pl.ds(start, pair)]
        for n, value in enumerate((h, u, v)):
            hidden = value.shape[1]
            out[:, pair + n * hidden : pair + (n + 1) * hidden] = value.astype(BF16)


def turn_kernel(*refs):
    for ref, out in zip(refs[: len(refs) // 2], refs[len(refs) // 2 :]):
        step = ref.shape[0] // W_CHUNKS
        for k in range(W_CHUNKS):
            part = slice(k * step, (k + 1) * step)
            out[:, part] = ref[part, :].T


def pass_kernel(*refs):
    pass


def project_kernel(group, capacity, n_dp, *refs):
    received = restore(refs[:group], DISPATCH_ORDER)
    w_down, u_in, v_in, h_in, inputs = refs[group : group + 5]
    sends = refs[group + 5 + TURNED : -4]
    da_out, db_out, gate_out, rows_buf = refs[-4:]
    rows, hidden = u_in.shape
    width = w_down.shape[1]
    span = width // SEND_CUTS
    me = lax.axis_index("expert")
    packed = SEND_CUTS * capacity
    every = jnp.concatenate([ref[...] for ref in received], axis=0)
    to = iota((rows, group * packed), 0)
    at = iota((rows, group * packed), 1)
    source = (at // packed) ^ me
    within = at % packed
    match = (to // capacity == source) & (to % capacity == within % capacity)
    projected = jnp.zeros((rows, hidden), F32)
    for cut in range(SEND_CUTS):
        select = (match & (within // capacity == cut)).astype(F32).astype(BF16)
        piece = nn(select, every).astype(BF16)
        rows_buf[:, cut * span : (cut + 1) * span] = piece
        projected += nt(piece, w_down[:, cut * span : (cut + 1) * span])
    da = (projected * v_in[...]).astype(BF16)
    db = (projected * u_in[...]).astype(BF16)
    h = h_in[...]
    da_out[...] = da
    db_out[...] = db
    gate = jnp.sum(h * projected, axis=1, keepdims=True)
    lane = iota((rows, GATE_LANES), 1)
    gate_out[...] = jnp.where(lane == me // (group // EXPERTS_W), gate, 0.0).astype(BF16)
    h = h.astype(BF16)
    if n_dp != PAIRED:
        sends[0][...] = rows_buf[...]
        sends[1][...] = h
        return
    pair = 2 * (width // n_dp)
    chip = lax.axis_index("dp") // 2
    for m, send in enumerate(sends):
        start = pl.multiple_of((chip ^ m) * pair, 128)
        base = 0
        if m < LAST:
            send[:, 0:pair] = inputs[:, pl.ds(start, pair)]
            send[:, pair : pair + hidden] = h
            base = pair + hidden
        send[:, base : base + pair] = rows_buf[:, pl.ds(start, pair)]
        if m < LAST:
            send[:, base + pair : base + pair + hidden] = da
            send[:, base + pair + hidden :] = db
        else:
            send[:, pair:] = projected.astype(BF16)


def input_kernel(group, capacity, da, db, gate, w_gate, w_up, *refs):
    outs = refs[-group:]
    rows = da.shape[0]
    width = max(w_gate.shape)
    span = width // BACK_CUTS
    step = width // W_CHUNKS
    per = W_CHUNKS // BACK_CUTS
    me = lax.axis_index("expert")
    packed = BACK_CUTS * capacity
    to = iota((group * packed, rows), 0)
    at = iota((group * packed, rows), 1)
    target = (to // packed) ^ me
    within = to % packed
    match = (at // capacity == target) & (at % capacity == within % capacity)
    selects = [
        (match & (within // capacity == cut)).astype(F32).astype(BF16) for cut in range(BACK_CUTS)
    ]
    total = [jnp.zeros((group * packed, step), F32) for _ in range(per)]
    for k in range(W_CHUNKS):
        piece = slice(k * step, (k + 1) * step)
        part = nn(da[...], w_gate[:, piece])
        if TURNED > 1:
            part += nn(db[...], w_up[:, piece])
        else:
            part += nt(db[...], w_up[piece, :])
        total[k % per] += nn(selects[k // per], part.astype(BF16))
    gates = nn(selects[0], gate[...])
    for n, out in enumerate(outs):
        for q in range(per):
            out[:, q * step : (q + 1) * step] = total[q][n * packed : (n + 1) * packed].astype(BF16)
        out[:, span:] = gates[n * packed : (n + 1) * packed].astype(BF16)


def rows_of(block, hidden, core, refs):
    start = pl.multiple_of(core * block, 128)
    pair = 2 * block
    first, last = refs[0], refs[-1]
    base = pair + hidden if len(refs) == 1 else 0
    grads = last[:, pl.ds(pl.multiple_of(base + start, 128), block)]
    base += pair
    da = last[:, base : base + hidden]
    if len(refs) == 1:
        db = last[:, base + hidden : base + 2 * hidden]
    else:
        projected = da.astype(F32)
        u, v = (first[:, pair + n * hidden : pair + (n + 1) * hidden] for n in (1, 2))
        da = (projected * v.astype(F32)).astype(BF16)
        db = (projected * u.astype(F32)).astype(BF16)
    return first[:, pl.ds(start, block)], first[:, pair : pair + hidden], grads, da, db


def chips_of(refs):
    return [refs[n : n + 1] for n in range(LAST)] + [refs[LAST:]]


def share_kernel(block, hidden, *refs):
    out = refs[-1]
    core = 1 - lax.axis_index("dp") % 2
    for m, chip in enumerate(chips_of(refs[:-1])):
        rows = chip[0].shape[0]
        at = 0
        for value in rows_of(block, hidden, core, chip):
            out[m * rows : (m + 1) * rows, at : at + value.shape[1]] = value
            at += value.shape[1]


def weight_kernel(block, hidden, *refs):
    out = refs[-1]
    core = lax.axis_index("dp") % 2
    chips = [rows_of(block, hidden, core, chip) for chip in chips_of(refs[:-1])]
    inputs, h, grads, da, db = (jnp.concatenate(values, axis=0) for values in zip(*chips))
    out[0] = tn(inputs, da)
    out[1] = tn(inputs, db)
    out[2] = tn(grads, h)


def finish_weights(hidden, partial, shared, out_hbm, buf, sems):
    block = buf.shape[1]
    middle = block + hidden
    inputs, h = shared[:, 0:block], shared[:, block:middle]
    grads, da = shared[:, middle : middle + block], shared[:, middle + block : 2 * middle]
    copies = []
    for n, (left, right) in enumerate(((inputs, da), (inputs, shared[:, 2 * middle :]), (grads, h))):
        buf[n] = partial[n] + tn(left, right)
        copies.append(pltpu.make_async_copy(buf.at[n], out_hbm.at[n], sems.at[n]))
        copies[-1].start()
    return copies


def finish_kernel(group, capacity, hidden, *refs):
    backs = restore(refs[:group], RETURN_ORDER)
    routes, levels, slots = refs[group : group + 3]
    copies = []
    if hidden > 0:
        partial, shared = refs[group + 3 : group + 5]
        input_hbm, gate_hbm, weight_hbm, weight_buf, weight_sems = refs[-8:-3]
        copies += finish_weights(hidden, partial, shared, weight_hbm, weight_buf, weight_sems)
    else:
        input_hbm, gate_hbm = refs[-5:-3]
    input_buf, gate_buf, sems = refs[-3:]
    tokens, width = input_buf.shape
    span = width // BACK_CUTS
    packed = BACK_CUTS * capacity
    shards = group // EXPERTS_W
    me = lax.axis_index("expert")
    every = jnp.concatenate([ref[...] for ref in backs], axis=0)
    row = iota((group * packed, tokens), 0)
    expert = ((row // packed) ^ me) // shards
    within = row % packed
    slot = jnp.where(expert == 0, slots[0:1, :], slots[1:2, :])
    match = within % capacity == slot
    picks = [
        (match & (within // capacity == cut)).astype(F32).astype(BF16) for cut in range(BACK_CUTS)
    ]
    gates = tn(every[:, span:], picks[0])
    for k in range(2):
        route = routes[k : k + 1, :]
        value = jnp.where(route == 0, gates[0:1, :], jnp.where(route == 1, gates[1:2, :], 0.0))
        gate_buf[k : k + 1, :] = value * (16.0 / levels[k : k + 1, :].astype(F32))
    copies.append(pltpu.make_async_copy(gate_buf, gate_hbm, sems.at[2 * BACK_CUTS]))
    copies[-1].start()
    for cut, pick in enumerate(picks):
        half = span // 2
        for n in range(2):
            part = pl.ds(cut * span + n * half, half)
            input_buf[:, part] = tn(pick, every[:, n * half : (n + 1) * half]).astype(BF16)
            copy = pltpu.make_async_copy(
                input_buf.at[:, part], input_hbm.at[:, part], sems.at[2 * cut + n]
            )
            copy.start()
            copies.append(copy)
    for copy in copies:
        copy.wait()


def swap(array, axis, size, mask):
    return lax.ppermute(array, axis, [(n, n ^ mask) for n in range(size)])


def far_first(group):
    return [*range(group // 2, group), *range(1, group // 2)]


def plain_weights(inputs, grads, rights):
    inputs = lax.all_to_all(inputs, "dp", split_axis=1, concat_axis=0, tiled=True)
    grads = lax.all_to_all(grads, "dp", split_axis=1, concat_axis=0, tiled=True)
    rights = [lax.all_gather(right, "dp", axis=0, tiled=True) for right in rights]
    return jnp.stack([tn(inputs, rights[0]), tn(inputs, rights[1]), tn(grads, rights[2])])


def per_device(grad_out, routes, gate_levels, saved_inputs, w_gate, w_up, w_down):
    group = lax.axis_size("expert")
    n_dp = lax.axis_size("dp")
    shards = group // EXPERTS_W
    rows, width = saved_inputs.shape
    capacity = rows // group
    hidden = w_gate.shape[1]
    tokens = grad_out.shape[0]
    block = width // n_dp
    paired = n_dp == PAIRED
    routes = routes.T
    gate_levels = gate_levels.T
    shape = jax.ShapeDtypeStruct

    packed = shape((SEND_CUTS * capacity, width // SEND_CUTS), BF16)
    own, other, slots = call(
        functools.partial(pick_kernel, shards, capacity),
        (packed, packed, shape((8, tokens), jnp.int32)),
        (routes, gate_levels, grad_out),
        [HBM] * 3,
        [
            pltpu.VMEM(routes.shape, jnp.int32),
            pltpu.VMEM(routes.shape, jnp.int32),
            pltpu.VMEM(grad_out.shape, BF16),
            pltpu.SemaphoreType.DMA((2 + SEND_CUTS,)),
        ],
        name="pick",
    )
    own, other = call(
        pass_kernel,
        (packed,) * 2,
        (own, other),
        [VMEM] * 2,
        aliases={0: 0, 1: 1},
        flops=HEAVY,
        name="pass",
    )
    received = [own] + [None] * (group - 1)
    for mask in far_first(group):
        received[mask] = swap(own if mask < shards else other, "expert", group, mask)
    part = shape((rows, hidden), F32)
    ahead = shape((rows, 2 * block + 3 * hidden), BF16)
    *ahead, u, v, h = call(
        functools.partial(hidden_kernel, n_dp),
        (ahead,) * paired + (part,) * 3,
        (saved_inputs, w_gate, w_up),
        [VMEM] * 3,
        flops=HEAVY,
        name="hidden",
    )
    turned = call(
        turn_kernel,
        (shape((hidden, width), BF16),) * TURNED,
        (w_gate, w_up)[:TURNED],
        [VMEM] * TURNED,
        flops=HEAVY,
        name="turn",
    )
    half = shape((rows, hidden), BF16)
    late = shape((rows, 2 * block + hidden), BF16)
    full = shape((rows, 4 * block + 3 * hidden), BF16)
    outward = (full,) * LAST + (late,) if paired else (shape((rows, width), BF16), half)
    *sends, da, db, gate = call(
        functools.partial(project_kernel, group, capacity, n_dp),
        outward + (half, half, shape((rows, GATE_LANES), BF16)),
        (*arrange(received, DISPATCH_ORDER), w_down, u, v, h, saved_inputs, *turned),
        [VMEM] * (group + 5) + [UNUSED] * TURNED,
        [pltpu.VMEM((rows, width), BF16)],
        name="project",
    )
    ahead = [swap(array, "dp", n_dp, 2 * LAST) for array in ahead]
    back = shape((BACK_CUTS * capacity, width // BACK_CUTS + GATE_LANES), BF16)
    returns = call(
        functools.partial(input_kernel, group, capacity),
        (back,) * group,
        (da, db, gate, *turned, *(w_gate, w_up)[TURNED:], *ahead),
        [VMEM] * 5 + [UNUSED] * len(ahead),
        flops=HEAVY,
        name="input",
    )
    backs = [returns[0]] + [None] * (group - 1)
    for mask in far_first(group):
        backs[mask] = swap(returns[mask], "expert", group, mask)
    if paired:
        got = [sends[0]] + [swap(sends[m], "dp", n_dp, 2 * m) for m in range(1, LAST + 1)]
        buffers = got[:LAST] + ahead + got[LAST:]
        sharing = call(
            functools.partial(share_kernel, block, hidden),
            shape(((LAST + 1) * rows, 2 * block + 3 * hidden), BF16),
            buffers,
            [VMEM] * len(buffers),
            name="share",
        )
        shared = swap(sharing, "dp", n_dp, 1)
        block_shape = shape((3, block, hidden), F32)
        partial = call(
            functools.partial(weight_kernel, block, hidden),
            block_shape,
            buffers,
            [VMEM] * len(buffers),
            flops=HEAVY,
            name="weight",
        )
        extra = (partial, shared)
    else:
        extra = ()
    finished = (shape((tokens, width), BF16), shape((2, tokens), F32))
    scratch = [
        pltpu.VMEM((tokens, width), BF16),
        pltpu.VMEM((2, tokens), F32),
        pltpu.SemaphoreType.DMA((2 * BACK_CUTS + 1,)),
    ]
    if paired:
        finished += (block_shape,)
        scratch = [pltpu.VMEM(block_shape.shape, F32), pltpu.SemaphoreType.DMA((3,))] + scratch
    input_grad, gate_grad, *weight_grad = call(
        functools.partial(finish_kernel, group, capacity, hidden if paired else 0),
        finished,
        (*arrange(backs, RETURN_ORDER), routes, gate_levels, slots, *extra),
        [VMEM] * (group + 3 + len(extra)),
        scratch,
        near=False,
        out_specs=(HBM,) * len(finished),
        flops=HEAVY,
        name="finish",
    )
    if paired:
        (weight_grad,) = weight_grad
    else:
        weight_grad = plain_weights(saved_inputs, sends[0], (da, db, sends[1]))
    return input_grad, gate_grad.T, weight_grad.transpose(1, 0, 2)


def solution(mesh):
    in_specs = (
        P(("dp", "expert"), None),
        P(("dp", "expert"), None),
        P(("dp", "expert"), None),
        P(("dp", "expert"), None),
        P(None, "expert"),
        P(None, "expert"),
        P("expert", None),
    )
    out_specs = (P(("dp", "expert"), None), P(("dp", "expert"), None), P("dp", None, "expert"))
    return jax.shard_map(
        per_device, mesh=mesh, in_specs=in_specs, out_specs=out_specs, check_vma=False
    )
```

```python
import functools

import jax
import jax.numpy as jnp
from jax import lax
from jax.experimental import pallas as pl
from jax.experimental.pallas import tpu as pltpu
from jax.sharding import PartitionSpec as P

EXPERTS_W = 2
SEND_CUTS = 4
BACK_CUTS = 2
GATE_LANES = 128
W_CHUNKS = 4
TURNED = 2
LAST = 3
HEAVY = 10**10
DISPATCH_ORDER = (0, 3, 2, 1)
RETURN_ORDER = (0, 3, 2, 1)
PAIRED = 8
F32 = jnp.float32
BF16 = jnp.bfloat16
VMEM = pl.BlockSpec(memory_space=pltpu.VMEM)
HBM = pl.BlockSpec(memory_space=pltpu.HBM)
UNUSED = pl.BlockSpec(memory_space=pl.ANY)


def nn(left, right):
    return lax.dot_general(left, right, (((1,), (0,)), ((), ())), preferred_element_type=F32)


def nt(left, right):
    return lax.dot_general(left, right, (((1,), (1,)), ((), ())), preferred_element_type=F32)


def tn(left, right):
    return lax.dot_general(left, right, (((0,), (0,)), ((), ())), preferred_element_type=F32)


def iota(shape, dim):
    return lax.broadcasted_iota(jnp.int32, shape, dim)


def call(kernel, outs, args, specs, scratch=(), near=True, out_specs=None, flops=0, name=None):
    args = [
        pltpu.with_memory_space_constraint(arg, pltpu.HBM) if spec is HBM else arg
        for arg, spec in zip(args, specs)
    ]
    if near:
        outs = jax.tree.map(lambda out: pltpu.VMEM(out.shape, out.dtype), outs)
    return pl.pallas_call(
        kernel,
        out_shape=outs,
        in_specs=specs,
        out_specs=out_specs or jax.tree.map(lambda _: VMEM, outs),
        scratch_shapes=scratch,
        compiler_params=pltpu.CompilerParams(vmem_limit_bytes=24 * 1024 * 1024),
        cost_estimate=pl.CostEstimate(flops=flops, bytes_accessed=0, transcendentals=0),
        name=name,
    )(*args)


def arrange(arrays, order):
    return [arrays[mask] for mask in order] if len(arrays) == len(order) else arrays


def restore(refs, order):
    if len(refs) != len(order):
        return refs
    return [refs[order.index(mask)] for mask in range(len(refs))]


def pick_kernel(
    shards, capacity, routes_hbm, levels_hbm, grad_hbm, own_out, other_out, slots_out,
    routes, levels, grad, sems,
):
    tokens, width = grad.shape
    span = width // SEND_CUTS
    rows = SEND_CUTS * capacity
    small = [
        pltpu.make_async_copy(routes_hbm, routes, sems.at[0]),
        pltpu.make_async_copy(levels_hbm, levels, sems.at[1]),
    ]
    large = [
        pltpu.make_async_copy(
            grad_hbm.at[:, pl.ds(cut * span, span)],
            grad.at[:, pl.ds(cut * span, span)],
            sems.at[2 + cut],
        )
        for cut in range(SEND_CUTS)
    ]
    for copy in small + large:
        copy.start()
    mine = lax.axis_index("expert") // shards
    upto = (iota((tokens, tokens), 0) <= iota((tokens, tokens), 1)).astype(BF16)
    for copy in small:
        copy.wait()
    first, second = routes[0:1, :], routes[1:2, :]
    found = jnp.zeros((8, tokens), F32)
    for expert in range(EXPERTS_W):
        hit = ((first == expert) | (second == expert)).astype(F32)
        found = jnp.where(iota((8, tokens), 0) == expert, hit, found)
    counted = nn(found.astype(BF16), upto)
    slots = jnp.where(found > 0, counted - 1.0, -4096.0).astype(jnp.int32)
    slots_out[...] = slots
    slot_of, gate_of = [], []
    for expert in (mine, 1 - mine):
        level = jnp.where(first == expert, levels[0:1, :], levels[1:2, :])
        slot_of.append(jnp.where(expert == 0, slots[0:1, :], slots[1:2, :]))
        gate_of.append(level.astype(F32) * (1.0 / 16.0))
    row = iota((2 * rows, tokens), 0)
    slot = jnp.where(row < rows, slot_of[0], slot_of[1])
    gate = jnp.where(row < rows, gate_of[0], gate_of[1])
    place = row % rows
    total = jnp.zeros((2 * rows, span), F32)
    for cut in range(SEND_CUTS):
        lead = jnp.where(slot == place - cut * capacity, gate, 0.0).astype(BF16)
        large[cut].wait()
        total += nn(lead, grad[:, cut * span : (cut + 1) * span])
    own_out[...] = total[:rows].astype(BF16)
    other_out[...] = total[rows:].astype(BF16)


def hidden_kernel(n_dp, inputs, w_gate, w_up, *refs):
    ahead, (u_out, v_out, h_out) = refs[:-3], refs[-3:]
    a = nn(inputs[...], w_gate[...])
    b = nn(inputs[...], w_up[...])
    s = jax.nn.sigmoid(a)
    u = a * s
    v = b * s * (1.0 + a * (1.0 - s))
    u_out[...] = u
    v_out[...] = v
    h = u * b
    h_out[...] = h
    pair = 2 * (inputs.shape[1] // n_dp)
    for out in ahead:
        start = pl.multiple_of(((lax.axis_index("dp") // 2) ^ LAST) * pair, 128)
        out[:, 0:pair] = inputs[:, pl.ds(start, pair)]
        for n, value in enumerate((h, u, v)):
            hidden = value.shape[1]
            out[:, pair + n * hidden : pair + (n + 1) * hidden] = value.astype(BF16)


def turn_kernel(*refs):
    for ref, out in zip(refs[: len(refs) // 2], refs[len(refs) // 2 :]):
        step = ref.shape[0] // W_CHUNKS
        for k in range(W_CHUNKS):
            part = slice(k * step, (k + 1) * step)
            out[:, part] = ref[part, :].T


def pass_kernel(own, other, own_out, other_out):
    own_out[...] = own[...]
    other_out[...] = other[...]


def project_kernel(group, capacity, n_dp, *refs):
    received = restore(refs[:group], DISPATCH_ORDER)
    w_down, u_in, v_in, h_in, inputs = refs[group : group + 5]
    sends = refs[group + 5 + TURNED : -4]
    da_out, db_out, gate_out, rows_buf = refs[-4:]
    rows, hidden = u_in.shape
    width = w_down.shape[1]
    span = width // SEND_CUTS
    me = lax.axis_index("expert")
    packed = SEND_CUTS * capacity
    every = jnp.concatenate([ref[...] for ref in received], axis=0)
    to = iota((rows, group * packed), 0)
    at = iota((rows, group * packed), 1)
    source = (at // packed) ^ me
    within = at % packed
    match = (to // capacity == source) & (to % capacity == within % capacity)
    projected = jnp.zeros((rows, hidden), F32)
    for cut in range(SEND_CUTS):
        select = (match & (within // capacity == cut)).astype(F32).astype(BF16)
        piece = nn(select, every).astype(BF16)
        rows_buf[:, cut * span : (cut + 1) * span] = piece
        projected += nt(piece, w_down[:, cut * span : (cut + 1) * span])
    da = (projected * v_in[...]).astype(BF16)
    db = (projected * u_in[...]).astype(BF16)
    h = h_in[...]
    da_out[...] = da
    db_out[...] = db
    gate = jnp.sum(h * projected, axis=1, keepdims=True)
    lane = iota((rows, GATE_LANES), 1)
    gate_out[...] = jnp.where(lane == me // (group // EXPERTS_W), gate, 0.0).astype(BF16)
    h = h.astype(BF16)
    if n_dp != PAIRED:
        sends[0][...] = rows_buf[...]
        sends[1][...] = h
        return
    pair = 2 * (width // n_dp)
    chip = lax.axis_index("dp") // 2
    for m, send in enumerate(sends):
        start = pl.multiple_of((chip ^ m) * pair, 128)
        base = 0
        if m < LAST:
            send[:, 0:pair] = inputs[:, pl.ds(start, pair)]
            send[:, pair : pair + hidden] = h
            base = pair + hidden
        send[:, base : base + pair] = rows_buf[:, pl.ds(start, pair)]
        if m < LAST:
            send[:, base + pair : base + pair + hidden] = da
            send[:, base + pair + hidden :] = db
        else:
            send[:, pair:] = projected.astype(BF16)


def input_kernel(group, capacity, da, db, gate, w_gate, w_up, *refs):
    outs = refs[-group:]
    rows = da.shape[0]
    width = max(w_gate.shape)
    span = width // BACK_CUTS
    step = width // W_CHUNKS
    per = W_CHUNKS // BACK_CUTS
    me = lax.axis_index("expert")
    packed = BACK_CUTS * capacity
    to = iota((group * packed, rows), 0)
    at = iota((group * packed, rows), 1)
    target = (to // packed) ^ me
    within = to % packed
    match = (at // capacity == target) & (at % capacity == within % capacity)
    selects = [
        (match & (within // capacity == cut)).astype(F32).astype(BF16) for cut in range(BACK_CUTS)
    ]
    total = [jnp.zeros((group * packed, step), F32) for _ in range(per)]
    for k in range(W_CHUNKS):
        piece = slice(k * step, (k + 1) * step)
        part = nn(da[...], w_gate[:, piece])
        if TURNED > 1:
            part += nn(db[...], w_up[:, piece])
        else:
            part += nt(db[...], w_up[piece, :])
        total[k % per] += nn(selects[k // per], part.astype(BF16))
    gates = nn(selects[0], gate[...])
    for n, out in enumerate(outs):
        for q in range(per):
            out[:, q * step : (q + 1) * step] = total[q][n * packed : (n + 1) * packed].astype(BF16)
        out[:, span:] = gates[n * packed : (n + 1) * packed].astype(BF16)


def rows_of(block, hidden, core, refs):
    start = pl.multiple_of(core * block, 128)
    pair = 2 * block
    first, last = refs[0], refs[-1]
    base = pair + hidden if len(refs) == 1 else 0
    grads = last[:, pl.ds(pl.multiple_of(base + start, 128), block)]
    base += pair
    da = last[:, base : base + hidden]
    if len(refs) == 1:
        db = last[:, base + hidden : base + 2 * hidden]
    else:
        projected = da.astype(F32)
        u, v = (first[:, pair + n * hidden : pair + (n + 1) * hidden] for n in (1, 2))
        da = (projected * v.astype(F32)).astype(BF16)
        db = (projected * u.astype(F32)).astype(BF16)
    return first[:, pl.ds(start, block)], first[:, pair : pair + hidden], grads, da, db


def chips_of(refs):
    return [refs[n : n + 1] for n in range(LAST)] + [refs[LAST:]]


def share_kernel(block, hidden, *refs):
    out = refs[-1]
    core = 1 - lax.axis_index("dp") % 2
    for m, chip in enumerate(chips_of(refs[:-1])):
        rows = chip[0].shape[0]
        at = 0
        for value in rows_of(block, hidden, core, chip):
            out[m * rows : (m + 1) * rows, at : at + value.shape[1]] = value
            at += value.shape[1]


def weight_kernel(block, hidden, *refs):
    out = refs[-1]
    core = lax.axis_index("dp") % 2
    chips = [rows_of(block, hidden, core, chip) for chip in chips_of(refs[:-1])]
    inputs, h, grads, da, db = (jnp.concatenate(values, axis=0) for values in zip(*chips))
    out[0] = tn(inputs, da)
    out[1] = tn(inputs, db)
    out[2] = tn(grads, h)


def finish_weights(hidden, partial, shared, out_hbm, buf, sems):
    block = buf.shape[1]
    middle = block + hidden
    inputs, h = shared[:, 0:block], shared[:, block:middle]
    grads, da = shared[:, middle : middle + block], shared[:, middle + block : 2 * middle]
    copies = []
    for n, (left, right) in enumerate(((inputs, da), (inputs, shared[:, 2 * middle :]), (grads, h))):
        buf[n] = partial[n] + tn(left, right)
        copies.append(pltpu.make_async_copy(buf.at[n], out_hbm.at[n], sems.at[n]))
        copies[-1].start()
    return copies


def finish_kernel(group, capacity, hidden, *refs):
    backs = restore(refs[:group], RETURN_ORDER)
    routes, levels, slots = refs[group : group + 3]
    copies = []
    if hidden > 0:
        partial, shared = refs[group + 3 : group + 5]
        input_hbm, gate_hbm, weight_hbm, weight_buf, weight_sems = refs[-8:-3]
        copies += finish_weights(hidden, partial, shared, weight_hbm, weight_buf, weight_sems)
    else:
        input_hbm, gate_hbm = refs[-5:-3]
    input_buf, gate_buf, sems = refs[-3:]
    tokens, width = input_buf.shape
    span = width // BACK_CUTS
    packed = BACK_CUTS * capacity
    shards = group // EXPERTS_W
    me = lax.axis_index("expert")
    every = jnp.concatenate([ref[...] for ref in backs], axis=0)
    row = iota((group * packed, tokens), 0)
    expert = ((row // packed) ^ me) // shards
    within = row % packed
    slot = jnp.where(expert == 0, slots[0:1, :], slots[1:2, :])
    match = within % capacity == slot
    picks = [
        (match & (within // capacity == cut)).astype(F32).astype(BF16) for cut in range(BACK_CUTS)
    ]
    gates = tn(every[:, span:], picks[0])
    for k in range(2):
        route = routes[k : k + 1, :]
        value = jnp.where(route == 0, gates[0:1, :], jnp.where(route == 1, gates[1:2, :], 0.0))
        gate_buf[k : k + 1, :] = value * (16.0 / levels[k : k + 1, :].astype(F32))
    copies.append(pltpu.make_async_copy(gate_buf, gate_hbm, sems.at[2 * BACK_CUTS]))
    copies[-1].start()
    for cut, pick in enumerate(picks):
        half = span // 2
        for n in range(2):
            part = pl.ds(cut * span + n * half, half)
            input_buf[:, part] = tn(pick, every[:, n * half : (n + 1) * half]).astype(BF16)
            copy = pltpu.make_async_copy(
                input_buf.at[:, part], input_hbm.at[:, part], sems.at[2 * cut + n]
            )
            copy.start()
            copies.append(copy)
    for copy in copies:
        copy.wait()


def swap(array, axis, size, mask):
    return lax.ppermute(array, axis, [(n, n ^ mask) for n in range(size)])


def far_first(group):
    return [*range(group // 2, group), *range(1, group // 2)]


def plain_weights(inputs, grads, rights):
    inputs = lax.all_to_all(inputs, "dp", split_axis=1, concat_axis=0, tiled=True)
    grads = lax.all_to_all(grads, "dp", split_axis=1, concat_axis=0, tiled=True)
    rights = [lax.all_gather(right, "dp", axis=0, tiled=True) for right in rights]
    return jnp.stack([tn(inputs, rights[0]), tn(inputs, rights[1]), tn(grads, rights[2])])


def per_device(grad_out, routes, gate_levels, saved_inputs, w_gate, w_up, w_down):
    group = lax.axis_size("expert")
    n_dp = lax.axis_size("dp")
    shards = group // EXPERTS_W
    rows, width = saved_inputs.shape
    capacity = rows // group
    hidden = w_gate.shape[1]
    tokens = grad_out.shape[0]
    block = width // n_dp
    paired = n_dp == PAIRED
    routes = routes.T
    gate_levels = gate_levels.T
    shape = jax.ShapeDtypeStruct

    packed = shape((SEND_CUTS * capacity, width // SEND_CUTS), BF16)
    own, other, slots = call(
        functools.partial(pick_kernel, shards, capacity),
        (packed, packed, shape((8, tokens), jnp.int32)),
        (routes, gate_levels, grad_out),
        [HBM] * 3,
        [
            pltpu.VMEM(routes.shape, jnp.int32),
            pltpu.VMEM(routes.shape, jnp.int32),
            pltpu.VMEM(grad_out.shape, BF16),
            pltpu.SemaphoreType.DMA((2 + SEND_CUTS,)),
        ],
        name="pick",
    )
    own, other = call(
        pass_kernel,
        (packed,) * 2,
        (own, other),
        [VMEM] * 2,
        flops=HEAVY,
        name="pass",
    )
    received = [own] + [None] * (group - 1)
    for mask in far_first(group):
        received[mask] = swap(own if mask < shards else other, "expert", group, mask)
    part = shape((rows, hidden), F32)
    ahead = shape((rows, 2 * block + 3 * hidden), BF16)
    *ahead, u, v, h = call(
        functools.partial(hidden_kernel, n_dp),
        (ahead,) * paired + (part,) * 3,
        (saved_inputs, w_gate, w_up),
        [VMEM] * 3,
        flops=HEAVY,
        name="hidden",
    )
    turned = call(
        turn_kernel,
        (shape((hidden, width), BF16),) * TURNED,
        (w_gate, w_up)[:TURNED],
        [VMEM] * TURNED,
        flops=HEAVY,
        name="turn",
    )
    half = shape((rows, hidden), BF16)
    late = shape((rows, 2 * block + hidden), BF16)
    full = shape((rows, 4 * block + 3 * hidden), BF16)
    outward = (full,) * LAST + (late,) if paired else (shape((rows, width), BF16), half)
    *sends, da, db, gate = call(
        functools.partial(project_kernel, group, capacity, n_dp),
        outward + (half, half, shape((rows, GATE_LANES), BF16)),
        (*arrange(received, DISPATCH_ORDER), w_down, u, v, h, saved_inputs, *turned),
        [VMEM] * (group + 5) + [UNUSED] * TURNED,
        [pltpu.VMEM((rows, width), BF16)],
        name="project",
    )
    ahead = [swap(array, "dp", n_dp, 2 * LAST) for array in ahead]
    back = shape((BACK_CUTS * capacity, width // BACK_CUTS + GATE_LANES), BF16)
    returns = call(
        functools.partial(input_kernel, group, capacity),
        (back,) * group,
        (da, db, gate, *turned, *(w_gate, w_up)[TURNED:], *ahead),
        [VMEM] * 5 + [UNUSED] * len(ahead),
        flops=HEAVY,
        name="input",
    )
    backs = [returns[0]] + [None] * (group - 1)
    for mask in far_first(group):
        backs[mask] = swap(returns[mask], "expert", group, mask)
    if paired:
        got = [sends[0]] + [swap(sends[m], "dp", n_dp, 2 * m) for m in range(1, LAST + 1)]
        buffers = got[:LAST] + ahead + got[LAST:]
        sharing = call(
            functools.partial(share_kernel, block, hidden),
            shape(((LAST + 1) * rows, 2 * block + 3 * hidden), BF16),
            buffers,
            [VMEM] * len(buffers),
            name="share",
        )
        shared = swap(sharing, "dp", n_dp, 1)
        block_shape = shape((3, block, hidden), F32)
        partial = call(
            functools.partial(weight_kernel, block, hidden),
            block_shape,
            buffers,
            [VMEM] * len(buffers),
            flops=HEAVY,
            name="weight",
        )
        extra = (partial, shared)
    else:
        extra = ()
    finished = (shape((tokens, width), BF16), shape((2, tokens), F32))
    scratch = [
        pltpu.VMEM((tokens, width), BF16),
        pltpu.VMEM((2, tokens), F32),
        pltpu.SemaphoreType.DMA((2 * BACK_CUTS + 1,)),
    ]
    if paired:
        finished += (block_shape,)
        scratch = [pltpu.VMEM(block_shape.shape, F32), pltpu.SemaphoreType.DMA((3,))] + scratch
    input_grad, gate_grad, *weight_grad = call(
        functools.partial(finish_kernel, group, capacity, hidden if paired else 0),
        finished,
        (*arrange(backs, RETURN_ORDER), routes, gate_levels, slots, *extra),
        [VMEM] * (group + 3 + len(extra)),
        scratch,
        near=False,
        out_specs=(HBM,) * len(finished),
        flops=HEAVY,
        name="finish",
    )
    if paired:
        (weight_grad,) = weight_grad
    else:
        weight_grad = plain_weights(saved_inputs, sends[0], (da, db, sends[1]))
    return input_grad, gate_grad.T, weight_grad.transpose(1, 0, 2)


def solution(mesh):
    in_specs = (
        P(("dp", "expert"), None),
        P(("dp", "expert"), None),
        P(("dp", "expert"), None),
        P(("dp", "expert"), None),
        P(None, "expert"),
        P(None, "expert"),
        P("expert", None),
    )
    out_specs = (P(("dp", "expert"), None), P(("dp", "expert"), None), P("dp", None, "expert"))
    return jax.shard_map(
        per_device, mesh=mesh, in_specs=in_specs, out_specs=out_specs, check_vma=False
    )
```

```python
import functools

import jax
import jax.numpy as jnp
from jax import lax
from jax.experimental import pallas as pl
from jax.experimental.pallas import tpu as pltpu
from jax.sharding import PartitionSpec as P

EXPERTS_W = 2
SEND_CUTS = 4
BACK_CUTS = 2
GATE_LANES = 128
W_CHUNKS = 2
TURNED = 2
LAST = 3
HEAVY = 10**10
DISPATCH_ORDER = (0, 3, 2, 1)
RETURN_ORDER = (0, 3, 2, 1)
PAIRED = 8
F32 = jnp.float32
BF16 = jnp.bfloat16
VMEM = pl.BlockSpec(memory_space=pltpu.VMEM)
HBM = pl.BlockSpec(memory_space=pltpu.HBM)
UNUSED = pl.BlockSpec(memory_space=pl.ANY)


def nn(left, right):
    return lax.dot_general(left, right, (((1,), (0,)), ((), ())), preferred_element_type=F32)


def nt(left, right):
    return lax.dot_general(left, right, (((1,), (1,)), ((), ())), preferred_element_type=F32)


def tn(left, right):
    return lax.dot_general(left, right, (((0,), (0,)), ((), ())), preferred_element_type=F32)


def iota(shape, dim):
    return lax.broadcasted_iota(jnp.int32, shape, dim)


def call(kernel, outs, args, specs, scratch=(), near=True, out_specs=None, flops=0, name=None):
    args = [
        pltpu.with_memory_space_constraint(arg, pltpu.HBM) if spec is HBM else arg
        for arg, spec in zip(args, specs)
    ]
    if near:
        outs = jax.tree.map(lambda out: pltpu.VMEM(out.shape, out.dtype), outs)
    return pl.pallas_call(
        kernel,
        out_shape=outs,
        in_specs=specs,
        out_specs=out_specs or jax.tree.map(lambda _: VMEM, outs),
        scratch_shapes=scratch,
        compiler_params=pltpu.CompilerParams(vmem_limit_bytes=24 * 1024 * 1024),
        cost_estimate=pl.CostEstimate(flops=flops, bytes_accessed=0, transcendentals=0),
        name=name,
    )(*args)


def arrange(arrays, order):
    return [arrays[mask] for mask in order] if len(arrays) == len(order) else arrays


def restore(refs, order):
    if len(refs) != len(order):
        return refs
    return [refs[order.index(mask)] for mask in range(len(refs))]


def pick_kernel(
    shards, capacity, routes_hbm, levels_hbm, grad_hbm, own_out, other_out, slots_out,
    routes, levels, grad, sems,
):
    tokens, width = grad.shape
    span = width // SEND_CUTS
    rows = SEND_CUTS * capacity
    small = [
        pltpu.make_async_copy(routes_hbm, routes, sems.at[0]),
        pltpu.make_async_copy(levels_hbm, levels, sems.at[1]),
    ]
    large = [
        pltpu.make_async_copy(
            grad_hbm.at[:, pl.ds(cut * span, span)],
            grad.at[:, pl.ds(cut * span, span)],
            sems.at[2 + cut],
        )
        for cut in range(SEND_CUTS)
    ]
    for copy in small + large:
        copy.start()
    mine = lax.axis_index("expert") // shards
    upto = (iota((tokens, tokens), 0) <= iota((tokens, tokens), 1)).astype(BF16)
    for copy in small:
        copy.wait()
    first, second = routes[0:1, :], routes[1:2, :]
    found = jnp.zeros((8, tokens), F32)
    for expert in range(EXPERTS_W):
        hit = ((first == expert) | (second == expert)).astype(F32)
        found = jnp.where(iota((8, tokens), 0) == expert, hit, found)
    counted = nn(found.astype(BF16), upto)
    slots = jnp.where(found > 0, counted - 1.0, -4096.0).astype(jnp.int32)
    slots_out[...] = slots
    slot_of, gate_of = [], []
    for expert in (mine, 1 - mine):
        level = jnp.where(first == expert, levels[0:1, :], levels[1:2, :])
        slot_of.append(jnp.where(expert == 0, slots[0:1, :], slots[1:2, :]))
        gate_of.append(level.astype(F32) * (1.0 / 16.0))
    row = iota((2 * rows, tokens), 0)
    slot = jnp.where(row < rows, slot_of[0], slot_of[1])
    gate = jnp.where(row < rows, gate_of[0], gate_of[1])
    place = row % rows
    total = jnp.zeros((2 * rows, span), F32)
    for cut in range(SEND_CUTS):
        lead = jnp.where(slot == place - cut * capacity, gate, 0.0).astype(BF16)
        large[cut].wait()
        total += nn(lead, grad[:, cut * span : (cut + 1) * span])
    own_out[...] = total[:rows].astype(BF16)
    other_out[...] = total[rows:].astype(BF16)


def hidden_kernel(n_dp, inputs, w_gate, w_up, *refs):
    ahead, (u_out, v_out, h_out) = refs[:-3], refs[-3:]
    a = nn(inputs[...], w_gate[...])
    b = nn(inputs[...], w_up[...])
    s = jax.nn.sigmoid(a)
    u = a * s
    v = b * s * (1.0 + a * (1.0 - s))
    u_out[...] = u
    v_out[...] = v
    h = u * b
    h_out[...] = h
    pair = 2 * (inputs.shape[1] // n_dp)
    for out in ahead:
        start = pl.multiple_of(((lax.axis_index("dp") // 2) ^ LAST) * pair, 128)
        out[:, 0:pair] = inputs[:, pl.ds(start, pair)]
        for n, value in enumerate((h, u, v)):
            hidden = value.shape[1]
            out[:, pair + n * hidden : pair + (n + 1) * hidden] = value.astype(BF16)


def turn_kernel(*refs):
    for ref, out in zip(refs[: len(refs) // 2], refs[len(refs) // 2 :]):
        step = ref.shape[0] // W_CHUNKS
        for k in range(W_CHUNKS):
            part = slice(k * step, (k + 1) * step)
            out[:, part] = ref[part, :].T


def pass_kernel(own, other, own_out, other_out):
    own_out[...] = own[...]
    other_out[...] = other[...]


def project_kernel(group, capacity, n_dp, *refs):
    received = restore(refs[:group], DISPATCH_ORDER)
    w_down, u_in, v_in, h_in, inputs = refs[group : group + 5]
    sends = refs[group + 5 + TURNED : -4]
    da_out, db_out, gate_out, rows_buf = refs[-4:]
    rows, hidden = u_in.shape
    width = w_down.shape[1]
    span = width // SEND_CUTS
    me = lax.axis_index("expert")
    packed = SEND_CUTS * capacity
    every = jnp.concatenate([ref[...] for ref in received], axis=0)
    to = iota((rows, group * packed), 0)
    at = iota((rows, group * packed), 1)
    source = (at // packed) ^ me
    within = at % packed
    match = (to // capacity == source) & (to % capacity == within % capacity)
    projected = jnp.zeros((rows, hidden), F32)
    for cut in range(SEND_CUTS):
        select = (match & (within // capacity == cut)).astype(F32).astype(BF16)
        piece = nn(select, every).astype(BF16)
        rows_buf[:, cut * span : (cut + 1) * span] = piece
        projected += nt(piece, w_down[:, cut * span : (cut + 1) * span])
    da = (projected * v_in[...]).astype(BF16)
    db = (projected * u_in[...]).astype(BF16)
    h = h_in[...]
    da_out[...] = da
    db_out[...] = db
    gate = jnp.sum(h * projected, axis=1, keepdims=True)
    lane = iota((rows, GATE_LANES), 1)
    gate_out[...] = jnp.where(lane == me // (group // EXPERTS_W), gate, 0.0).astype(BF16)
    h = h.astype(BF16)
    if n_dp != PAIRED:
        sends[0][...] = rows_buf[...]
        sends[1][...] = h
        return
    pair = 2 * (width // n_dp)
    chip = lax.axis_index("dp") // 2
    for m, send in enumerate(sends):
        start = pl.multiple_of((chip ^ m) * pair, 128)
        base = 0
        if m < LAST:
            send[:, 0:pair] = inputs[:, pl.ds(start, pair)]
            send[:, pair : pair + hidden] = h
            base = pair + hidden
        send[:, base : base + pair] = rows_buf[:, pl.ds(start, pair)]
        if m < LAST:
            send[:, base + pair : base + pair + hidden] = da
            send[:, base + pair + hidden :] = db
        else:
            send[:, pair:] = projected.astype(BF16)


def input_kernel(group, capacity, da, db, gate, w_gate, w_up, *refs):
    outs = refs[-group:]
    rows = da.shape[0]
    width = max(w_gate.shape)
    span = width // BACK_CUTS
    step = width // W_CHUNKS
    per = W_CHUNKS // BACK_CUTS
    me = lax.axis_index("expert")
    packed = BACK_CUTS * capacity
    to = iota((group * packed, rows), 0)
    at = iota((group * packed, rows), 1)
    target = (to // packed) ^ me
    within = to % packed
    match = (at // capacity == target) & (at % capacity == within % capacity)
    selects = [
        (match & (within // capacity == cut)).astype(F32).astype(BF16) for cut in range(BACK_CUTS)
    ]
    total = [jnp.zeros((group * packed, step), F32) for _ in range(per)]
    for k in range(W_CHUNKS):
        piece = slice(k * step, (k + 1) * step)
        part = nn(da[...], w_gate[:, piece])
        if TURNED > 1:
            part += nn(db[...], w_up[:, piece])
        else:
            part += nt(db[...], w_up[piece, :])
        total[k % per] += nn(selects[k // per], part.astype(BF16))
    gates = nn(selects[0], gate[...])
    for n, out in enumerate(outs):
        for q in range(per):
            out[:, q * step : (q + 1) * step] = total[q][n * packed : (n + 1) * packed].astype(BF16)
        out[:, span:] = gates[n * packed : (n + 1) * packed].astype(BF16)


def rows_of(block, hidden, core, refs):
    start = pl.multiple_of(core * block, 128)
    pair = 2 * block
    first, last = refs[0], refs[-1]
    base = pair + hidden if len(refs) == 1 else 0
    grads = last[:, pl.ds(pl.multiple_of(base + start, 128), block)]
    base += pair
    da = last[:, base : base + hidden]
    if len(refs) == 1:
        db = last[:, base + hidden : base + 2 * hidden]
    else:
        projected = da.astype(F32)
        u, v = (first[:, pair + n * hidden : pair + (n + 1) * hidden] for n in (1, 2))
        da = (projected * v.astype(F32)).astype(BF16)
        db = (projected * u.astype(F32)).astype(BF16)
    return first[:, pl.ds(start, block)], first[:, pair : pair + hidden], grads, da, db


def chips_of(refs):
    return [refs[n : n + 1] for n in range(LAST)] + [refs[LAST:]]


def share_kernel(block, hidden, *refs):
    out = refs[-1]
    core = 1 - lax.axis_index("dp") % 2
    for m, chip in enumerate(chips_of(refs[:-1])):
        rows = chip[0].shape[0]
        at = 0
        for value in rows_of(block, hidden, core, chip):
            out[m * rows : (m + 1) * rows, at : at + value.shape[1]] = value
            at += value.shape[1]


def weight_kernel(block, hidden, *refs):
    out = refs[-1]
    core = lax.axis_index("dp") % 2
    chips = [rows_of(block, hidden, core, chip) for chip in chips_of(refs[:-1])]
    inputs, h, grads, da, db = (jnp.concatenate(values, axis=0) for values in zip(*chips))
    out[0] = tn(inputs, da)
    out[1] = tn(inputs, db)
    out[2] = tn(grads, h)


def finish_weights(hidden, partial, shared, out_hbm, buf, sems):
    block = buf.shape[1]
    middle = block + hidden
    inputs, h = shared[:, 0:block], shared[:, block:middle]
    grads, da = shared[:, middle : middle + block], shared[:, middle + block : 2 * middle]
    copies = []
    for n, (left, right) in enumerate(((inputs, da), (inputs, shared[:, 2 * middle :]), (grads, h))):
        buf[n] = partial[n] + tn(left, right)
        copies.append(pltpu.make_async_copy(buf.at[n], out_hbm.at[n], sems.at[n]))
        copies[-1].start()
    return copies


def finish_kernel(group, capacity, hidden, *refs):
    backs = restore(refs[:group], RETURN_ORDER)
    routes, levels, slots = refs[group : group + 3]
    copies = []
    if hidden > 0:
        partial, shared = refs[group + 3 : group + 5]
        input_hbm, gate_hbm, weight_hbm, weight_buf, weight_sems = refs[-8:-3]
        copies += finish_weights(hidden, partial, shared, weight_hbm, weight_buf, weight_sems)
    else:
        input_hbm, gate_hbm = refs[-5:-3]
    input_buf, gate_buf, sems = refs[-3:]
    tokens, width = input_buf.shape
    span = width // BACK_CUTS
    packed = BACK_CUTS * capacity
    shards = group // EXPERTS_W
    me = lax.axis_index("expert")
    every = jnp.concatenate([ref[...] for ref in backs], axis=0)
    row = iota((group * packed, tokens), 0)
    expert = ((row // packed) ^ me) // shards
    within = row % packed
    slot = jnp.where(expert == 0, slots[0:1, :], slots[1:2, :])
    match = within % capacity == slot
    picks = [
        (match & (within // capacity == cut)).astype(F32).astype(BF16) for cut in range(BACK_CUTS)
    ]
    gates = tn(every[:, span:], picks[0])
    for k in range(2):
        route = routes[k : k + 1, :]
        value = jnp.where(route == 0, gates[0:1, :], jnp.where(route == 1, gates[1:2, :], 0.0))
        gate_buf[k : k + 1, :] = value * (16.0 / levels[k : k + 1, :].astype(F32))
    copies.append(pltpu.make_async_copy(gate_buf, gate_hbm, sems.at[2 * BACK_CUTS]))
    copies[-1].start()
    for cut, pick in enumerate(picks):
        half = span // 2
        for n in range(2):
            part = pl.ds(cut * span + n * half, half)
            input_buf[:, part] = tn(pick, every[:, n * half : (n + 1) * half]).astype(BF16)
            copy = pltpu.make_async_copy(
                input_buf.at[:, part], input_hbm.at[:, part], sems.at[2 * cut + n]
            )
            copy.start()
            copies.append(copy)
    for copy in copies:
        copy.wait()


def swap(array, axis, size, mask):
    return lax.ppermute(array, axis, [(n, n ^ mask) for n in range(size)])


def far_first(group):
    return [*range(group // 2, group), *range(1, group // 2)]


def plain_weights(inputs, grads, rights):
    inputs = lax.all_to_all(inputs, "dp", split_axis=1, concat_axis=0, tiled=True)
    grads = lax.all_to_all(grads, "dp", split_axis=1, concat_axis=0, tiled=True)
    rights = [lax.all_gather(right, "dp", axis=0, tiled=True) for right in rights]
    return jnp.stack([tn(inputs, rights[0]), tn(inputs, rights[1]), tn(grads, rights[2])])


def per_device(grad_out, routes, gate_levels, saved_inputs, w_gate, w_up, w_down):
    group = lax.axis_size("expert")
    n_dp = lax.axis_size("dp")
    shards = group // EXPERTS_W
    rows, width = saved_inputs.shape
    capacity = rows // group
    hidden = w_gate.shape[1]
    tokens = grad_out.shape[0]
    block = width // n_dp
    paired = n_dp == PAIRED
    routes = routes.T
    gate_levels = gate_levels.T
    shape = jax.ShapeDtypeStruct

    packed = shape((SEND_CUTS * capacity, width // SEND_CUTS), BF16)
    own, other, slots = call(
        functools.partial(pick_kernel, shards, capacity),
        (packed, packed, shape((8, tokens), jnp.int32)),
        (routes, gate_levels, grad_out),
        [HBM] * 3,
        [
            pltpu.VMEM(routes.shape, jnp.int32),
            pltpu.VMEM(routes.shape, jnp.int32),
            pltpu.VMEM(grad_out.shape, BF16),
            pltpu.SemaphoreType.DMA((2 + SEND_CUTS,)),
        ],
        name="pick",
    )
    own, other = call(
        pass_kernel,
        (packed,) * 2,
        (own, other),
        [VMEM] * 2,
        flops=HEAVY,
        name="pass",
    )
    received = [own] + [None] * (group - 1)
    for mask in far_first(group):
        received[mask] = swap(own if mask < shards else other, "expert", group, mask)
    part = shape((rows, hidden), F32)
    ahead = shape((rows, 2 * block + 3 * hidden), BF16)
    *ahead, u, v, h = call(
        functools.partial(hidden_kernel, n_dp),
        (ahead,) * paired + (part,) * 3,
        (saved_inputs, w_gate, w_up),
        [VMEM] * 3,
        flops=HEAVY,
        name="hidden",
    )
    turned = call(
        turn_kernel,
        (shape((hidden, width), BF16),) * TURNED,
        (w_gate, w_up)[:TURNED],
        [VMEM] * TURNED,
        flops=HEAVY,
        name="turn",
    )
    half = shape((rows, hidden), BF16)
    late = shape((rows, 2 * block + hidden), BF16)
    full = shape((rows, 4 * block + 3 * hidden), BF16)
    outward = (full,) * LAST + (late,) if paired else (shape((rows, width), BF16), half)
    *sends, da, db, gate = call(
        functools.partial(project_kernel, group, capacity, n_dp),
        outward + (half, half, shape((rows, GATE_LANES), BF16)),
        (*arrange(received, DISPATCH_ORDER), w_down, u, v, h, saved_inputs, *turned),
        [VMEM] * (group + 5) + [UNUSED] * TURNED,
        [pltpu.VMEM((rows, width), BF16)],
        name="project",
    )
    ahead = [swap(array, "dp", n_dp, 2 * LAST) for array in ahead]
    back = shape((BACK_CUTS * capacity, width // BACK_CUTS + GATE_LANES), BF16)
    returns = call(
        functools.partial(input_kernel, group, capacity),
        (back,) * group,
        (da, db, gate, *turned, *(w_gate, w_up)[TURNED:], *ahead),
        [VMEM] * 5 + [UNUSED] * len(ahead),
        flops=HEAVY,
        name="input",
    )
    backs = [returns[0]] + [None] * (group - 1)
    for mask in far_first(group):
        backs[mask] = swap(returns[mask], "expert", group, mask)
    if paired:
        got = [sends[0]] + [swap(sends[m], "dp", n_dp, 2 * m) for m in range(1, LAST + 1)]
        buffers = got[:LAST] + ahead + got[LAST:]
        sharing = call(
            functools.partial(share_kernel, block, hidden),
            shape(((LAST + 1) * rows, 2 * block + 3 * hidden), BF16),
            buffers,
            [VMEM] * len(buffers),
            name="share",
        )
        shared = swap(sharing, "dp", n_dp, 1)
        block_shape = shape((3, block, hidden), F32)
        partial = call(
            functools.partial(weight_kernel, block, hidden),
            block_shape,
            buffers,
            [VMEM] * len(buffers),
            flops=HEAVY,
            name="weight",
        )
        extra = (partial, shared)
    else:
        extra = ()
    finished = (shape((tokens, width), BF16), shape((2, tokens), F32))
    scratch = [
        pltpu.VMEM((tokens, width), BF16),
        pltpu.VMEM((2, tokens), F32),
        pltpu.SemaphoreType.DMA((2 * BACK_CUTS + 1,)),
    ]
    if paired:
        finished += (block_shape,)
        scratch = [pltpu.VMEM(block_shape.shape, F32), pltpu.SemaphoreType.DMA((3,))] + scratch
    input_grad, gate_grad, *weight_grad = call(
        functools.partial(finish_kernel, group, capacity, hidden if paired else 0),
        finished,
        (*arrange(backs, RETURN_ORDER), routes, gate_levels, slots, *extra),
        [VMEM] * (group + 3 + len(extra)),
        scratch,
        near=False,
        out_specs=(HBM,) * len(finished),
        flops=HEAVY,
        name="finish",
    )
    if paired:
        (weight_grad,) = weight_grad
    else:
        weight_grad = plain_weights(saved_inputs, sends[0], (da, db, sends[1]))
    return input_grad, gate_grad.T, weight_grad.transpose(1, 0, 2)


def solution(mesh):
    in_specs = (
        P(("dp", "expert"), None),
        P(("dp", "expert"), None),
        P(("dp", "expert"), None),
        P(("dp", "expert"), None),
        P(None, "expert"),
        P(None, "expert"),
        P("expert", None),
    )
    out_specs = (P(("dp", "expert"), None), P(("dp", "expert"), None), P("dp", None, "expert"))
    return jax.shard_map(
        per_device, mesh=mesh, in_specs=in_specs, out_specs=out_specs, check_vma=False
    )
```

```python
import functools

import jax
import jax.numpy as jnp
from jax import lax
from jax.experimental import pallas as pl
from jax.experimental.pallas import tpu as pltpu
from jax.sharding import PartitionSpec as P

EXPERTS_W = 2
SEND_CUTS = 4
BACK_CUTS = 2
HEAD = 8
GATE_LANES = 128
W_CHUNKS = 2
TURNED = 2
LAST = 3
HEAVY = 10**10
DISPATCH_ORDER = (0, 3, 2, 1)
RETURN_ORDER = (0, 3, 2, 1)
PAIRED = 8
F32 = jnp.float32
BF16 = jnp.bfloat16
VMEM = pl.BlockSpec(memory_space=pltpu.VMEM)
HBM = pl.BlockSpec(memory_space=pltpu.HBM)
UNUSED = pl.BlockSpec(memory_space=pl.ANY)


def nn(left, right):
    return lax.dot_general(left, right, (((1,), (0,)), ((), ())), preferred_element_type=F32)


def nt(left, right):
    return lax.dot_general(left, right, (((1,), (1,)), ((), ())), preferred_element_type=F32)


def tn(left, right):
    return lax.dot_general(left, right, (((0,), (0,)), ((), ())), preferred_element_type=F32)


def iota(shape, dim):
    return lax.broadcasted_iota(jnp.int32, shape, dim)


def call(kernel, outs, args, specs, scratch=(), near=True, out_specs=None, flops=0, name=None):
    args = [
        pltpu.with_memory_space_constraint(arg, pltpu.HBM) if spec is HBM else arg
        for arg, spec in zip(args, specs)
    ]
    if near:
        outs = jax.tree.map(lambda out: pltpu.VMEM(out.shape, out.dtype), outs)
    return pl.pallas_call(
        kernel,
        out_shape=outs,
        in_specs=specs,
        out_specs=out_specs or jax.tree.map(lambda _: VMEM, outs),
        scratch_shapes=scratch,
        compiler_params=pltpu.CompilerParams(vmem_limit_bytes=24 * 1024 * 1024),
        cost_estimate=pl.CostEstimate(flops=flops, bytes_accessed=0, transcendentals=0),
        name=name,
    )(*args)


def arrange(arrays, order):
    return [arrays[mask] for mask in order] if len(arrays) == len(order) else arrays


def restore(refs, order):
    if len(refs) != len(order):
        return refs
    return [refs[order.index(mask)] for mask in range(len(refs))]


def pick_kernel(
    shards, capacity, routes_hbm, levels_hbm, grad_hbm, own_out, other_out, slots_out,
    routes, levels, grad, sems,
):
    tokens, width = grad.shape
    span = width // SEND_CUTS
    rows = SEND_CUTS * capacity
    small = [
        pltpu.make_async_copy(routes_hbm, routes, sems.at[0]),
        pltpu.make_async_copy(levels_hbm, levels, sems.at[1]),
    ]
    large = [
        pltpu.make_async_copy(
            grad_hbm.at[:, pl.ds(cut * span, span)],
            grad.at[:, pl.ds(cut * span, span)],
            sems.at[2 + cut],
        )
        for cut in range(SEND_CUTS)
    ]
    for copy in small + large:
        copy.start()
    mine = lax.axis_index("expert") // shards
    upto = (iota((tokens, tokens), 0) <= iota((tokens, tokens), 1)).astype(BF16)
    for copy in small:
        copy.wait()
    first, second = routes[0:1, :], routes[1:2, :]
    found = jnp.zeros((8, tokens), F32)
    for expert in range(EXPERTS_W):
        hit = ((first == expert) | (second == expert)).astype(F32)
        found = jnp.where(iota((8, tokens), 0) == expert, hit, found)
    counted = nn(found.astype(BF16), upto)
    slots = jnp.where(found > 0, counted - 1.0, -4096.0).astype(jnp.int32)
    slots_out[...] = slots
    slot_of, gate_of = [], []
    for expert in (mine, 1 - mine):
        level = jnp.where(first == expert, levels[0:1, :], levels[1:2, :])
        slot_of.append(jnp.where(expert == 0, slots[0:1, :], slots[1:2, :]))
        gate_of.append(level.astype(F32) * (1.0 / 16.0))
    row = iota((2 * rows, tokens), 0)
    slot = jnp.where(row < rows, slot_of[0], slot_of[1])
    gate = jnp.where(row < rows, gate_of[0], gate_of[1])
    place = row % rows
    total = jnp.zeros((2 * rows, span), F32)
    for cut in range(SEND_CUTS):
        lead = jnp.where(slot == place - cut * capacity, gate, 0.0).astype(BF16)
        large[cut].wait()
        total += nn(lead, grad[:, cut * span : (cut + 1) * span])
    own_out[...] = total[:rows].astype(BF16)
    other_out[...] = total[rows:].astype(BF16)


def hidden_kernel(n_dp, inputs, w_gate, w_up, *refs):
    ahead, (u_out, v_out, h_out) = refs[:-3], refs[-3:]
    a = nn(inputs[...], w_gate[...])
    b = nn(inputs[...], w_up[...])
    s = jax.nn.sigmoid(a)
    u = a * s
    v = b * s * (1.0 + a * (1.0 - s))
    u_out[...] = u
    v_out[...] = v
    h = u * b
    h_out[...] = h
    pair = 2 * (inputs.shape[1] // n_dp)
    for out in ahead:
        start = pl.multiple_of(((lax.axis_index("dp") // 2) ^ LAST) * pair, 128)
        out[:, 0:pair] = inputs[:, pl.ds(start, pair)]
        for n, value in enumerate((h, u, v)):
            hidden = value.shape[1]
            out[:, pair + n * hidden : pair + (n + 1) * hidden] = value.astype(BF16)


def turn_kernel(*refs):
    for ref, out in zip(refs[: len(refs) // 2], refs[len(refs) // 2 :]):
        step = ref.shape[0] // W_CHUNKS
        for k in range(W_CHUNKS):
            part = slice(k * step, (k + 1) * step)
            out[:, part] = ref[part, :].T


def pass_kernel(own, other, own_out, other_out):
    own_out[...] = own[...]
    other_out[...] = other[...]


def project_kernel(group, capacity, n_dp, *refs):
    received = restore(refs[:group], DISPATCH_ORDER)
    w_down, u_in, v_in, h_in, inputs = refs[group : group + 5]
    sends = refs[group + 5 + TURNED : -4]
    da_out, db_out, gate_out, rows_buf = refs[-4:]
    rows, hidden = u_in.shape
    width = w_down.shape[1]
    span = width // SEND_CUTS
    me = lax.axis_index("expert")
    packed = SEND_CUTS * capacity
    every = jnp.concatenate([ref[...] for ref in received], axis=0)
    to = iota((rows, group * packed), 0)
    at = iota((rows, group * packed), 1)
    source = (at // packed) ^ me
    within = at % packed
    match = (to // capacity == source) & (to % capacity == within % capacity)
    projected = jnp.zeros((rows, hidden), F32)
    for cut in range(SEND_CUTS):
        select = (match & (within // capacity == cut)).astype(F32).astype(BF16)
        piece = nn(select, every).astype(BF16)
        rows_buf[:, cut * span : (cut + 1) * span] = piece
        projected += nt(piece, w_down[:, cut * span : (cut + 1) * span])
    da = (projected * v_in[...]).astype(BF16)
    db = (projected * u_in[...]).astype(BF16)
    h = h_in[...]
    da_out[...] = da
    db_out[...] = db
    gate = jnp.sum(h * projected, axis=1, keepdims=True)
    lane = iota((rows, GATE_LANES), 1)
    own = (lane < BACK_CUTS * EXPERTS_W) & (lane % EXPERTS_W == me // (group // EXPERTS_W))
    gate_out[...] = jnp.where(own, gate, 0.0).astype(BF16)
    h = h.astype(BF16)
    if n_dp != PAIRED:
        sends[0][...] = rows_buf[...]
        sends[1][...] = h
        return
    pair = 2 * (width // n_dp)
    chip = lax.axis_index("dp") // 2
    for m, send in enumerate(sends):
        start = pl.multiple_of((chip ^ m) * pair, 128)
        base = 0
        if m < LAST:
            send[:, 0:pair] = inputs[:, pl.ds(start, pair)]
            send[:, pair : pair + hidden] = h
            base = pair + hidden
        send[:, base : base + pair] = rows_buf[:, pl.ds(start, pair)]
        if m < LAST:
            send[:, base + pair : base + pair + hidden] = da
            send[:, base + pair + hidden :] = db
        else:
            send[:, pair:] = projected.astype(BF16)


def input_kernel(group, capacity, da, db, gate, w_gate, w_up, *refs):
    outs = refs[-group:]
    rows = da.shape[0]
    width = w_gate.shape[1]
    span = width // BACK_CUTS
    tail = capacity - HEAD
    me = lax.axis_index("expert")
    to = iota((group * HEAD, rows), 0)
    at = iota((group * HEAD, rows), 1)
    place = to % HEAD
    mine = at // capacity == (to // HEAD) ^ me
    head = (mine & (at % capacity == place)).astype(F32).astype(BF16)
    rest = mine & (at % capacity == HEAD + place % tail)
    rests = [(rest & (place // tail == cut)).astype(F32).astype(BF16) for cut in range(BACK_CUTS)]
    heads = []
    lower = jnp.zeros((group * HEAD, span), F32)
    for cut in range(BACK_CUTS):
        piece = slice(cut * span, (cut + 1) * span)
        part = (nn(da[...], w_gate[:, piece]) + nn(db[...], w_up[:, piece])).astype(BF16)
        heads.append(nn(head, part))
        lower += nn(rests[cut], part)
    gates = gate[...].astype(F32)
    early = iota(gates.shape, 1) < EXPERTS_W
    gates = nn(head, jnp.where(early, gates, 0.0).astype(BF16)) + nn(
        rests[0], jnp.where(early, 0.0, gates).astype(BF16)
    )
    for n, out in enumerate(outs):
        block = slice(n * HEAD, (n + 1) * HEAD)
        for cut, value in enumerate((*heads, lower)):
            out[:, cut * span : (cut + 1) * span] = value[block].astype(BF16)
        out[:, width + span :] = gates[block].astype(BF16)


def rows_of(block, hidden, core, refs):
    start = pl.multiple_of(core * block, 128)
    pair = 2 * block
    first, last = refs[0], refs[-1]
    base = pair + hidden if len(refs) == 1 else 0
    grads = last[:, pl.ds(pl.multiple_of(base + start, 128), block)]
    base += pair
    da = last[:, base : base + hidden]
    if len(refs) == 1:
        db = last[:, base + hidden : base + 2 * hidden]
    else:
        projected = da.astype(F32)
        u, v = (first[:, pair + n * hidden : pair + (n + 1) * hidden] for n in (1, 2))
        da = (projected * v.astype(F32)).astype(BF16)
        db = (projected * u.astype(F32)).astype(BF16)
    return first[:, pl.ds(start, block)], first[:, pair : pair + hidden], grads, da, db


def chips_of(refs):
    return [refs[n : n + 1] for n in range(LAST)] + [refs[LAST:]]


def share_kernel(block, hidden, *refs):
    out = refs[-1]
    core = 1 - lax.axis_index("dp") % 2
    for m, chip in enumerate(chips_of(refs[:-1])):
        rows = chip[0].shape[0]
        at = 0
        for value in rows_of(block, hidden, core, chip):
            out[m * rows : (m + 1) * rows, at : at + value.shape[1]] = value
            at += value.shape[1]


def weight_kernel(block, hidden, *refs):
    out = refs[-1]
    core = lax.axis_index("dp") % 2
    chips = [rows_of(block, hidden, core, chip) for chip in chips_of(refs[:-1])]
    inputs, h, grads, da, db = (jnp.concatenate(values, axis=0) for values in zip(*chips))
    out[0] = tn(inputs, da)
    out[1] = tn(inputs, db)
    out[2] = tn(grads, h)


def finish_weights(hidden, partial, shared, out_hbm, buf, sems):
    block = buf.shape[1]
    middle = block + hidden
    inputs, h = shared[:, 0:block], shared[:, block:middle]
    grads, da = shared[:, middle : middle + block], shared[:, middle + block : 2 * middle]
    copies = []
    for n, (left, right) in enumerate(((inputs, da), (inputs, shared[:, 2 * middle :]), (grads, h))):
        buf[n] = partial[n] + tn(left, right)
        copies.append(pltpu.make_async_copy(buf.at[n], out_hbm.at[n], sems.at[n]))
        copies[-1].start()
    return copies


def finish_kernel(group, capacity, hidden, *refs):
    backs = restore(refs[:group], RETURN_ORDER)
    routes, levels, slots = refs[group : group + 3]
    copies = []
    if hidden > 0:
        partial, shared = refs[group + 3 : group + 5]
        input_hbm, gate_hbm, weight_hbm, weight_buf, weight_sems = refs[-8:-3]
        copies += finish_weights(hidden, partial, shared, weight_hbm, weight_buf, weight_sems)
    else:
        input_hbm, gate_hbm = refs[-5:-3]
    input_buf, gate_buf, sems = refs[-3:]
    tokens, width = input_buf.shape
    span = width // BACK_CUTS
    shards = group // EXPERTS_W
    tail = capacity - HEAD
    me = lax.axis_index("expert")
    every = jnp.concatenate([ref[...] for ref in backs], axis=0)
    row = iota((group * HEAD, tokens), 0)
    expert = ((row // HEAD) ^ me) // shards
    place = row % HEAD
    slot = jnp.where(expert == 0, slots[0:1, :], slots[1:2, :])
    head = (slot == place).astype(F32).astype(BF16)
    rest = slot == HEAD + place % tail
    rests = [(rest & (place // tail == cut)).astype(F32).astype(BF16) for cut in range(BACK_CUTS)]
    gates = tn(every[:, width + span :], head)[0:EXPERTS_W]
    gates += tn(every[:, width + span :], rests[0])[EXPERTS_W : 2 * EXPERTS_W]
    for k in range(2):
        route = routes[k : k + 1, :]
        value = jnp.where(route == 0, gates[0:1, :], jnp.where(route == 1, gates[1:2, :], 0.0))
        gate_buf[k : k + 1, :] = value * (16.0 / levels[k : k + 1, :].astype(F32))
    copies.append(pltpu.make_async_copy(gate_buf, gate_hbm, sems.at[2 * BACK_CUTS]))
    copies[-1].start()
    half = span // 2
    for cut in range(BACK_CUTS):
        pick = jnp.concatenate([head, rests[cut]], axis=0)
        for n in range(2):
            start = cut * span + n * half
            lower = every[:, width + n * half : width + (n + 1) * half]
            values = jnp.concatenate([every[:, start : start + half], lower], axis=0)
            part = pl.ds(start, half)
            input_buf[:, part] = tn(pick, values).astype(BF16)
            copy = pltpu.make_async_copy(
                input_buf.at[:, part], input_hbm.at[:, part], sems.at[2 * cut + n]
            )
            copy.start()
            copies.append(copy)
    for copy in copies:
        copy.wait()


def swap(array, axis, size, mask):
    return lax.ppermute(array, axis, [(n, n ^ mask) for n in range(size)])


def far_first(group):
    return [*range(group // 2, group), *range(1, group // 2)]


def plain_weights(inputs, grads, rights):
    inputs = lax.all_to_all(inputs, "dp", split_axis=1, concat_axis=0, tiled=True)
    grads = lax.all_to_all(grads, "dp", split_axis=1, concat_axis=0, tiled=True)
    rights = [lax.all_gather(right, "dp", axis=0, tiled=True) for right in rights]
    return jnp.stack([tn(inputs, rights[0]), tn(inputs, rights[1]), tn(grads, rights[2])])


def per_device(grad_out, routes, gate_levels, saved_inputs, w_gate, w_up, w_down):
    group = lax.axis_size("expert")
    n_dp = lax.axis_size("dp")
    shards = group // EXPERTS_W
    rows, width = saved_inputs.shape
    capacity = rows // group
    hidden = w_gate.shape[1]
    tokens = grad_out.shape[0]
    block = width // n_dp
    paired = n_dp == PAIRED
    routes = routes.T
    gate_levels = gate_levels.T
    shape = jax.ShapeDtypeStruct

    packed = shape((SEND_CUTS * capacity, width // SEND_CUTS), BF16)
    own, other, slots = call(
        functools.partial(pick_kernel, shards, capacity),
        (packed, packed, shape((8, tokens), jnp.int32)),
        (routes, gate_levels, grad_out),
        [HBM] * 3,
        [
            pltpu.VMEM(routes.shape, jnp.int32),
            pltpu.VMEM(routes.shape, jnp.int32),
            pltpu.VMEM(grad_out.shape, BF16),
            pltpu.SemaphoreType.DMA((2 + SEND_CUTS,)),
        ],
        name="pick",
    )
    own, other = call(
        pass_kernel,
        (packed,) * 2,
        (own, other),
        [VMEM] * 2,
        flops=HEAVY,
        name="pass",
    )
    received = [own] + [None] * (group - 1)
    for mask in far_first(group):
        received[mask] = swap(own if mask < shards else other, "expert", group, mask)
    part = shape((rows, hidden), F32)
    ahead = shape((rows, 2 * block + 3 * hidden), BF16)
    *ahead, u, v, h = call(
        functools.partial(hidden_kernel, n_dp),
        (ahead,) * paired + (part,) * 3,
        (saved_inputs, w_gate, w_up),
        [VMEM] * 3,
        flops=HEAVY,
        name="hidden",
    )
    turned = call(
        turn_kernel,
        (shape((hidden, width), BF16),) * TURNED,
        (w_gate, w_up)[:TURNED],
        [VMEM] * TURNED,
        flops=HEAVY,
        name="turn",
    )
    half = shape((rows, hidden), BF16)
    late = shape((rows, 2 * block + hidden), BF16)
    full = shape((rows, 4 * block + 3 * hidden), BF16)
    outward = (full,) * LAST + (late,) if paired else (shape((rows, width), BF16), half)
    *sends, da, db, gate = call(
        functools.partial(project_kernel, group, capacity, n_dp),
        outward + (half, half, shape((rows, GATE_LANES), BF16)),
        (*arrange(received, DISPATCH_ORDER), w_down, u, v, h, saved_inputs, *turned),
        [VMEM] * (group + 5) + [UNUSED] * TURNED,
        [pltpu.VMEM((rows, width), BF16)],
        name="project",
    )
    ahead = [swap(array, "dp", n_dp, 2 * LAST) for array in ahead]
    back = shape((HEAD, width + width // BACK_CUTS + GATE_LANES), BF16)
    returns = call(
        functools.partial(input_kernel, group, capacity),
        (back,) * group,
        (da, db, gate, *turned, *(w_gate, w_up)[TURNED:], *ahead),
        [VMEM] * 5 + [UNUSED] * len(ahead),
        flops=HEAVY,
        name="input",
    )
    backs = [returns[0]] + [None] * (group - 1)
    for mask in far_first(group):
        backs[mask] = swap(returns[mask], "expert", group, mask)
    if paired:
        got = [sends[0]] + [swap(sends[m], "dp", n_dp, 2 * m) for m in range(1, LAST + 1)]
        buffers = got[:LAST] + ahead + got[LAST:]
        sharing = call(
            functools.partial(share_kernel, block, hidden),
            shape(((LAST + 1) * rows, 2 * block + 3 * hidden), BF16),
            buffers,
            [VMEM] * len(buffers),
            name="share",
        )
        shared = swap(sharing, "dp", n_dp, 1)
        block_shape = shape((3, block, hidden), F32)
        partial = call(
            functools.partial(weight_kernel, block, hidden),
            block_shape,
            buffers,
            [VMEM] * len(buffers),
            flops=HEAVY,
            name="weight",
        )
        extra = (partial, shared)
    else:
        extra = ()
    finished = (shape((tokens, width), BF16), shape((2, tokens), F32))
    scratch = [
        pltpu.VMEM((tokens, width), BF16),
        pltpu.VMEM((2, tokens), F32),
        pltpu.SemaphoreType.DMA((2 * BACK_CUTS + 1,)),
    ]
    if paired:
        finished += (block_shape,)
        scratch = [pltpu.VMEM(block_shape.shape, F32), pltpu.SemaphoreType.DMA((3,))] + scratch
    input_grad, gate_grad, *weight_grad = call(
        functools.partial(finish_kernel, group, capacity, hidden if paired else 0),
        finished,
        (*arrange(backs, RETURN_ORDER), routes, gate_levels, slots, *extra),
        [VMEM] * (group + 3 + len(extra)),
        scratch,
        near=False,
        out_specs=(HBM,) * len(finished),
        flops=HEAVY,
        name="finish",
    )
    if paired:
        (weight_grad,) = weight_grad
    else:
        weight_grad = plain_weights(saved_inputs, sends[0], (da, db, sends[1]))
    return input_grad, gate_grad.T, weight_grad.transpose(1, 0, 2)


def solution(mesh):
    in_specs = (
        P(("dp", "expert"), None),
        P(("dp", "expert"), None),
        P(("dp", "expert"), None),
        P(("dp", "expert"), None),
        P(None, "expert"),
        P(None, "expert"),
        P("expert", None),
    )
    out_specs = (P(("dp", "expert"), None), P(("dp", "expert"), None), P("dp", None, "expert"))
    return jax.shard_map(
        per_device, mesh=mesh, in_specs=in_specs, out_specs=out_specs, check_vma=False
    )
```
